256 devices in a mesh: prompt: 16 (over x, z_hi), comp: 16 (over z_lo, y, core).
Axes of the slice: x: 4, y: 4, z: 8 (z_hi: 4, z_lo: 2; z = z_hi * 2 + z_lo), core: 2. Of those that a mesh axis runs over, the one named last changes fastest.
Arguments:
- normed_hidden_input: bfloat16 [16, 2048, 5120], P('comp', 'prompt'), may hold values from -6 to 6
- frozen_query_base: bfloat16 [16, 2048, 2560], P('comp', 'prompt'), may hold values from -5 to 5
- attention_output_grad: bfloat16 [16, 2048, 2560], P('comp', 'prompt'), may hold values from -6 to 6
- completion_keys: bfloat16 [16, 2048, 512], P('comp', 'prompt'), may hold values from -6 to 6
- completion_values: bfloat16 [16, 2048, 512], P('comp', 'prompt'), may hold values from -6 to 6
- owner_prompt_keys: bfloat16 [16, 2048, 512], P('comp', 'prompt'), may hold values from -5 to 5
- owner_prompt_values: bfloat16 [16, 2048, 512], P('comp', 'prompt'), may hold values from -6 to 6
- adapter_down_weight: bfloat16 [5120, 64], replicated, may hold values from -0.078125 to 0.078125
- adapter_up_weight: bfloat16 [64, 2560], replicated, may hold values from -0.75 to 0.75
- adapter_rank: int32 [1], replicated, may hold values from 16 to 64
- route: int32 [16, 16, 16], P('comp', 'prompt'), may hold values from 0 to 15, each once within a row
- lengths: int32 [16, 16, 16], P('comp', 'prompt'), may hold values from 1 to 8, as said below
Outputs:
- grad_query: bfloat16 [16, 2048, 2560], P('comp', 'prompt')
- grad_self_keys: bfloat16 [16, 2048, 512], P('comp', 'prompt')
- grad_self_values: bfloat16 [16, 2048, 512], P('comp', 'prompt')
- grad_prompt_keys: bfloat16 [16, 2048, 512], P('comp', 'prompt')
- grad_prompt_values: bfloat16 [16, 2048, 512], P('comp', 'prompt')
- grad_down: float32 [5120, 64], replicated
- grad_up: float32 [64, 2560], replicated
The draws below stay inside these ranges and needn't reach their ends.
Inputs may be any that keep to these rules, and one draw needn't show every extreme that they name: `route`: each device's 16 entries name every owner of its group once. `lengths`: every device holds a completion of full length 8.
All inputs are finite; a program needn't handle non-finite values.
Results may differ from the reference program's by a relative error of at most 0.013.
The reference program's roundings to bfloat16 on the way count: a program that leaves them out, or rounds other values in their place, can miss the bound.
Values may be sent and summed in bfloat16 or wider, within the bound.
No kernel may reach another device: no remote copies, remote signals or barrier semaphores. Data moves between devices by JAX's collectives and lax.ppermute only.
A program may use at most 64 MiB of HBM per device.

```python
import math
import jax
import jax.numpy as jnp
from jax import lax

MODEL_WIDTH = 5120
KEY_VALUE_HEADS = 4
GROUP = 5
HEAD_SIZE = 128
PADDED_RANK = 64
PLEN = 128
CL = 8
QUERY_HEADS = 20
COMP_ROWS = 2048
PROMPT_ROWS = 2048
N_PROMPT = 16
N_COMP = 16


def draw_frozen_query_base(key, part):
    key = jax.random.fold_in(key, 11)
    rows = N_COMP * COMP_ROWS
    width = QUERY_HEADS * HEAD_SIZE
    base = jnp.clip(jax.random.normal(key, (rows, width), jnp.float32), -4.5, 4.5)
    return base.reshape(N_COMP, COMP_ROWS, width).astype(jnp.bfloat16)


def draw_owner_prompt_keys(key, part):
    key = jax.random.fold_in(key, 13)
    rows = N_COMP * PROMPT_ROWS
    width = KEY_VALUE_HEADS * HEAD_SIZE
    base = jnp.clip(jax.random.normal(key, (rows, width), jnp.float32), -4.5, 4.5)
    return base.reshape(N_COMP, PROMPT_ROWS, width).astype(jnp.bfloat16)


def draw_lengths(key, part):
    key = jax.random.fold_in(key, 5)
    first, second = jax.random.split(key)
    base = jax.random.randint(first, (N_COMP, N_PROMPT, N_PROMPT), 1, CL + 1)
    full = jax.random.randint(second, (N_COMP, N_PROMPT, 1), 0, N_PROMPT)
    slot = jnp.arange(N_PROMPT)[None, None, :]
    return jnp.where(slot == full, CL, base).astype(jnp.int32)


def levels(own_key, dims, shards, smallest, largest):
    def one(axis_at, shards_of):
        steps = jax.random.uniform(jax.random.fold_in(jax.random.fold_in(own_key, 6), axis_at), (shards_of,), jnp.float32, smallest / len(shards), largest / len(shards))
        return jnp.repeat(jnp.exp(steps), dims[axis_at] // shards_of).reshape((-1,) + (1,) * (len(dims) - axis_at - 1))

    gain = one(*shards[0])
    for cut in shards[1:]:
        gain = gain * one(*cut)
    return gain


def scatter_about(own_key, dims, scale, bound, pieces=(), dtype=jnp.bfloat16):
    level = levels(own_key, dims, pieces, -0.22, 0.18) if pieces else 1.0
    drawn = jax.random.normal(own_key, dims, jnp.float32) * scale * level
    return jnp.minimum(jnp.maximum(drawn, -bound), bound).astype(dtype)


def setup_inputs(seed: int = 0) -> dict:
    arg_keys = jax.random.split(jax.random.key(seed), 13)
    normed_hidden_input = scatter_about(arg_keys[0], (N_COMP, COMP_ROWS, MODEL_WIDTH), 1.0, 6.0, ((0, 16), (1, 16)))
    frozen_query_base = draw_frozen_query_base(jax.random.fold_in(arg_keys[12], 71), 0)
    attention_output_grad = scatter_about(arg_keys[2], (N_COMP, COMP_ROWS, QUERY_HEADS * HEAD_SIZE), 1.0, 6.0, ((0, 16), (1, 16)))
    completion_keys = scatter_about(arg_keys[3], (N_COMP, COMP_ROWS, KEY_VALUE_HEADS * HEAD_SIZE), 1.0, 6.0, ((0, 16), (1, 16)))
    completion_values = scatter_about(arg_keys[4], (N_COMP, COMP_ROWS, KEY_VALUE_HEADS * HEAD_SIZE), 1.0, 6.0, ((0, 16), (1, 16)))
    owner_prompt_keys = draw_owner_prompt_keys(jax.random.fold_in(arg_keys[12], 71), 0)
    owner_prompt_values = scatter_about(arg_keys[6], (N_COMP, PROMPT_ROWS, KEY_VALUE_HEADS * HEAD_SIZE), 1.0, 6.0, ((0, 16), (1, 16)))
    adapter_down_weight = scatter_about(arg_keys[7], (MODEL_WIDTH, PADDED_RANK), MODEL_WIDTH ** -0.5, 0.078125)
    adapter_up_weight = scatter_about(arg_keys[8], (PADDED_RANK, QUERY_HEADS * HEAD_SIZE), PADDED_RANK ** -0.5, 0.75)
    adapter_rank = jax.random.randint(arg_keys[9], (1,), PADDED_RANK // 4, PADDED_RANK + 1).astype(jnp.int32)
    route = jax.vmap(lambda own: jax.random.permutation(own, N_PROMPT))(jax.random.split(arg_keys[10], N_COMP * N_PROMPT)).reshape((N_COMP, N_PROMPT, N_PROMPT)).astype(jnp.int32)
    lengths = draw_lengths(jax.random.fold_in(arg_keys[12], 71), 0)
    return {"normed_hidden_input": normed_hidden_input, "frozen_query_base": frozen_query_base, "attention_output_grad": attention_output_grad, "completion_keys": completion_keys, "completion_values": completion_values, "owner_prompt_keys": owner_prompt_keys, "owner_prompt_values": owner_prompt_values, "adapter_down_weight": adapter_down_weight, "adapter_up_weight": adapter_up_weight, "adapter_rank": adapter_rank, "route": route, "lengths": lengths}


adapter_strength = 32.0
masked_score = -1e+30

def self_mask(count):
    index = jnp.arange(count * CL)
    same = index[:, None] // CL == index[None, :] // CL
    causal = index[None, :] <= index[:, None]
    return same & causal

def rounded(values):
    return lax.optimization_barrier(values.astype(jnp.bfloat16)).astype(jnp.float32)

def per_device_step(hidden_rows, query_base_local, output_grad_local, self_key_local, self_value_local, owner_order, length_list, prompt_key_local, prompt_value_local, down_matrix, up_matrix, keep_mask, adapter_scale):
    count = owner_order.shape[0]
    token_rows = count * CL
    inv_sqrt = 1.0 / math.sqrt(HEAD_SIZE)
    low_rank_rows = (jnp.dot(hidden_rows, down_matrix, preferred_element_type=jnp.float32) * keep_mask).astype(jnp.bfloat16)
    query = (query_base_local.astype(jnp.float32) + adapter_scale * jnp.dot(low_rank_rows, up_matrix, preferred_element_type=jnp.float32)).astype(jnp.bfloat16)
    q_slots = query.astype(jnp.float32).reshape(count, CL, KEY_VALUE_HEADS, GROUP, HEAD_SIZE)
    q_tok = q_slots.reshape(token_rows, KEY_VALUE_HEADS, GROUP, HEAD_SIZE)
    prompt_key_rows = jnp.take(prompt_key_local, owner_order, axis=0).astype(jnp.float32)
    prompt_value_rows = jnp.take(prompt_value_local, owner_order, axis=0).astype(jnp.float32)
    self_key_rows = self_key_local.astype(jnp.float32).reshape(token_rows, KEY_VALUE_HEADS, HEAD_SIZE)
    self_value_rows = self_value_local.astype(jnp.float32).reshape(token_rows, KEY_VALUE_HEADS, HEAD_SIZE)
    sp = jnp.einsum('sqkgd,spkd->sqkgp', q_slots, prompt_key_rows) * inv_sqrt
    ss = jnp.einsum('qkgd,tkd->qkgt', q_tok, self_key_rows) * inv_sqrt
    ss = jnp.where(self_mask(count)[:, None, None, :], ss, masked_score)
    top = jnp.maximum(lax.optimization_barrier(jnp.max(sp, -1)).reshape(token_rows, KEY_VALUE_HEADS, GROUP), lax.optimization_barrier(jnp.max(ss, -1)))
    top_slots = top.reshape(count, CL, KEY_VALUE_HEADS, GROUP)
    total = lax.optimization_barrier(jnp.sum(jnp.exp(sp - top_slots[..., None]), -1)).reshape(token_rows, KEY_VALUE_HEADS, GROUP)
    total = total + lax.optimization_barrier(jnp.sum(jnp.exp(ss - top[..., None]), -1))
    lse = top + jnp.log(total)
    lse_slots = lse.reshape(count, CL, KEY_VALUE_HEADS, GROUP)
    pp = jnp.exp(sp - lse_slots[..., None])
    ps = jnp.exp(ss - lse[..., None])
    ppb = rounded(pp)
    psb = rounded(ps)
    attended = jnp.einsum('sqkgp,spkd->sqkgd', ppb, prompt_value_rows).reshape(token_rows, KEY_VALUE_HEADS, GROUP, HEAD_SIZE)
    attended = attended + jnp.einsum('qkgt,tkd->qkgd', psb, self_value_rows)
    live = (jnp.arange(CL)[None, :] < length_list[:, None]).reshape(token_rows)
    gmask = output_grad_local * live.astype(jnp.bfloat16)[:, None]
    g_tok = gmask.astype(jnp.float32).reshape(token_rows, KEY_VALUE_HEADS, GROUP, HEAD_SIZE)
    g_slots = g_tok.reshape(count, CL, KEY_VALUE_HEADS, GROUP, HEAD_SIZE)
    delta = lax.optimization_barrier(jnp.sum(g_tok * attended, -1))
    delta_slots = delta.reshape(count, CL, KEY_VALUE_HEADS, GROUP)
    dpp = jnp.einsum('sqkgd,spkd->sqkgp', g_slots, prompt_value_rows)
    dps = jnp.einsum('qkgd,tkd->qkgt', g_tok, self_value_rows)
    dsp = rounded(pp * (dpp - delta_slots[..., None]))
    dss = rounded(ps * (dps - delta[..., None]))
    dq = jnp.einsum('sqkgp,spkd->sqkgd', dsp, prompt_key_rows).reshape(token_rows, KEY_VALUE_HEADS, GROUP, HEAD_SIZE)
    dq = (dq + jnp.einsum('qkgt,tkd->qkgd', dss, self_key_rows)) * inv_sqrt
    query_grad_adapter = dq.reshape(token_rows, KEY_VALUE_HEADS * GROUP * HEAD_SIZE).astype(jnp.bfloat16)
    self_key_grad = (jnp.einsum('qkgt,qkgd->tkd', dss, q_tok) * inv_sqrt).reshape(token_rows, KEY_VALUE_HEADS * HEAD_SIZE).astype(jnp.bfloat16)
    self_value_grad = jnp.einsum('qkgt,qkgd->tkd', psb, g_tok).reshape(token_rows, KEY_VALUE_HEADS * HEAD_SIZE).astype(jnp.bfloat16)
    prompt_key_grad = jnp.einsum('sqkgp,sqkgd->spkd', dsp, q_slots) * inv_sqrt
    prompt_value_grad = jnp.einsum('sqkgp,sqkgd->spkd', ppb, g_slots)
    up_gradient = adapter_scale * jnp.dot(low_rank_rows.T, query_grad_adapter, preferred_element_type=jnp.float32)
    lifted_rows = (adapter_scale * jnp.dot(query_grad_adapter, up_matrix.T, preferred_element_type=jnp.float32) * keep_mask).astype(jnp.bfloat16)
    down_gradient = jnp.dot(hidden_rows.T, lifted_rows, preferred_element_type=jnp.float32)
    return (query_grad_adapter, self_key_grad, self_value_grad, prompt_key_grad, prompt_value_grad, down_gradient, up_gradient)

def reference(normed_hidden_input, frozen_query_base, attention_output_grad, completion_keys, completion_values, owner_prompt_keys, owner_prompt_values, adapter_down_weight, adapter_up_weight, adapter_rank, route, lengths):
    rank_value = adapter_rank[0]
    keep_mask = (jnp.arange(PADDED_RANK) < rank_value).astype(jnp.float32)
    adapter_scale = adapter_strength / rank_value.astype(jnp.float32)
    rows = N_PROMPT * CL

    def column(carry, items):
        xs, qs, gs, sks, svs, pks, pvs, orders, length_list = items
        prompt_key_rows = pks.reshape(N_PROMPT, PLEN, KEY_VALUE_HEADS, HEAD_SIZE)
        prompt_value_rows = pvs.reshape(N_PROMPT, PLEN, KEY_VALUE_HEADS, HEAD_SIZE)

        def device(inner, part_list):
            hidden_rows, query_base_local, output_grad_local, self_key_local, self_value_local, owner_order, token_length = part_list
            query_grad_adapter, self_key_grad, self_value_grad, prompt_key_grad, prompt_value_grad, down_gradient, up_gradient = per_device_step(hidden_rows, query_base_local, output_grad_local, self_key_local, self_value_local, owner_order, token_length, prompt_key_rows, prompt_value_rows, adapter_down_weight, adapter_up_weight, keep_mask, adapter_scale)
            acc_k, acc_v, acc_a, acc_b = inner
            acc_k = acc_k.at[owner_order].add(prompt_key_grad)
            acc_v = acc_v.at[owner_order].add(prompt_value_grad)
            return ((acc_k, acc_v, acc_a + down_gradient, acc_b + up_gradient), (query_grad_adapter, self_key_grad, self_value_grad))
        zero_kv = jnp.zeros((N_PROMPT, PLEN, KEY_VALUE_HEADS, HEAD_SIZE), jnp.float32)
        init = (zero_kv, zero_kv, carry[0], carry[1])
        part_list = (xs.reshape(N_PROMPT, rows, MODEL_WIDTH), qs.reshape(N_PROMPT, rows, -1), gs.reshape(N_PROMPT, rows, -1), sks.reshape(N_PROMPT, rows, -1), svs.reshape(N_PROMPT, rows, -1), orders, length_list)
        (acc_k, acc_v, acc_a, acc_b), (query_grad_adapter, self_key_grad, self_value_grad) = lax.scan(device, init, part_list)
        outs = (query_grad_adapter.reshape(N_PROMPT * rows, -1), self_key_grad.reshape(N_PROMPT * rows, -1), self_value_grad.reshape(N_PROMPT * rows, -1), acc_k.reshape(N_PROMPT * PLEN, KEY_VALUE_HEADS * HEAD_SIZE).astype(jnp.bfloat16), acc_v.reshape(N_PROMPT * PLEN, KEY_VALUE_HEADS * HEAD_SIZE).astype(jnp.bfloat16))
        return ((acc_a, acc_b), outs)
    init = (jnp.zeros((MODEL_WIDTH, PADDED_RANK), jnp.float32), jnp.zeros((PADDED_RANK, KEY_VALUE_HEADS * GROUP * HEAD_SIZE), jnp.float32))
    (down_gradient, up_gradient), outs = lax.scan(column, init, (normed_hidden_input, frozen_query_base, attention_output_grad, completion_keys, completion_values, owner_prompt_keys, owner_prompt_values, route, lengths))
    return (outs[0], outs[1], outs[2], outs[3], outs[4], down_gradient, up_gradient)
```

```python
import math

import jax
import jax.numpy as jnp
from jax import lax
from jax.experimental import pallas as pl
from jax.experimental.pallas import tpu as pltpu
from jax.sharding import PartitionSpec as P

KEY_VALUE_HEADS = 4
GROUP = 5
HEAD_SIZE = 128
PLEN = 128
CL = 8
SLOTS = 16
TOKENS = SLOTS * CL
QUERY_HEADS = KEY_VALUE_HEADS * GROUP
PAIRS = QUERY_HEADS // 2
HALF = PAIRS * HEAD_SIZE
KV_HALF = KEY_VALUE_HEADS * HEAD_SIZE // 2
ROWS = 2 * TOKENS
MODEL_WIDTH = 5120
PADDED_RANK = 64
QUERY_WIDTH = QUERY_HEADS * HEAD_SIZE
SEND_WIDTH = 2 * HALF + 128
BACK_WIDTH = HALF + 128
DOWN_BLOCKS = MODEL_WIDTH // 128
GRAD_BLOCKS = (MODEL_WIDTH + QUERY_WIDTH) // 128

INV_SQRT = 1.0 / math.sqrt(HEAD_SIZE)
adapter_strength = 32.0
masked_score = -1e30

BF16 = jnp.bfloat16
F32 = jnp.float32


def dot(a, b, dims):
    return lax.dot_general(a, b, (dims, ((), ())), preferred_element_type=F32)


def nt(a, b):
    return dot(a, b, ((1,), (1,)))


def nn(a, b):
    return dot(a, b, ((1,), (0,)))


def tn(a, b):
    return dot(a, b, ((0,), (0,)))


def fold(wide):
    width = wide.shape[1] // 2
    left = wide[:, :width].reshape(SLOTS, 1, CL, width)
    right = wide[:, width:].reshape(SLOTS, 1, CL, width)
    return jnp.concatenate([left, right], axis=1).reshape(ROWS, width)


def unfold(rows):
    split = rows.reshape(SLOTS, 2, CL, rows.shape[1])
    return split[:, 0].reshape(TOKENS, -1), split[:, 1].reshape(TOKENS, -1)


def own_mask():
    key = lax.broadcasted_iota(jnp.int32, (ROWS, ROWS), 0)
    row = lax.broadcasted_iota(jnp.int32, (ROWS, ROWS), 1)
    return (key // CL == row // CL) & (key <= row)


def pack_stats(rows):
    value = jnp.concatenate(rows, axis=0)
    first = value.astype(BF16).astype(F32)
    rest = value - first
    second = rest.astype(BF16).astype(F32)
    third = rest - second
    pad = jnp.zeros((128 - 3 * len(rows), ROWS), F32)
    return jnp.concatenate([first, second, third, pad], axis=0).T.astype(BF16)


def unpack_stats(columns, count):
    parts = columns.astype(F32).T
    return parts[:count] + (parts[count : 2 * count] + parts[2 * count : 3 * count])


def prepare_kernel(
    rank_ref, route_ref, length_ref, x_ref, base_ref, g_ref, sk_ref, sv_ref, wd_ref, wu_ref,
    low_ref, send_ref, rows_ref,
):
    rank = rank_ref[0]
    scale = adapter_strength / rank.astype(F32)
    keep = lax.broadcasted_iota(jnp.int32, (TOKENS, PADDED_RANK), 1) < rank
    low = jnp.where(keep, nn(x_ref[...], wd_ref[...]), 0.0).astype(BF16)
    low_ref[...] = low
    query = base_ref[...].astype(F32) + scale * nn(low, wu_ref[...])
    rows_ref[:, :HALF] = fold(query).astype(BF16)
    position = lax.broadcasted_iota(jnp.int32, (CL, 128), 0)
    live = jnp.concatenate(
        [jnp.where(position < length_ref[0, 0, s], 1.0, 0.0) for s in range(SLOTS)], axis=0
    )
    for n in range(PAIRS):
        left, right = (g_ref[:, m * 128 : (m + 1) * 128].astype(F32) * live for m in (n, n + PAIRS))
        rows_ref[:, HALF + n * 128 : HALF + (n + 1) * 128] = fold(
            jnp.concatenate([left, right], axis=1)
        ).astype(BF16)
    keys = fold(sk_ref[...].astype(F32)).astype(BF16)
    values = fold(sv_ref[...].astype(F32)).astype(BF16)
    mask = own_mask()
    lses, deltas = [], []
    for b in range(PAIRS):
        h = b // GROUP
        q = rows_ref[:, b * 128 : (b + 1) * 128]
        g = rows_ref[:, HALF + b * 128 : HALF + (b + 1) * 128]
        scores = jnp.where(mask, nt(keys[:, h * 128 : (h + 1) * 128], q) * INV_SQRT, masked_score)
        top = jnp.max(scores, axis=0, keepdims=True)
        weight = jnp.exp(scores - top)
        total = jnp.sum(weight, axis=0, keepdims=True)
        dprob = nt(values[:, h * 128 : (h + 1) * 128], g)
        lses.append(top + jnp.log(total))
        deltas.append(jnp.sum(weight * dprob, axis=0, keepdims=True) / total)
    rows_ref[:, 2 * HALF :] = pack_stats(lses + deltas)
    for s in range(SLOTS):
        send_ref[route_ref[0, 0, s]] = rows_ref[s * 16 : (s + 1) * 16, :]


def owner_kernel(rows_ref, k_ref, v_ref, back_ref, dk_ref, dv_ref):
    lower = lax.broadcasted_iota(jnp.int32, (PLEN, ROWS), 1) // CL % 2 == 0
    stats = unpack_stats(rows_ref[:, 2 * HALF :], 2 * PAIRS)

    def stacked(ref, h):
        return jnp.concatenate(
            [ref[:, m * 128 : (m + 1) * 128] for m in (h, h + 2)], axis=0
        )

    def picked(both):
        return jnp.where(lower, both[:PLEN], both[PLEN:])

    def spread(one):
        return jnp.concatenate(
            [jnp.where(lower, one, 0.0), jnp.where(lower, 0.0, one)], axis=0
        ).astype(BF16)

    lses, deltas = [], []
    for h in range(2):
        keys, values = stacked(k_ref, h), stacked(v_ref, h)
        dk = jnp.zeros((2 * PLEN, HEAD_SIZE), F32)
        dv = jnp.zeros((2 * PLEN, HEAD_SIZE), F32)
        for b in range(h * GROUP, (h + 1) * GROUP):
            q = rows_ref[:, b * 128 : (b + 1) * 128]
            g = rows_ref[:, HALF + b * 128 : HALF + (b + 1) * 128]
            own_lse, own_delta = stats[b : b + 1], stats[PAIRS + b : PAIRS + b + 1]
            scores = picked(nt(keys, q)) * INV_SQRT
            dprob = picked(nt(values, g))
            top = jnp.max(scores, axis=0, keepdims=True)
            weight = jnp.exp(scores - top)
            prompt_lse = top + jnp.log(jnp.sum(weight, axis=0, keepdims=True))
            high = jnp.maximum(prompt_lse, own_lse)
            lse = high + jnp.log(jnp.exp(prompt_lse - high) + jnp.exp(own_lse - high))
            probs = weight * jnp.exp(top - lse)
            probs_b = probs.astype(BF16).astype(F32)
            delta = jnp.sum(probs_b * dprob, axis=0, keepdims=True) + own_delta * jnp.exp(own_lse - lse)
            probs_2 = spread(probs_b)
            dscore_2 = spread(probs * (dprob - delta))
            dv = dv + nn(probs_2, g)
            dk = dk + nn(dscore_2, q)
            back_ref[:, b * 128 : (b + 1) * 128] = (tn(dscore_2, keys) * INV_SQRT).astype(BF16)
            lses.append(lse)
            deltas.append(delta)
        for at, m in ((0, h), (PLEN, h + 2)):
            dk_ref[:, m * 128 : (m + 1) * 128] = (dk[at : at + PLEN] * INV_SQRT).astype(BF16)
            dv_ref[:, m * 128 : (m + 1) * 128] = dv[at : at + PLEN].astype(BF16)
    back_ref[:, HALF:] = pack_stats(lses + deltas)


def finish_kernel(
    rank_ref, route_ref, x_ref, sk_ref, sv_ref, wu_ref, low_ref, send_ref, back_ref,
    dq_ref, dsk_ref, dsv_ref, grads_ref, rows_ref, dq_rows_ref,
):
    rank = rank_ref[0]
    scale = adapter_strength / rank.astype(F32)
    for s in range(SLOTS):
        owner = route_ref[0, 0, s]
        rows_ref[s * 16 : (s + 1) * 16, :] = send_ref[owner]
        dq_rows_ref[s * 16 : (s + 1) * 16, :] = back_ref[owner]
    keys = fold(sk_ref[...].astype(F32)).astype(BF16)
    values = fold(sv_ref[...].astype(F32)).astype(BF16)
    stats = unpack_stats(dq_rows_ref[:, HALF:], 2 * PAIRS)
    mask = own_mask()
    for h in range(2):
        k2, v2 = keys[:, h * 128 : (h + 1) * 128], values[:, h * 128 : (h + 1) * 128]
        dsk = jnp.zeros((ROWS, HEAD_SIZE), F32)
        dsv = jnp.zeros((ROWS, HEAD_SIZE), F32)
        for b in range(h * GROUP, (h + 1) * GROUP):
            q = rows_ref[:, b * 128 : (b + 1) * 128]
            g = rows_ref[:, HALF + b * 128 : HALF + (b + 1) * 128]
            lse, delta = stats[b : b + 1], stats[PAIRS + b : PAIRS + b + 1]
            probs = jnp.exp(jnp.where(mask, nt(k2, q) * INV_SQRT - lse, masked_score))
            dscore = (probs * (nt(v2, g) - delta)).astype(BF16)
            dsv = dsv + nn(probs.astype(BF16), g)
            dsk = dsk + nn(dscore, q)
            dq = dq_rows_ref[:, b * 128 : (b + 1) * 128].astype(F32) + tn(dscore, k2) * INV_SQRT
            for at, part in zip((b, b + PAIRS), unfold(dq)):
                dq_ref[0, :, at * 128 : (at + 1) * 128] = part.astype(BF16)
        for at, k_part, v_part in zip((h, h + 2), unfold(dsk * INV_SQRT), unfold(dsv)):
            dsk_ref[0, :, at * 128 : (at + 1) * 128] = k_part.astype(BF16)
            dsv_ref[0, :, at * 128 : (at + 1) * 128] = v_part.astype(BF16)
    dq = dq_ref[0]
    keep = lax.broadcasted_iota(jnp.int32, (TOKENS, PADDED_RANK), 1) < rank
    lifted = jnp.where(keep, scale * nt(dq, wu_ref[...]), 0.0).astype(BF16)
    down = tn(lifted, x_ref[...])
    up = scale * tn(low_ref[...], dq)
    for c in range(GRAD_BLOCKS):
        part = (
            down[:, c * 128 : (c + 1) * 128]
            if c < DOWN_BLOCKS
            else up[:, (c - DOWN_BLOCKS) * 128 : (c - DOWN_BLOCKS + 1) * 128]
        )
        grads_ref[c * PADDED_RANK : (c + 1) * PADDED_RANK, :] = part.astype(BF16)


def spread_kernel(grads_ref, down_ref, up_ref):
    for c in range(GRAD_BLOCKS):
        part = grads_ref[c * PADDED_RANK : (c + 1) * PADDED_RANK, :].astype(F32)
        if c < DOWN_BLOCKS:
            down_ref[c * 128 : (c + 1) * 128, :] = part.T
        else:
            at = (c - DOWN_BLOCKS) * 128
            up_ref[:, at : at + 128] = part


VMEM = pl.BlockSpec(memory_space=pltpu.VMEM)
SMEM = pl.BlockSpec(memory_space=pltpu.SMEM)


def call(kernel, in_specs, outs, scratch=()):
    return pl.pallas_call(
        kernel,
        out_shape=[jax.ShapeDtypeStruct(shape, dtype) for shape, dtype in outs],
        in_specs=in_specs,
        out_specs=[VMEM] * len(outs),
        scratch_shapes=list(scratch),
        compiler_params=pltpu.CompilerParams(vmem_limit_bytes=48 * 1024 * 1024),
    )


def replicate(part, count):
    return jnp.broadcast_to(part[None], (count,) + part.shape)


def sum_all(grads):
    rows = GRAD_BLOCKS * PADDED_RANK
    parts = lax.all_to_all(grads.reshape(16, rows // 16, 128), "comp", 0, 0, tiled=True)
    total = jnp.sum(parts.astype(F32), axis=0)
    flips = (
        lambda i: i ^ 4,
        lambda i: (3 - i // 4) * 4 + i % 4,
        lambda i: i ^ 1,
        lambda i: i // 4 * 4 + 3 - i % 4,
    )
    for flip in flips:
        total = total + lax.ppermute(total, "prompt", [(i, flip(i)) for i in range(16)])
    whole = lax.all_to_all(replicate(total.astype(BF16), 16), "comp", 0, 0, tiled=True)
    return whole.reshape(rows, 128)


def per_device(
    normed_hidden_input,
    frozen_query_base,
    attention_output_grad,
    completion_keys,
    completion_values,
    owner_prompt_keys,
    owner_prompt_values,
    adapter_down_weight,
    adapter_up_weight,
    adapter_rank,
    route,
    lengths,
):
    hidden = normed_hidden_input[0]
    keys, values = completion_keys[0], completion_values[0]
    low, send = call(
        prepare_kernel,
        [SMEM] * 3 + [VMEM] * 7,
        [((TOKENS, PADDED_RANK), BF16), ((SLOTS, 16, SEND_WIDTH), BF16)],
        [pltpu.VMEM((ROWS, SEND_WIDTH), BF16)],
    )(
        adapter_rank, route, lengths, hidden, frozen_query_base[0], attention_output_grad[0],
        keys, values, adapter_down_weight, adapter_up_weight,
    )
    arrived = lax.all_to_all(send, "prompt", 0, 0, tiled=True)
    back, dk, dv = call(
        owner_kernel,
        [VMEM] * 3,
        [((ROWS, BACK_WIDTH), BF16)] + [((PLEN, KEY_VALUE_HEADS * HEAD_SIZE), BF16)] * 2,
    )(arrived.reshape(ROWS, SEND_WIDTH), owner_prompt_keys[0], owner_prompt_values[0])
    back = lax.all_to_all(back.reshape(SLOTS, 16, BACK_WIDTH), "prompt", 0, 0, tiled=True)
    dq, dsk, dsv, grads = call(
        finish_kernel,
        [SMEM] * 2 + [VMEM] * 7,
        [
            ((1, TOKENS, QUERY_WIDTH), BF16),
            ((1, TOKENS, KEY_VALUE_HEADS * HEAD_SIZE), BF16),
            ((1, TOKENS, KEY_VALUE_HEADS * HEAD_SIZE), BF16),
            ((GRAD_BLOCKS * PADDED_RANK, 128), BF16),
        ],
        [pltpu.VMEM((ROWS, SEND_WIDTH), BF16), pltpu.VMEM((ROWS, BACK_WIDTH), BF16)],
    )(adapter_rank, route, hidden, keys, values, adapter_up_weight, low, send, back)
    down, up = call(
        spread_kernel,
        [VMEM],
        [((MODEL_WIDTH, PADDED_RANK), F32), ((PADDED_RANK, QUERY_WIDTH), F32)],
    )(sum_all(grads))
    return dq, dsk, dsv, dk[None], dv[None], down, up


def solution(mesh):
    split = P("comp", "prompt", None)
    return jax.shard_map(
        per_device,
        mesh=mesh,
        in_specs=(split,) * 7 + (P(),) * 3 + (split,) * 2,
        out_specs=(split,) * 5 + (P(),) * 2,
        check_vma=False,
    )
```

```python
import math

import jax
import jax.numpy as jnp
from jax import lax
from jax.experimental import pallas as pl
from jax.experimental.pallas import tpu as pltpu
from jax.sharding import PartitionSpec as P

KEY_VALUE_HEADS = 4
GROUP = 5
HEAD_SIZE = 128
PLEN = 128
CL = 8
SLOTS = 16
TOKENS = SLOTS * CL
QUERY_HEADS = KEY_VALUE_HEADS * GROUP
PAIRS = QUERY_HEADS // 2
HALF = PAIRS * HEAD_SIZE
KV_HALF = KEY_VALUE_HEADS * HEAD_SIZE // 2
ROWS = 2 * TOKENS
MODEL_WIDTH = 5120
PADDED_RANK = 64
QUERY_WIDTH = QUERY_HEADS * HEAD_SIZE
SEND_WIDTH = 2 * HALF + 128
BACK_WIDTH = HALF + 128
DOWN_BLOCKS = MODEL_WIDTH // 128
GRAD_BLOCKS = (MODEL_WIDTH + QUERY_WIDTH) // 128

INV_SQRT = 1.0 / math.sqrt(HEAD_SIZE)
adapter_strength = 32.0
masked_score = -1e30

BF16 = jnp.bfloat16
F32 = jnp.float32


def dot(a, b, dims):
    return lax.dot_general(a, b, (dims, ((), ())), preferred_element_type=F32)


def nt(a, b):
    return dot(a, b, ((1,), (1,)))


def nn(a, b):
    return dot(a, b, ((1,), (0,)))


def tn(a, b):
    return dot(a, b, ((0,), (0,)))


def fold(wide):
    width = wide.shape[1] // 2
    left = wide[:, :width].reshape(SLOTS, 1, CL, width)
    right = wide[:, width:].reshape(SLOTS, 1, CL, width)
    return jnp.concatenate([left, right], axis=1).reshape(ROWS, width)


def unfold(rows):
    split = rows.reshape(SLOTS, 2, CL, rows.shape[1])
    return split[:, 0].reshape(TOKENS, -1), split[:, 1].reshape(TOKENS, -1)


def own_mask():
    key = lax.broadcasted_iota(jnp.int32, (TOKENS, ROWS), 0)
    row = lax.broadcasted_iota(jnp.int32, (TOKENS, ROWS), 1) % TOKENS
    return (key // CL == row // CL) & (key <= row)


def own_scores(keys, rows):
    return jnp.concatenate(
        [nt(keys[at : at + TOKENS], rows[at : at + TOKENS]) for at in (0, TOKENS)], axis=1
    )


def own_product(scores, rows, product):
    return jnp.concatenate(
        [product(scores[:, at : at + TOKENS], rows[at : at + TOKENS]) for at in (0, TOKENS)], axis=0
    )


def pack_stats(rows):
    value = jnp.concatenate(rows, axis=0)
    first = value.astype(BF16).astype(F32)
    rest = value - first
    second = rest.astype(BF16).astype(F32)
    third = rest - second
    pad = jnp.zeros((128 - 3 * len(rows), ROWS), F32)
    return jnp.concatenate([first, second, third, pad], axis=0).T.astype(BF16)


def unpack_stats(columns, count):
    parts = columns.astype(F32).T
    return parts[:count] + (parts[count : 2 * count] + parts[2 * count : 3 * count])


def prepare_kernel(
    rank_ref, route_ref, length_ref, x_hbm, base_hbm, g_hbm, sk_hbm, sv_hbm, wd_hbm, wu_hbm,
    low_ref, send_ref, rows_ref,
    x_ref, base_ref, g_ref, sk_ref, sv_ref, wd_ref, wu_ref, sems,
):
    sources = (g_hbm, sv_hbm, sk_hbm, wd_hbm, x_hbm, wu_hbm, base_hbm)
    targets = (g_ref, sv_ref, sk_ref, wd_ref, x_ref, wu_ref, base_ref)
    copies = [
        pltpu.make_async_copy(source, target, sems.at[i])
        for i, (source, target) in enumerate(zip(sources, targets))
    ]
    for copy in copies:
        copy.start()
    rank = rank_ref[0]
    scale = adapter_strength / rank.astype(F32)
    position = lax.broadcasted_iota(jnp.int32, (CL, 128), 0)
    live = jnp.concatenate(
        [jnp.where(position < length_ref[0, 0, s], 1.0, 0.0) for s in range(SLOTS)], axis=0
    )
    mask = own_mask()
    copies[0].wait()
    for n in range(PAIRS):
        left, right = (g_ref[:, m * 128 : (m + 1) * 128].astype(F32) * live for m in (n, n + PAIRS))
        rows_ref[:, HALF + n * 128 : HALF + (n + 1) * 128] = fold(
            jnp.concatenate([left, right], axis=1)
        ).astype(BF16)
    copies[1].wait()
    values = fold(sv_ref[...].astype(F32)).astype(BF16)
    copies[2].wait()
    keys = fold(sk_ref[...].astype(F32)).astype(BF16)
    copies[3].wait()
    copies[4].wait()
    keep = lax.broadcasted_iota(jnp.int32, (TOKENS, PADDED_RANK), 1) < rank
    low = jnp.where(keep, nt(x_ref[...], wd_ref[...]), 0.0).astype(BF16)
    low_ref[...] = low
    copies[5].wait()
    copies[6].wait()
    lses, deltas = [], []
    for b in range(PAIRS):
        h = b // GROUP
        left, right = (
            base_ref[:, m * 128 : (m + 1) * 128].astype(F32)
            + scale * nn(low, wu_ref[:, m * 128 : (m + 1) * 128])
            for m in (b, b + PAIRS)
        )
        q = fold(jnp.concatenate([left, right], axis=1)).astype(BF16)
        rows_ref[:, b * 128 : (b + 1) * 128] = q
        g = rows_ref[:, HALF + b * 128 : HALF + (b + 1) * 128]
        scores = jnp.where(
            mask, own_scores(keys[:, h * 128 : (h + 1) * 128], q) * INV_SQRT, masked_score
        )
        top = jnp.max(scores, axis=0, keepdims=True)
        weight = jnp.exp(scores - top)
        total = jnp.sum(weight, axis=0, keepdims=True)
        dprob = own_scores(values[:, h * 128 : (h + 1) * 128], g)
        lses.append(top + jnp.log(total))
        deltas.append(jnp.sum(weight * dprob, axis=0, keepdims=True) / total)
    rows_ref[:, 2 * HALF :] = pack_stats(lses + deltas)
    for s in range(SLOTS):
        send_ref[route_ref[0, 0, s]] = rows_ref[s * 16 : (s + 1) * 16, :]


def owner_kernel(rows_ref, k_ref, v_ref, back_ref, dk_ref, dv_ref):
    lower = (lax.broadcasted_iota(jnp.int32, (ROWS, HEAD_SIZE), 0) // CL % 2 == 0).astype(F32)
    lower, upper = lower.astype(BF16), (1.0 - lower).astype(BF16)
    stats = unpack_stats(rows_ref[:, 2 * HALF :], 2 * PAIRS)

    def beside(ref, h):
        return jnp.concatenate([ref[:, m * 128 : (m + 1) * 128] for m in (h, h + 2)], axis=1)

    def apart(rows):
        return jnp.concatenate([rows * lower, rows * upper], axis=1)

    lses, deltas = [], []
    for h in range(2):
        keys, values = beside(k_ref, h), beside(v_ref, h)
        dk = jnp.zeros((PLEN, 2 * HEAD_SIZE), F32)
        dv = jnp.zeros((PLEN, 2 * HEAD_SIZE), F32)
        for b in range(h * GROUP, (h + 1) * GROUP):
            q = apart(rows_ref[:, b * 128 : (b + 1) * 128])
            g = apart(rows_ref[:, HALF + b * 128 : HALF + (b + 1) * 128])
            own_lse, own_delta = stats[b : b + 1], stats[PAIRS + b : PAIRS + b + 1]
            scores = nt(keys, q) * INV_SQRT
            dprob = nt(values, g)
            top = jnp.max(scores, axis=0, keepdims=True)
            weight = jnp.exp(scores - top)
            prompt_lse = top + jnp.log(jnp.sum(weight, axis=0, keepdims=True))
            high = jnp.maximum(prompt_lse, own_lse)
            lse = high + jnp.log(jnp.exp(prompt_lse - high) + jnp.exp(own_lse - high))
            probs = weight * jnp.exp(top - lse)
            probs_b = probs.astype(BF16)
            delta = jnp.sum(probs_b.astype(F32) * dprob, axis=0, keepdims=True) + own_delta * jnp.exp(
                own_lse - lse
            )
            dscore = (probs * (dprob - delta)).astype(BF16)
            dv = dv + nn(probs_b, g)
            dk = dk + nn(dscore, q)
            dq = (tn(dscore, keys) * INV_SQRT).reshape(SLOTS, 2, CL, 2 * HEAD_SIZE)
            dq = jnp.concatenate([dq[:, :1, :, :HEAD_SIZE], dq[:, 1:, :, HEAD_SIZE:]], axis=1)
            back_ref[:, b * 128 : (b + 1) * 128] = dq.reshape(ROWS, HEAD_SIZE).astype(BF16)
            lses.append(lse)
            deltas.append(delta)
        for at, m in ((0, h), (HEAD_SIZE, h + 2)):
            dk_ref[:, m * 128 : (m + 1) * 128] = (dk[:, at : at + HEAD_SIZE] * INV_SQRT).astype(BF16)
            dv_ref[:, m * 128 : (m + 1) * 128] = dv[:, at : at + HEAD_SIZE].astype(BF16)
    back_ref[:, HALF:] = pack_stats(lses + deltas)


def finish_kernel(
    rank_ref, route_ref, x_ref, sk_ref, sv_ref, wu_ref, low_ref, rows_ref, back_ref,
    dq_ref, dsk_ref, dsv_ref, grads_ref, dq_rows_ref,
):
    rank = rank_ref[0]
    scale = adapter_strength / rank.astype(F32)
    for s in range(SLOTS):
        dq_rows_ref[s * 16 : (s + 1) * 16, :] = back_ref[route_ref[0, 0, s]]
    keys = fold(sk_ref[...].astype(F32)).astype(BF16)
    values = fold(sv_ref[...].astype(F32)).astype(BF16)
    stats = unpack_stats(dq_rows_ref[:, HALF:], 2 * PAIRS)
    mask = own_mask()
    for h in range(2):
        k2, v2 = keys[:, h * 128 : (h + 1) * 128], values[:, h * 128 : (h + 1) * 128]
        dsk = jnp.zeros((ROWS, HEAD_SIZE), F32)
        dsv = jnp.zeros((ROWS, HEAD_SIZE), F32)
        for b in range(h * GROUP, (h + 1) * GROUP):
            q = rows_ref[:, b * 128 : (b + 1) * 128]
            g = rows_ref[:, HALF + b * 128 : HALF + (b + 1) * 128]
            lse, delta = stats[b : b + 1], stats[PAIRS + b : PAIRS + b + 1]
            probs = jnp.exp(jnp.where(mask, own_scores(k2, q) * INV_SQRT - lse, masked_score))
            dscore = (probs * (own_scores(v2, g) - delta)).astype(BF16)
            dsv = dsv + own_product(probs.astype(BF16), g, nn)
            dsk = dsk + own_product(dscore, q, nn)
            dq = dq_rows_ref[:, b * 128 : (b + 1) * 128].astype(F32)
            dq = dq + own_product(dscore, k2, tn) * INV_SQRT
            for at, part in zip((b, b + PAIRS), unfold(dq)):
                dq_ref[0, :, at * 128 : (at + 1) * 128] = part.astype(BF16)
        for at, k_part, v_part in zip((h, h + 2), unfold(dsk * INV_SQRT), unfold(dsv)):
            dsk_ref[0, :, at * 128 : (at + 1) * 128] = k_part.astype(BF16)
            dsv_ref[0, :, at * 128 : (at + 1) * 128] = v_part.astype(BF16)
    dq = dq_ref[0]
    keep = lax.broadcasted_iota(jnp.int32, (TOKENS, PADDED_RANK), 1) < rank
    lifted = jnp.where(keep, scale * nt(dq, wu_ref[...]), 0.0).astype(BF16)
    low = low_ref[...]
    for c in range(GRAD_BLOCKS):
        if c < DOWN_BLOCKS:
            part = tn(lifted, x_ref[:, c * 128 : (c + 1) * 128])
        else:
            at = (c - DOWN_BLOCKS) * 128
            part = scale * tn(low, dq[:, at : at + 128])
        grads_ref[c * PADDED_RANK : (c + 1) * PADDED_RANK, :] = part.astype(BF16)


def spread_kernel(grads_ref, down_ref, up_ref):
    for c in range(GRAD_BLOCKS):
        part = grads_ref[c * PADDED_RANK : (c + 1) * PADDED_RANK, :].astype(F32)
        if c < DOWN_BLOCKS:
            down_ref[:, c * 128 : (c + 1) * 128] = part
        else:
            at = (c - DOWN_BLOCKS) * 128
            up_ref[:, at : at + 128] = part


VMEM = pl.BlockSpec(memory_space=pltpu.VMEM)
SMEM = pl.BlockSpec(memory_space=pltpu.SMEM)
HBM = pl.BlockSpec(memory_space=pltpu.HBM)


def call(kernel, in_specs, outs, scratch=()):
    return pl.pallas_call(
        kernel,
        out_shape=[jax.ShapeDtypeStruct(shape, dtype) for shape, dtype in outs],
        in_specs=in_specs,
        out_specs=[VMEM] * len(outs),
        scratch_shapes=list(scratch),
        compiler_params=pltpu.CompilerParams(vmem_limit_bytes=48 * 1024 * 1024),
    )


def replicate(part, count):
    return jnp.broadcast_to(part[None], (count,) + part.shape)


def sum_all(grads):
    rows = GRAD_BLOCKS * PADDED_RANK
    parts = lax.all_to_all(grads.reshape(16, rows // 16, 128), "comp", 0, 0, tiled=True)
    total = jnp.sum(parts.astype(F32), axis=0)
    flips = (
        lambda i: i ^ 4,
        lambda i: (3 - i // 4) * 4 + i % 4,
        lambda i: i ^ 1,
        lambda i: i // 4 * 4 + 3 - i % 4,
    )
    for flip in flips:
        total = total + lax.ppermute(total, "prompt", [(i, flip(i)) for i in range(16)])
    whole = lax.all_to_all(replicate(total.astype(BF16), 16), "comp", 0, 0, tiled=True)
    return whole.reshape(rows, 128)


def per_device(
    normed_hidden_input,
    frozen_query_base,
    attention_output_grad,
    completion_keys,
    completion_values,
    owner_prompt_keys,
    owner_prompt_values,
    adapter_down_weight,
    adapter_up_weight,
    adapter_rank,
    route,
    lengths,
):
    hidden = normed_hidden_input[0]
    keys, values = completion_keys[0], completion_values[0]
    arrays = (
        hidden, frozen_query_base[0], attention_output_grad[0], keys, values,
        adapter_down_weight.T, adapter_up_weight,
    )
    low, send, rows = call(
        prepare_kernel,
        [SMEM] * 3 + [HBM] * 7,
        [
            ((TOKENS, PADDED_RANK), BF16),
            ((SLOTS, 16, SEND_WIDTH), BF16),
            ((ROWS, SEND_WIDTH), BF16),
        ],
        [pltpu.VMEM(a.shape, BF16) for a in arrays] + [pltpu.SemaphoreType.DMA((7,))],
    )(adapter_rank, route, lengths, *arrays)
    arrived = lax.all_to_all(send, "prompt", 0, 0, tiled=True)
    back, dk, dv = call(
        owner_kernel,
        [VMEM] * 3,
        [((ROWS, BACK_WIDTH), BF16)] + [((PLEN, KEY_VALUE_HEADS * HEAD_SIZE), BF16)] * 2,
    )(arrived.reshape(ROWS, SEND_WIDTH), owner_prompt_keys[0], owner_prompt_values[0])
    back = lax.all_to_all(back.reshape(SLOTS, 16, BACK_WIDTH), "prompt", 0, 0, tiled=True)
    dq, dsk, dsv, grads = call(
        finish_kernel,
        [SMEM] * 2 + [VMEM] * 7,
        [
            ((1, TOKENS, QUERY_WIDTH), BF16),
            ((1, TOKENS, KEY_VALUE_HEADS * HEAD_SIZE), BF16),
            ((1, TOKENS, KEY_VALUE_HEADS * HEAD_SIZE), BF16),
            ((GRAD_BLOCKS * PADDED_RANK, 128), BF16),
        ],
        [pltpu.VMEM((ROWS, BACK_WIDTH), BF16)],
    )(adapter_rank, route, hidden, keys, values, adapter_up_weight, low, rows, back)
    down, up = call(
        spread_kernel,
        [VMEM],
        [((PADDED_RANK, MODEL_WIDTH), F32), ((PADDED_RANK, QUERY_WIDTH), F32)],
    )(sum_all(grads))
    return dq, dsk, dsv, dk[None], dv[None], down.T, up


def solution(mesh):
    split = P("comp", "prompt", None)
    return jax.shard_map(
        per_device,
        mesh=mesh,
        in_specs=(split,) * 7 + (P(),) * 3 + (split,) * 2,
        out_specs=(split,) * 5 + (P(),) * 2,
        check_vma=False,
    )
```

```python
import math

import jax
import jax.numpy as jnp
from jax import lax
from jax.experimental import pallas as pl
from jax.experimental.pallas import tpu as pltpu
from jax.sharding import PartitionSpec as P

KEY_VALUE_HEADS = 4
GROUP = 5
HEAD_SIZE = 128
PLEN = 128
CL = 8
SLOTS = 16
TOKENS = SLOTS * CL
QUERY_HEADS = KEY_VALUE_HEADS * GROUP
PAIRS = QUERY_HEADS // 2
HALF = PAIRS * HEAD_SIZE
KV_HALF = KEY_VALUE_HEADS * HEAD_SIZE // 2
ROWS = 2 * TOKENS
MODEL_WIDTH = 5120
PADDED_RANK = 64
QUERY_WIDTH = QUERY_HEADS * HEAD_SIZE
SEND_WIDTH = 2 * HALF + 128
BACK_WIDTH = HALF + 128
DOWN_BLOCKS = MODEL_WIDTH // 128
GRAD_BLOCKS = (MODEL_WIDTH + QUERY_WIDTH) // 128

INV_SQRT = 1.0 / math.sqrt(HEAD_SIZE)
adapter_strength = 32.0
masked_score = -1e30

BF16 = jnp.bfloat16
F32 = jnp.float32


def dot(a, b, dims):
    return lax.dot_general(a, b, (dims, ((), ())), preferred_element_type=F32)


def nt(a, b):
    return dot(a, b, ((1,), (1,)))


def nn(a, b):
    return dot(a, b, ((1,), (0,)))


def tn(a, b):
    return dot(a, b, ((0,), (0,)))


def fold(wide):
    width = wide.shape[1] // 2
    left = wide[:, :width].reshape(SLOTS, 1, CL, width)
    right = wide[:, width:].reshape(SLOTS, 1, CL, width)
    return jnp.concatenate([left, right], axis=1).reshape(ROWS, width)


def unfold(rows):
    split = rows.reshape(SLOTS, 2, CL, rows.shape[1])
    return split[:, 0].reshape(TOKENS, -1), split[:, 1].reshape(TOKENS, -1)


def own_mask():
    key = lax.broadcasted_iota(jnp.int32, (TOKENS, ROWS), 0)
    row = lax.broadcasted_iota(jnp.int32, (TOKENS, ROWS), 1) % TOKENS
    return (key // CL == row // CL) & (key <= row)


def own_scores(keys, rows):
    return jnp.concatenate(
        [nt(keys[at : at + TOKENS], rows[at : at + TOKENS]) for at in (0, TOKENS)], axis=1
    )


def own_product(scores, rows, product):
    return jnp.concatenate(
        [product(scores[:, at : at + TOKENS], rows[at : at + TOKENS]) for at in (0, TOKENS)], axis=0
    )


def pack_stats(rows):
    value = jnp.concatenate(rows, axis=0)
    first = value.astype(BF16).astype(F32)
    rest = value - first
    second = rest.astype(BF16).astype(F32)
    third = rest - second
    pad = jnp.zeros((128 - 3 * len(rows), ROWS), F32)
    return jnp.concatenate([first, second, third, pad], axis=0).T.astype(BF16)


def unpack_stats(columns, count):
    parts = columns.astype(F32).T
    return parts[:count] + (parts[count : 2 * count] + parts[2 * count : 3 * count])


def prepare_kernel(
    rank_ref, route_ref, length_ref, x_hbm, base_hbm, g_hbm, sk_hbm, sv_hbm, wd_hbm, wu_hbm,
    low_ref, send_hbm,
    x_ref, base_ref, g_ref, sk_ref, sv_ref, wd_ref, wu_ref, rows_ref, sems,
):
    sources = (g_hbm, sv_hbm, sk_hbm, wd_hbm, x_hbm, wu_hbm, base_hbm)
    targets = (g_ref, sv_ref, sk_ref, wd_ref, x_ref, wu_ref, base_ref)
    copies = [
        pltpu.make_async_copy(source, target, sems.at[i])
        for i, (source, target) in enumerate(zip(sources, targets))
    ]
    for copy in copies:
        copy.start()
    rank = rank_ref[0]
    scale = adapter_strength / rank.astype(F32)
    position = lax.broadcasted_iota(jnp.int32, (CL, 128), 0)
    live = jnp.concatenate(
        [jnp.where(position < length_ref[0, 0, s], 1.0, 0.0) for s in range(SLOTS)], axis=0
    )
    mask = own_mask()
    copies[0].wait()
    for n in range(PAIRS):
        left, right = (g_ref[:, m * 128 : (m + 1) * 128].astype(F32) * live for m in (n, n + PAIRS))
        rows_ref[:, HALF + n * 128 : HALF + (n + 1) * 128] = fold(
            jnp.concatenate([left, right], axis=1)
        ).astype(BF16)
    copies[1].wait()
    values = fold(sv_ref[...].astype(F32)).astype(BF16)
    copies[2].wait()
    keys = fold(sk_ref[...].astype(F32)).astype(BF16)
    copies[3].wait()
    copies[4].wait()
    keep = lax.broadcasted_iota(jnp.int32, (TOKENS, PADDED_RANK), 1) < rank
    low = jnp.where(keep, nt(x_ref[...], wd_ref[...]), 0.0).astype(BF16)
    low_ref[...] = low
    copies[5].wait()
    copies[6].wait()
    lses, deltas = [], []
    for b in range(PAIRS):
        h = b // GROUP
        left, right = (
            base_ref[:, m * 128 : (m + 1) * 128].astype(F32)
            + scale * nn(low, wu_ref[:, m * 128 : (m + 1) * 128])
            for m in (b, b + PAIRS)
        )
        q = fold(jnp.concatenate([left, right], axis=1)).astype(BF16)
        rows_ref[:, b * 128 : (b + 1) * 128] = q
        g = rows_ref[:, HALF + b * 128 : HALF + (b + 1) * 128]
        scores = jnp.where(
            mask, own_scores(keys[:, h * 128 : (h + 1) * 128], q) * INV_SQRT, masked_score
        )
        top = jnp.max(scores, axis=0, keepdims=True)
        weight = jnp.exp(scores - top)
        total = jnp.sum(weight, axis=0, keepdims=True)
        dprob = own_scores(values[:, h * 128 : (h + 1) * 128], g)
        lses.append(top + jnp.log(total))
        deltas.append(jnp.sum(weight * dprob, axis=0, keepdims=True) / total)
    rows_ref[:, 2 * HALF :] = pack_stats(lses + deltas)
    sends = [
        pltpu.make_async_copy(
            rows_ref.at[pl.ds(s * 16, 16)], send_hbm.at[route_ref[0, 0, s]], sems.at[7 + s]
        )
        for s in range(SLOTS)
    ]
    for copy in sends:
        copy.start()
    for copy in sends:
        copy.wait()


def owner_kernel(rows_ref, k_ref, v_ref, back_ref, dk_ref, dv_ref):
    lower = (lax.broadcasted_iota(jnp.int32, (ROWS, HEAD_SIZE), 0) // CL % 2 == 0).astype(F32)
    lower, upper = lower.astype(BF16), (1.0 - lower).astype(BF16)
    stats = unpack_stats(rows_ref[:, 2 * HALF :], 2 * PAIRS)

    def beside(ref, h):
        return jnp.concatenate([ref[:, m * 128 : (m + 1) * 128] for m in (h, h + 2)], axis=1)

    def apart(rows):
        return jnp.concatenate([rows * lower, rows * upper], axis=1)

    lses, deltas = [], []
    for h in range(2):
        keys, values = beside(k_ref, h), beside(v_ref, h)
        dk = jnp.zeros((PLEN, 2 * HEAD_SIZE), F32)
        dv = jnp.zeros((PLEN, 2 * HEAD_SIZE), F32)
        for b in range(h * GROUP, (h + 1) * GROUP):
            q = apart(rows_ref[:, b * 128 : (b + 1) * 128])
            g = apart(rows_ref[:, HALF + b * 128 : HALF + (b + 1) * 128])
            own_lse, own_delta = stats[b : b + 1], stats[PAIRS + b : PAIRS + b + 1]
            scores = nt(keys, q) * INV_SQRT
            dprob = nt(values, g)
            top = jnp.max(scores, axis=0, keepdims=True)
            weight = jnp.exp(scores - top)
            prompt_lse = top + jnp.log(jnp.sum(weight, axis=0, keepdims=True))
            high = jnp.maximum(prompt_lse, own_lse)
            lse = high + jnp.log(jnp.exp(prompt_lse - high) + jnp.exp(own_lse - high))
            probs = weight * jnp.exp(top - lse)
            probs_b = probs.astype(BF16)
            delta = jnp.sum(probs_b.astype(F32) * dprob, axis=0, keepdims=True) + own_delta * jnp.exp(
                own_lse - lse
            )
            dscore = (probs * (dprob - delta)).astype(BF16)
            dv = dv + nn(probs_b, g)
            dk = dk + nn(dscore, q)
            dq = (tn(dscore, keys) * INV_SQRT).reshape(SLOTS, 2, CL, 2 * HEAD_SIZE)
            dq = jnp.concatenate([dq[:, :1, :, :HEAD_SIZE], dq[:, 1:, :, HEAD_SIZE:]], axis=1)
            back_ref[:, b * 128 : (b + 1) * 128] = dq.reshape(ROWS, HEAD_SIZE).astype(BF16)
            lses.append(lse)
            deltas.append(delta)
        for at, m in ((0, h), (HEAD_SIZE, h + 2)):
            dk_ref[:, m * 128 : (m + 1) * 128] = (dk[:, at : at + HEAD_SIZE] * INV_SQRT).astype(BF16)
            dv_ref[:, m * 128 : (m + 1) * 128] = dv[:, at : at + HEAD_SIZE].astype(BF16)
    back_ref[:, HALF:] = pack_stats(lses + deltas)


def finish_kernel(
    rank_ref, route_ref, x_ref, sk_ref, sv_ref, wu_ref, low_ref, send_ref, back_ref,
    dq_ref, dsk_ref, dsv_ref, grads_ref, rows_ref, dq_rows_ref,
):
    rank = rank_ref[0]
    scale = adapter_strength / rank.astype(F32)
    for s in range(SLOTS):
        owner = route_ref[0, 0, s]
        rows_ref[s * 16 : (s + 1) * 16, :] = send_ref[owner]
        dq_rows_ref[s * 16 : (s + 1) * 16, :] = back_ref[owner]
    keys = fold(sk_ref[...].astype(F32)).astype(BF16)
    values = fold(sv_ref[...].astype(F32)).astype(BF16)
    stats = unpack_stats(dq_rows_ref[:, HALF:], 2 * PAIRS)
    mask = own_mask()
    for h in range(2):
        k2, v2 = keys[:, h * 128 : (h + 1) * 128], values[:, h * 128 : (h + 1) * 128]
        dsk = jnp.zeros((ROWS, HEAD_SIZE), F32)
        dsv = jnp.zeros((ROWS, HEAD_SIZE), F32)
        for b in range(h * GROUP, (h + 1) * GROUP):
            q = rows_ref[:, b * 128 : (b + 1) * 128]
            g = rows_ref[:, HALF + b * 128 : HALF + (b + 1) * 128]
            lse, delta = stats[b : b + 1], stats[PAIRS + b : PAIRS + b + 1]
            probs = jnp.exp(jnp.where(mask, own_scores(k2, q) * INV_SQRT - lse, masked_score))
            dscore = (probs * (own_scores(v2, g) - delta)).astype(BF16)
            dsv = dsv + own_product(probs.astype(BF16), g, nn)
            dsk = dsk + own_product(dscore, q, nn)
            dq = dq_rows_ref[:, b * 128 : (b + 1) * 128].astype(F32)
            dq = dq + own_product(dscore, k2, tn) * INV_SQRT
            for at, part in zip((b, b + PAIRS), unfold(dq)):
                dq_ref[0, :, at * 128 : (at + 1) * 128] = part.astype(BF16)
        for at, k_part, v_part in zip((h, h + 2), unfold(dsk * INV_SQRT), unfold(dsv)):
            dsk_ref[0, :, at * 128 : (at + 1) * 128] = k_part.astype(BF16)
            dsv_ref[0, :, at * 128 : (at + 1) * 128] = v_part.astype(BF16)
    dq = dq_ref[0]
    keep = lax.broadcasted_iota(jnp.int32, (TOKENS, PADDED_RANK), 1) < rank
    lifted = jnp.where(keep, scale * nt(dq, wu_ref[...]), 0.0).astype(BF16)
    low = low_ref[...]
    for c in range(GRAD_BLOCKS):
        if c < DOWN_BLOCKS:
            part = tn(lifted, x_ref[:, c * 128 : (c + 1) * 128])
        else:
            at = (c - DOWN_BLOCKS) * 128
            part = scale * tn(low, dq[:, at : at + 128])
        grads_ref[c * PADDED_RANK : (c + 1) * PADDED_RANK, :] = part.astype(BF16)


def spread_kernel(grads_ref, down_ref, up_ref):
    for c in range(GRAD_BLOCKS):
        part = grads_ref[c * PADDED_RANK : (c + 1) * PADDED_RANK, :].astype(F32)
        if c < DOWN_BLOCKS:
            down_ref[:, c * 128 : (c + 1) * 128] = part
        else:
            at = (c - DOWN_BLOCKS) * 128
            up_ref[:, at : at + 128] = part


VMEM = pl.BlockSpec(memory_space=pltpu.VMEM)
SMEM = pl.BlockSpec(memory_space=pltpu.SMEM)
HBM = pl.BlockSpec(memory_space=pltpu.HBM)


def call(kernel, in_specs, outs, scratch=(), out_specs=None, vmem_mib=40):
    return pl.pallas_call(
        kernel,
        out_shape=[jax.ShapeDtypeStruct(shape, dtype) for shape, dtype in outs],
        in_specs=in_specs,
        out_specs=out_specs or [VMEM] * len(outs),
        scratch_shapes=list(scratch),
        compiler_params=pltpu.CompilerParams(vmem_limit_bytes=vmem_mib * 1024 * 1024),
    )


def replicate(part, count):
    return jnp.broadcast_to(part[None], (count,) + part.shape)


def sum_all(grads):
    rows = GRAD_BLOCKS * PADDED_RANK
    parts = lax.all_to_all(grads.reshape(16, rows // 16, 128), "comp", 0, 0, tiled=True)
    total = jnp.sum(parts.astype(F32), axis=0)
    flips = (
        lambda i: i ^ 4,
        lambda i: (3 - i // 4) * 4 + i % 4,
        lambda i: i ^ 1,
        lambda i: i // 4 * 4 + 3 - i % 4,
    )
    for flip in flips:
        total = total + lax.ppermute(total, "prompt", [(i, flip(i)) for i in range(16)])
    whole = lax.all_to_all(replicate(total.astype(BF16), 16), "comp", 0, 0, tiled=True)
    return whole.reshape(rows, 128)


def per_device(
    normed_hidden_input,
    frozen_query_base,
    attention_output_grad,
    completion_keys,
    completion_values,
    owner_prompt_keys,
    owner_prompt_values,
    adapter_down_weight,
    adapter_up_weight,
    adapter_rank,
    route,
    lengths,
):
    hidden = normed_hidden_input[0]
    keys, values = completion_keys[0], completion_values[0]
    arrays = (
        hidden, frozen_query_base[0], attention_output_grad[0], keys, values,
        adapter_down_weight.T, adapter_up_weight,
    )
    low, send = call(
        prepare_kernel,
        [SMEM] * 3 + [HBM] * 7,
        [((TOKENS, PADDED_RANK), BF16), ((SLOTS, 16, SEND_WIDTH), BF16)],
        [pltpu.VMEM(a.shape, BF16) for a in arrays]
        + [pltpu.VMEM((ROWS, SEND_WIDTH), BF16), pltpu.SemaphoreType.DMA((7 + SLOTS,))],
        [VMEM, HBM],
        60,
    )(adapter_rank, route, lengths, *arrays)
    arrived = lax.all_to_all(send, "prompt", 0, 0, tiled=True)
    back, dk, dv = call(
        owner_kernel,
        [VMEM] * 3,
        [((ROWS, BACK_WIDTH), BF16)] + [((PLEN, KEY_VALUE_HEADS * HEAD_SIZE), BF16)] * 2,
    )(arrived.reshape(ROWS, SEND_WIDTH), owner_prompt_keys[0], owner_prompt_values[0])
    back = lax.all_to_all(back.reshape(SLOTS, 16, BACK_WIDTH), "prompt", 0, 0, tiled=True)
    dq, dsk, dsv, grads = call(
        finish_kernel,
        [SMEM] * 2 + [VMEM] * 7,
        [
            ((1, TOKENS, QUERY_WIDTH), BF16),
            ((1, TOKENS, KEY_VALUE_HEADS * HEAD_SIZE), BF16),
            ((1, TOKENS, KEY_VALUE_HEADS * HEAD_SIZE), BF16),
            ((GRAD_BLOCKS * PADDED_RANK, 128), BF16),
        ],
        [pltpu.VMEM((ROWS, SEND_WIDTH), BF16), pltpu.VMEM((ROWS, BACK_WIDTH), BF16)],
    )(adapter_rank, route, hidden, keys, values, adapter_up_weight, low, send, back)
    down, up = call(
        spread_kernel,
        [VMEM],
        [((PADDED_RANK, MODEL_WIDTH), F32), ((PADDED_RANK, QUERY_WIDTH), F32)],
    )(sum_all(grads))
    return dq, dsk, dsv, dk[None], dv[None], down.T, up


def solution(mesh):
    split = P("comp", "prompt", None)
    return jax.shard_map(
        per_device,
        mesh=mesh,
        in_specs=(split,) * 7 + (P(),) * 3 + (split,) * 2,
        out_specs=(split,) * 5 + (P(),) * 2,
        check_vma=False,
    )
```

```python
import functools
import math

import jax
import jax.numpy as jnp
from jax import lax
from jax.experimental import pallas as pl
from jax.experimental.pallas import tpu as pltpu
from jax.sharding import PartitionSpec as P

KEY_VALUE_HEADS = 4
GROUP = 5
HEAD_SIZE = 128
PLEN = 128
CL = 8
SLOTS = 16
TOKENS = SLOTS * CL
QUERY_HEADS = KEY_VALUE_HEADS * GROUP
PAIRS = QUERY_HEADS // 2
HALF = PAIRS * HEAD_SIZE
KV_HALF = KEY_VALUE_HEADS * HEAD_SIZE // 2
ROWS = 2 * TOKENS
MODEL_WIDTH = 5120
PADDED_RANK = 64
QUERY_WIDTH = QUERY_HEADS * HEAD_SIZE
SEND_WIDTH = 2 * HALF + 128
BACK_WIDTH = HALF + 128
DOWN_BLOCKS = MODEL_WIDTH // 128
GRAD_BLOCKS = (MODEL_WIDTH + QUERY_WIDTH) // 128
CORE_BLOCKS = 32
CORE_ROWS = CORE_BLOCKS * PADDED_RANK

INV_SQRT = 1.0 / math.sqrt(HEAD_SIZE)
adapter_strength = 32.0
masked_score = -1e30

BF16 = jnp.bfloat16
F32 = jnp.float32


def dot(a, b, dims):
    return lax.dot_general(a, b, (dims, ((), ())), preferred_element_type=F32)


def nt(a, b):
    return dot(a, b, ((1,), (1,)))


def nn(a, b):
    return dot(a, b, ((1,), (0,)))


def tn(a, b):
    return dot(a, b, ((0,), (0,)))


def fold(wide):
    width = wide.shape[1] // 2
    left = wide[:, :width].reshape(SLOTS, 1, CL, width)
    right = wide[:, width:].reshape(SLOTS, 1, CL, width)
    return jnp.concatenate([left, right], axis=1).reshape(ROWS, width)


def unfold(rows):
    split = rows.reshape(SLOTS, 2, CL, rows.shape[1])
    return split[:, 0].reshape(TOKENS, -1), split[:, 1].reshape(TOKENS, -1)


def own_mask():
    key = lax.broadcasted_iota(jnp.int32, (TOKENS, ROWS), 0)
    row = lax.broadcasted_iota(jnp.int32, (TOKENS, ROWS), 1) % TOKENS
    return (key // CL == row // CL) & (key <= row)


def own_scores(keys, rows):
    return jnp.concatenate(
        [nt(keys[at : at + TOKENS], rows[at : at + TOKENS]) for at in (0, TOKENS)], axis=1
    )


def own_product(scores, rows, product):
    return jnp.concatenate(
        [product(scores[:, at : at + TOKENS], rows[at : at + TOKENS]) for at in (0, TOKENS)], axis=0
    )


def pack_stats(rows):
    value = jnp.concatenate(rows, axis=0)
    first = value.astype(BF16).astype(F32)
    rest = value - first
    second = rest.astype(BF16).astype(F32)
    third = rest - second
    pad = jnp.zeros((128 - 3 * len(rows), ROWS), F32)
    return jnp.concatenate([first, second, third, pad], axis=0).T.astype(BF16)


def unpack_stats(columns, count):
    parts = columns.astype(F32).T
    return parts[:count] + (parts[count : 2 * count] + parts[2 * count : 3 * count])


def prepare_kernel(
    rank_ref, route_ref, length_ref, x_hbm, base_hbm, g_hbm, sk_hbm, sv_hbm, wd_hbm, wu_hbm,
    low_ref, send_hbm,
    x_ref, base_ref, g_ref, sk_ref, sv_ref, wd_ref, wu_ref, rows_ref, sems,
):
    sources = (g_hbm, sv_hbm, sk_hbm, wd_hbm, x_hbm, wu_hbm, base_hbm)
    targets = (g_ref, sv_ref, sk_ref, wd_ref, x_ref, wu_ref, base_ref)
    copies = [
        pltpu.make_async_copy(source, target, sems.at[i])
        for i, (source, target) in enumerate(zip(sources, targets))
    ]
    for copy in copies:
        copy.start()
    rank = rank_ref[0]
    scale = adapter_strength / rank.astype(F32)
    position = lax.broadcasted_iota(jnp.int32, (CL, 128), 0)
    live = jnp.concatenate(
        [jnp.where(position < length_ref[0, 0, s], 1.0, 0.0) for s in range(SLOTS)], axis=0
    )
    mask = own_mask()
    copies[0].wait()
    for n in range(PAIRS):
        left, right = (g_ref[:, m * 128 : (m + 1) * 128].astype(F32) * live for m in (n, n + PAIRS))
        rows_ref[:, HALF + n * 128 : HALF + (n + 1) * 128] = fold(
            jnp.concatenate([left, right], axis=1)
        ).astype(BF16)
    copies[1].wait()
    values = fold(sv_ref[...].astype(F32)).astype(BF16)
    copies[2].wait()
    keys = fold(sk_ref[...].astype(F32)).astype(BF16)
    copies[3].wait()
    copies[4].wait()
    keep = lax.broadcasted_iota(jnp.int32, (TOKENS, PADDED_RANK), 1) < rank
    low = jnp.where(keep, nt(x_ref[...], wd_ref[...]), 0.0).astype(BF16)
    low_ref[...] = low
    copies[5].wait()
    copies[6].wait()
    lses, deltas = [], []
    for b in range(PAIRS):
        h = b // GROUP
        left, right = (
            base_ref[:, m * 128 : (m + 1) * 128].astype(F32)
            + scale * nn(low, wu_ref[:, m * 128 : (m + 1) * 128])
            for m in (b, b + PAIRS)
        )
        q = fold(jnp.concatenate([left, right], axis=1)).astype(BF16)
        rows_ref[:, b * 128 : (b + 1) * 128] = q
        g = rows_ref[:, HALF + b * 128 : HALF + (b + 1) * 128]
        scores = jnp.where(
            mask, own_scores(keys[:, h * 128 : (h + 1) * 128], q) * INV_SQRT, masked_score
        )
        top = jnp.max(scores, axis=0, keepdims=True)
        weight = jnp.exp(scores - top)
        total = jnp.sum(weight, axis=0, keepdims=True)
        dprob = own_scores(values[:, h * 128 : (h + 1) * 128], g)
        lses.append(top + jnp.log(total))
        deltas.append(jnp.sum(weight * dprob, axis=0, keepdims=True) / total)
    rows_ref[:, 2 * HALF :] = pack_stats(lses + deltas)
    sends = [
        pltpu.make_async_copy(
            rows_ref.at[pl.ds(s * 16, 16)], send_hbm.at[route_ref[0, 0, s]], sems.at[7 + s]
        )
        for s in range(SLOTS)
    ]
    for copy in sends:
        copy.start()
    for copy in sends:
        copy.wait()


def owner_kernel(rows_ref, k_ref, v_ref, back_ref, dk_ref, dv_ref):
    lower = (lax.broadcasted_iota(jnp.int32, (ROWS, HEAD_SIZE), 0) // CL % 2 == 0).astype(F32)
    lower, upper = lower.astype(BF16), (1.0 - lower).astype(BF16)
    stats = unpack_stats(rows_ref[:, 2 * HALF :], 2 * PAIRS)

    def beside(ref, h):
        return jnp.concatenate([ref[:, m * 128 : (m + 1) * 128] for m in (h, h + 2)], axis=1)

    def apart(rows):
        return jnp.concatenate([rows * lower, rows * upper], axis=1)

    lses, deltas = [], []
    for h in range(2):
        keys, values = beside(k_ref, h), beside(v_ref, h)
        dk = jnp.zeros((PLEN, 2 * HEAD_SIZE), F32)
        dv = jnp.zeros((PLEN, 2 * HEAD_SIZE), F32)
        for b in range(h * GROUP, (h + 1) * GROUP):
            q = apart(rows_ref[:, b * 128 : (b + 1) * 128])
            g = apart(rows_ref[:, HALF + b * 128 : HALF + (b + 1) * 128])
            own_lse, own_delta = stats[b : b + 1], stats[PAIRS + b : PAIRS + b + 1]
            scores = nt(keys, q) * INV_SQRT
            dprob = nt(values, g)
            top = jnp.max(scores, axis=0, keepdims=True)
            weight = jnp.exp(scores - top)
            prompt_lse = top + jnp.log(jnp.sum(weight, axis=0, keepdims=True))
            high = jnp.maximum(prompt_lse, own_lse)
            lse = high + jnp.log(jnp.exp(prompt_lse - high) + jnp.exp(own_lse - high))
            probs = weight * jnp.exp(top - lse)
            probs_b = probs.astype(BF16)
            delta = jnp.sum(probs_b.astype(F32) * dprob, axis=0, keepdims=True) + own_delta * jnp.exp(
                own_lse - lse
            )
            dscore = (probs * (dprob - delta)).astype(BF16)
            dv = dv + nn(probs_b, g)
            dk = dk + nn(dscore, q)
            dq = (tn(dscore, keys) * INV_SQRT).reshape(SLOTS, 2, CL, 2 * HEAD_SIZE)
            dq = jnp.concatenate([dq[:, :1, :, :HEAD_SIZE], dq[:, 1:, :, HEAD_SIZE:]], axis=1)
            back_ref[:, b * 128 : (b + 1) * 128] = dq.reshape(ROWS, HEAD_SIZE).astype(BF16)
            lses.append(lse)
            deltas.append(delta)
        for at, m in ((0, h), (HEAD_SIZE, h + 2)):
            dk_ref[:, m * 128 : (m + 1) * 128] = (dk[:, at : at + HEAD_SIZE] * INV_SQRT).astype(BF16)
            dv_ref[:, m * 128 : (m + 1) * 128] = dv[:, at : at + HEAD_SIZE].astype(BF16)
    back_ref[:, HALF:] = pack_stats(lses + deltas)


def finish_kernel(
    rank_ref, route_ref, core_ref, x_ref, sk_ref, sv_ref, wu_ref, low_ref, send_ref, back_ref,
    dq_ref, dsk_ref, dsv_ref, mine_ref, other_ref, rows_ref, dq_rows_ref,
):
    rank = rank_ref[0]
    scale = adapter_strength / rank.astype(F32)
    for s in range(SLOTS):
        owner = route_ref[0, 0, s]
        rows_ref[s * 16 : (s + 1) * 16, :] = send_ref[owner]
        dq_rows_ref[s * 16 : (s + 1) * 16, :] = back_ref[owner]
    keys = fold(sk_ref[...].astype(F32)).astype(BF16)
    values = fold(sv_ref[...].astype(F32)).astype(BF16)
    stats = unpack_stats(dq_rows_ref[:, HALF:], 2 * PAIRS)
    mask = own_mask()
    for h in range(2):
        k2, v2 = keys[:, h * 128 : (h + 1) * 128], values[:, h * 128 : (h + 1) * 128]
        dsk = jnp.zeros((ROWS, HEAD_SIZE), F32)
        dsv = jnp.zeros((ROWS, HEAD_SIZE), F32)
        for b in range(h * GROUP, (h + 1) * GROUP):
            q = rows_ref[:, b * 128 : (b + 1) * 128]
            g = rows_ref[:, HALF + b * 128 : HALF + (b + 1) * 128]
            lse, delta = stats[b : b + 1], stats[PAIRS + b : PAIRS + b + 1]
            probs = jnp.exp(jnp.where(mask, own_scores(k2, q) * INV_SQRT - lse, masked_score))
            dscore = (probs * (own_scores(v2, g) - delta)).astype(BF16)
            dsv = dsv + own_product(probs.astype(BF16), g, nn)
            dsk = dsk + own_product(dscore, q, nn)
            dq = dq_rows_ref[:, b * 128 : (b + 1) * 128].astype(F32)
            dq = dq + own_product(dscore, k2, tn) * INV_SQRT
            for at, part in zip((b, b + PAIRS), unfold(dq)):
                dq_ref[0, :, at * 128 : (at + 1) * 128] = part.astype(BF16)
        for at, k_part, v_part in zip((h, h + 2), unfold(dsk * INV_SQRT), unfold(dsv)):
            dsk_ref[0, :, at * 128 : (at + 1) * 128] = k_part.astype(BF16)
            dsv_ref[0, :, at * 128 : (at + 1) * 128] = v_part.astype(BF16)
    dq = dq_ref[0]
    keep = lax.broadcasted_iota(jnp.int32, (TOKENS, PADDED_RANK), 1) < rank
    lifted = jnp.where(keep, scale * nt(dq, wu_ref[...]), 0.0).astype(BF16)
    low = low_ref[...]

    def block(c):
        if c < DOWN_BLOCKS:
            return tn(lifted, x_ref[:, c * 128 : (c + 1) * 128])
        if c < GRAD_BLOCKS:
            at = (c - DOWN_BLOCKS) * 128
            return scale * tn(low, dq[:, at : at + 128])
        return jnp.zeros((PADDED_RANK, 128), F32)

    first = core_ref[0] == 0
    for c in range(CORE_BLOCKS):
        lower, upper = block(c), block(c + CORE_BLOCKS)
        at = slice(c * PADDED_RANK, (c + 1) * PADDED_RANK)
        mine_ref[at, :] = jnp.where(first, lower, upper).astype(BF16)
        other_ref[at, :] = jnp.where(first, upper, lower).astype(BF16)


def spread_kernel(core_ref, mine_ref, other_ref, down_ref, up_ref):
    first = core_ref[0] == 0
    for c in range(GRAD_BLOCKS):
        at = c % CORE_BLOCKS * PADDED_RANK
        mine = mine_ref[at : at + PADDED_RANK, :].astype(F32)
        other = other_ref[at : at + PADDED_RANK, :].astype(F32)
        part = jnp.where(first, mine, other) if c < CORE_BLOCKS else jnp.where(first, other, mine)
        if c < DOWN_BLOCKS:
            down_ref[:, c * 128 : (c + 1) * 128] = part
        else:
            at = (c - DOWN_BLOCKS) * 128
            up_ref[:, at : at + 128] = part


VMEM = pl.BlockSpec(memory_space=pltpu.VMEM)
SMEM = pl.BlockSpec(memory_space=pltpu.SMEM)
HBM = pl.BlockSpec(memory_space=pltpu.HBM)


def call(kernel, in_specs, outs, scratch=(), out_specs=None, vmem_mib=40):
    return pl.pallas_call(
        kernel,
        out_shape=[jax.ShapeDtypeStruct(shape, dtype) for shape, dtype in outs],
        in_specs=in_specs,
        out_specs=out_specs or [VMEM] * len(outs),
        scratch_shapes=list(scratch),
        compiler_params=pltpu.CompilerParams(vmem_limit_bytes=vmem_mib * 1024 * 1024),
    )


def by_core(part):
    return lax.ppermute(part, "comp", [(i, i ^ 1) for i in range(16)])


def layer_groups():
    return [
        [(x * 4 + z_hi) * 16 + zy * 2 + core for x in range(4) for zy in range(8)]
        for z_hi in range(4)
        for core in range(2)
    ]


def sum_all(mine, other):
    rows = CORE_ROWS // 32
    swap = functools.partial(
        lax.all_to_all, axis_name=("prompt", "comp"), split_axis=0, concat_axis=0,
        axis_index_groups=layer_groups(), tiled=True,
    )
    pair = (mine.astype(F32) + by_core(other).astype(F32)).astype(BF16)
    total = jnp.sum(swap(pair.reshape(32, rows, 128)).astype(F32), axis=0)
    for flip in (lambda i: i ^ 1, lambda i: i // 4 * 4 + 3 - i % 4):
        total = total + lax.ppermute(total, "prompt", [(i, flip(i)) for i in range(16)])
    total = total.astype(BF16)
    half = swap(jnp.broadcast_to(total[None], (32, rows, 128))).reshape(CORE_ROWS, 128)
    return half, by_core(half)


def per_device(
    normed_hidden_input,
    frozen_query_base,
    attention_output_grad,
    completion_keys,
    completion_values,
    owner_prompt_keys,
    owner_prompt_values,
    adapter_down_weight,
    adapter_up_weight,
    adapter_rank,
    route,
    lengths,
):
    hidden = normed_hidden_input[0]
    keys, values = completion_keys[0], completion_values[0]
    arrays = (
        hidden, frozen_query_base[0], attention_output_grad[0], keys, values,
        adapter_down_weight.T, adapter_up_weight,
    )
    low, send = call(
        prepare_kernel,
        [SMEM] * 3 + [HBM] * 7,
        [((TOKENS, PADDED_RANK), BF16), ((SLOTS, 16, SEND_WIDTH), BF16)],
        [pltpu.VMEM(a.shape, BF16) for a in arrays]
        + [pltpu.VMEM((ROWS, SEND_WIDTH), BF16), pltpu.SemaphoreType.DMA((7 + SLOTS,))],
        [VMEM, HBM],
        60,
    )(adapter_rank, route, lengths, *arrays)
    arrived = lax.all_to_all(send, "prompt", 0, 0, tiled=True)
    back, dk, dv = call(
        owner_kernel,
        [VMEM] * 3,
        [((ROWS, BACK_WIDTH), BF16)] + [((PLEN, KEY_VALUE_HEADS * HEAD_SIZE), BF16)] * 2,
    )(arrived.reshape(ROWS, SEND_WIDTH), owner_prompt_keys[0], owner_prompt_values[0])
    back = lax.all_to_all(back.reshape(SLOTS, 16, BACK_WIDTH), "prompt", 0, 0, tiled=True)
    core = (lax.axis_index("comp") % 2).astype(jnp.int32)[None]
    dq, dsk, dsv, mine, other = call(
        finish_kernel,
        [SMEM] * 3 + [VMEM] * 7,
        [
            ((1, TOKENS, QUERY_WIDTH), BF16),
            ((1, TOKENS, KEY_VALUE_HEADS * HEAD_SIZE), BF16),
            ((1, TOKENS, KEY_VALUE_HEADS * HEAD_SIZE), BF16),
            ((CORE_ROWS, 128), BF16),
            ((CORE_ROWS, 128), BF16),
        ],
        [pltpu.VMEM((ROWS, SEND_WIDTH), BF16), pltpu.VMEM((ROWS, BACK_WIDTH), BF16)],
    )(adapter_rank, route, core, hidden, keys, values, adapter_up_weight, low, send, back)
    down, up = call(
        spread_kernel,
        [SMEM] + [VMEM] * 2,
        [((PADDED_RANK, MODEL_WIDTH), F32), ((PADDED_RANK, QUERY_WIDTH), F32)],
    )(core, *sum_all(mine, other))
    return dq, dsk, dsv, dk[None], dv[None], down.T, up


def solution(mesh):
    split = P("comp", "prompt", None)
    return jax.shard_map(
        per_device,
        mesh=mesh,
        in_specs=(split,) * 7 + (P(),) * 3 + (split,) * 2,
        out_specs=(split,) * 5 + (P(),) * 2,
        check_vma=False,
    )
```

```python
import functools
import math

import jax
import jax.numpy as jnp
from jax import lax
from jax.experimental import pallas as pl
from jax.experimental.pallas import tpu as pltpu
from jax.sharding import PartitionSpec as P

KEY_VALUE_HEADS = 4
GROUP = 5
HEAD_SIZE = 128
PLEN = 128
CL = 8
SLOTS = 16
TOKENS = SLOTS * CL
QUERY_HEADS = KEY_VALUE_HEADS * GROUP
PAIRS = QUERY_HEADS // 2
HALF = PAIRS * HEAD_SIZE
KV_HALF = KEY_VALUE_HEADS * HEAD_SIZE // 2
ROWS = 2 * TOKENS
MODEL_WIDTH = 5120
PADDED_RANK = 64
QUERY_WIDTH = QUERY_HEADS * HEAD_SIZE
SEND_WIDTH = 2 * HALF + 128
X_PARTS = 4
X_PART = MODEL_WIDTH // X_PARTS
BACK_WIDTH = HALF + 128
DOWN_BLOCKS = MODEL_WIDTH // 128
GRAD_BLOCKS = (MODEL_WIDTH + QUERY_WIDTH) // 128
CORE_BLOCKS = 32
CORE_ROWS = CORE_BLOCKS * PADDED_RANK

INV_SQRT = 1.0 / math.sqrt(HEAD_SIZE)
adapter_strength = 32.0
masked_score = -1e30

BF16 = jnp.bfloat16
F32 = jnp.float32


def dot(a, b, dims):
    return lax.dot_general(a, b, (dims, ((), ())), preferred_element_type=F32)


def nt(a, b):
    return dot(a, b, ((1,), (1,)))


def nn(a, b):
    return dot(a, b, ((1,), (0,)))


def tn(a, b):
    return dot(a, b, ((0,), (0,)))


def fold(wide):
    width = wide.shape[1] // 2
    left = wide[:, :width].reshape(SLOTS, 1, CL, width)
    right = wide[:, width:].reshape(SLOTS, 1, CL, width)
    return jnp.concatenate([left, right], axis=1).reshape(ROWS, width)


def unfold(rows):
    split = rows.reshape(SLOTS, 2, CL, rows.shape[1])
    return split[:, 0].reshape(TOKENS, -1), split[:, 1].reshape(TOKENS, -1)


def own_mask():
    key = lax.broadcasted_iota(jnp.int32, (TOKENS, ROWS), 0)
    row = lax.broadcasted_iota(jnp.int32, (TOKENS, ROWS), 1) % TOKENS
    return (key // CL == row // CL) & (key <= row)


def own_scores(keys, rows):
    return jnp.concatenate(
        [nt(keys[at : at + TOKENS], rows[at : at + TOKENS]) for at in (0, TOKENS)], axis=1
    )


def own_product(scores, rows, product):
    return jnp.concatenate(
        [product(scores[:, at : at + TOKENS], rows[at : at + TOKENS]) for at in (0, TOKENS)], axis=0
    )


def pack_stats(rows):
    value = jnp.concatenate(rows, axis=0)
    first = value.astype(BF16).astype(F32)
    rest = value - first
    second = rest.astype(BF16).astype(F32)
    third = rest - second
    pad = jnp.zeros((128 - 3 * len(rows), ROWS), F32)
    return jnp.concatenate([first, second, third, pad], axis=0).T


def unpack_stats(columns, count):
    parts = columns.astype(F32).T
    return parts[:count] + (parts[count : 2 * count] + parts[2 * count : 3 * count])


def prepare_kernel(
    rank_hbm, route_hbm, length_hbm, x_hbm, base_hbm, g_hbm, sk_hbm, sv_hbm, wd_hbm, wu_hbm,
    send_hbm,
    rank_ref, route_ref, length_ref, x_ref, base_ref, g_ref, sk_ref, sv_ref, wd_ref, wu_ref, rows_ref, sems,
):
    columns = [slice(i * X_PART, (i + 1) * X_PART) for i in range(X_PARTS)]
    pairs = [(rank_hbm, rank_ref), (length_hbm, length_ref), (route_hbm, route_ref)]
    pairs += [(wd_hbm, wd_ref)] + [(x_hbm.at[:, c], x_ref.at[:, c]) for c in columns]
    pairs += [
        (g_hbm, g_ref), (sv_hbm, sv_ref), (sk_hbm, sk_ref), (wu_hbm, wu_ref), (base_hbm, base_ref)
    ]
    loads = [
        pltpu.make_async_copy(source, target, sems.at[i])
        for i, (source, target) in enumerate(pairs)
    ]
    for copy in loads:
        copy.start()

    def sends(start, width, sem):
        return [
            pltpu.make_async_copy(
                rows_ref.at[pl.ds(s * 16, 16), pl.ds(start, width)],
                send_hbm.at[route_ref[0, 0, s], :, pl.ds(start, width)],
                sems.at[sem + s],
            )
            for s in range(SLOTS)
        ]

    for copy in loads[:3]:
        copy.wait()
    rank = rank_ref[0]
    scale = adapter_strength / rank.astype(F32)
    position = lax.broadcasted_iota(jnp.int32, (CL, 128), 0)
    live = jnp.concatenate(
        [jnp.where(position < length_ref[0, 0, s], 1.0, 0.0) for s in range(SLOTS)], axis=0
    )
    mask = own_mask()
    loads[3].wait()
    low = jnp.zeros((TOKENS, PADDED_RANK), F32)
    for i, c in enumerate(columns):
        loads[4 + i].wait()
        low = low + nt(x_ref[:, c], wd_ref[:, c])
    rest = 4 + X_PARTS
    loads[rest].wait()
    for n in range(PAIRS):
        left, right = (g_ref[:, m * 128 : (m + 1) * 128].astype(F32) * live for m in (n, n + PAIRS))
        rows_ref[:, n * 128 : (n + 1) * 128] = fold(
            jnp.concatenate([left, right], axis=1)
        ).astype(BF16)
    early = sends(0, HALF, rest + 5)
    for copy in early:
        copy.start()
    for copy in loads[rest + 1 :]:
        copy.wait()
    values = fold(sv_ref[...].astype(F32)).astype(BF16)
    keys = fold(sk_ref[...].astype(F32)).astype(BF16)
    keep = lax.broadcasted_iota(jnp.int32, (TOKENS, PADDED_RANK), 1) < rank
    low = jnp.where(keep, low, 0.0).astype(BF16)
    query = base_ref[...].astype(F32) + scale * nn(low, wu_ref[...])
    rows_ref[:, HALF : 2 * HALF] = fold(query).astype(BF16)

    def products(b):
        h = b // GROUP
        g = rows_ref[:, b * 128 : (b + 1) * 128]
        q = rows_ref[:, HALF + b * 128 : HALF + (b + 1) * 128]
        return (
            own_scores(keys[:, h * 128 : (h + 1) * 128], q),
            own_scores(values[:, h * 128 : (h + 1) * 128], g),
        )

    lses, deltas = [], []
    ready = products(0)
    for b in range(PAIRS):
        scores, dprob = ready
        if b + 1 < PAIRS:
            ready = products(b + 1)
        scores = jnp.where(mask, scores * INV_SQRT, masked_score)
        top = jnp.max(scores, axis=0, keepdims=True)
        weight = jnp.exp(scores - top)
        total = jnp.sum(weight, axis=0, keepdims=True)
        lses.append(top + jnp.log(total))
        deltas.append(jnp.sum(weight * dprob, axis=0, keepdims=True) / total)
    none = jnp.zeros((TOKENS, PADDED_RANK), F32)
    low_rows = fold(jnp.concatenate([none, low.astype(F32), none, none], axis=1))
    rows_ref[:, 2 * HALF :] = (pack_stats(lses + deltas) + low_rows).astype(BF16)
    late = sends(HALF, SEND_WIDTH - HALF, rest + 5 + SLOTS)
    for copy in late:
        copy.start()
    for copy in early + late:
        copy.wait()


def owner_kernel(rows_ref, k_ref, v_ref, back_ref, dk_ref, dv_ref):
    lower = (lax.broadcasted_iota(jnp.int32, (ROWS, HEAD_SIZE), 0) // CL % 2 == 0).astype(F32)
    lower, upper = lower.astype(BF16), (1.0 - lower).astype(BF16)
    stats = unpack_stats(rows_ref[:, 2 * HALF :], 2 * PAIRS)

    def beside(ref, h):
        return jnp.concatenate([ref[:, m * 128 : (m + 1) * 128] for m in (h, h + 2)], axis=1)

    def apart(rows):
        return jnp.concatenate([rows * lower, rows * upper], axis=1)

    sides = [(beside(k_ref, h), beside(v_ref, h)) for h in range(2)]

    def products(b):
        g = apart(rows_ref[:, b * 128 : (b + 1) * 128])
        q = apart(rows_ref[:, HALF + b * 128 : HALF + (b + 1) * 128])
        keys, values = sides[b // GROUP]
        return q, g, nt(keys, q), nt(values, g)

    lses, deltas = [], []
    ready = products(0)
    for h in range(2):
        keys = sides[h][0]
        dk = jnp.zeros((PLEN, 2 * HEAD_SIZE), F32)
        dv = jnp.zeros((PLEN, 2 * HEAD_SIZE), F32)
        for b in range(h * GROUP, (h + 1) * GROUP):
            q, g, scores, dprob = ready
            if b + 1 < PAIRS:
                ready = products(b + 1)
            own_lse, own_delta = stats[b : b + 1], stats[PAIRS + b : PAIRS + b + 1]
            scores = scores * INV_SQRT
            top = jnp.max(scores, axis=0, keepdims=True)
            weight = jnp.exp(scores - top)
            prompt_lse = top + jnp.log(jnp.sum(weight, axis=0, keepdims=True))
            high = jnp.maximum(prompt_lse, own_lse)
            lse = high + jnp.log(jnp.exp(prompt_lse - high) + jnp.exp(own_lse - high))
            probs = weight * jnp.exp(top - lse)
            probs_b = probs.astype(BF16)
            delta = jnp.sum(probs_b.astype(F32) * dprob, axis=0, keepdims=True) + own_delta * jnp.exp(
                own_lse - lse
            )
            dscore = (probs * (dprob - delta)).astype(BF16)
            dv = dv + nn(probs_b, g)
            dk = dk + nn(dscore, q)
            dq = (tn(dscore, keys) * INV_SQRT).reshape(SLOTS, 2, CL, 2 * HEAD_SIZE)
            dq = jnp.concatenate([dq[:, :1, :, :HEAD_SIZE], dq[:, 1:, :, HEAD_SIZE:]], axis=1)
            back_ref[:, b * 128 : (b + 1) * 128] = dq.reshape(ROWS, HEAD_SIZE).astype(BF16)
            lses.append(lse)
            deltas.append(delta)
        for at, m in ((0, h), (HEAD_SIZE, h + 2)):
            dk_ref[:, m * 128 : (m + 1) * 128] = (dk[:, at : at + HEAD_SIZE] * INV_SQRT).astype(BF16)
            dv_ref[:, m * 128 : (m + 1) * 128] = dv[:, at : at + HEAD_SIZE].astype(BF16)
    back_ref[:, HALF:] = pack_stats(lses + deltas).astype(BF16)


def finish_kernel(
    route_hbm, rank_hbm, core_hbm, sk_hbm, sv_hbm, wu_hbm, x_hbm, send_hbm, back_hbm,
    dq_hbm, dsk_hbm, dsv_hbm, mine_ref, other_ref,
    route_ref, rank_ref, core_ref, sk_ref, sv_ref, wu_ref, x_ref, rows_ref, dq_rows_ref,
    dq_ref, dsk_ref, dsv_ref, sems,
):
    pairs = [
        (route_hbm, route_ref), (rank_hbm, rank_ref), (core_hbm, core_ref), (sk_hbm, sk_ref),
        (sv_hbm, sv_ref), (wu_hbm, wu_ref), (x_hbm, x_ref),
    ]
    loads = [
        pltpu.make_async_copy(source, target, sems.at[i])
        for i, (source, target) in enumerate(pairs)
    ]
    for copy in loads[:6]:
        copy.start()
    loads[0].wait()
    blocks = []
    for s in range(SLOTS):
        owner, at = route_ref[0, 0, s], pl.ds(s * 16, 16)
        blocks += [
            pltpu.make_async_copy(send_hbm.at[owner], rows_ref.at[at], sems.at[7 + 2 * s]),
            pltpu.make_async_copy(back_hbm.at[owner], dq_rows_ref.at[at], sems.at[8 + 2 * s]),
        ]
    for copy in blocks:
        copy.start()
    loads[6].start()
    for copy in loads[1:6]:
        copy.wait()
    rank = rank_ref[0]
    scale = adapter_strength / rank.astype(F32)
    mask = own_mask()
    keys = fold(sk_ref[...].astype(F32)).astype(BF16)
    values = fold(sv_ref[...].astype(F32)).astype(BF16)
    for copy in blocks:
        copy.wait()
    stats = unpack_stats(dq_rows_ref[:, HALF:], 2 * PAIRS)

    def products(b):
        h = b // GROUP
        g = rows_ref[:, b * 128 : (b + 1) * 128]
        q = rows_ref[:, HALF + b * 128 : HALF + (b + 1) * 128]
        return (
            q, g,
            own_scores(keys[:, h * 128 : (h + 1) * 128], q),
            own_scores(values[:, h * 128 : (h + 1) * 128], g),
        )

    ready = products(0)
    for h in range(2):
        k2 = keys[:, h * 128 : (h + 1) * 128]
        dsk = jnp.zeros((ROWS, HEAD_SIZE), F32)
        dsv = jnp.zeros((ROWS, HEAD_SIZE), F32)
        for b in range(h * GROUP, (h + 1) * GROUP):
            q, g, scores, dprob = ready
            if b + 1 < PAIRS:
                ready = products(b + 1)
            lse, delta = stats[b : b + 1], stats[PAIRS + b : PAIRS + b + 1]
            probs = jnp.exp(jnp.where(mask, scores * INV_SQRT - lse, masked_score))
            dscore = (probs * (dprob - delta)).astype(BF16)
            dsv = dsv + own_product(probs.astype(BF16), g, nn)
            dsk = dsk + own_product(dscore, q, nn)
            dq = dq_rows_ref[:, b * 128 : (b + 1) * 128].astype(F32)
            dq = dq + own_product(dscore, k2, tn) * INV_SQRT
            for at, part in zip((b, b + PAIRS), unfold(dq)):
                dq_ref[:, at * 128 : (at + 1) * 128] = part.astype(BF16)
        for at, k_part, v_part in zip((h, h + 2), unfold(dsk * INV_SQRT), unfold(dsv)):
            dsk_ref[:, at * 128 : (at + 1) * 128] = k_part.astype(BF16)
            dsv_ref[:, at * 128 : (at + 1) * 128] = v_part.astype(BF16)
    stores = [
        pltpu.make_async_copy(source, target.at[0], sems.at[7 + 2 * SLOTS + i])
        for i, (source, target) in enumerate(
            [(dq_ref, dq_hbm), (dsk_ref, dsk_hbm), (dsv_ref, dsv_hbm)]
        )
    ]
    for copy in stores:
        copy.start()
    dq = dq_ref[...]
    keep = lax.broadcasted_iota(jnp.int32, (TOKENS, PADDED_RANK), 1) < rank
    lifted = jnp.where(keep, scale * nt(dq, wu_ref[...]), 0.0).astype(BF16)
    low = unfold(rows_ref[:, 2 * HALF :].astype(F32))[0][:, PADDED_RANK:].astype(BF16)
    loads[6].wait()

    def block(c):
        if c < DOWN_BLOCKS:
            return tn(lifted, x_ref[:, c * 128 : (c + 1) * 128])
        if c < GRAD_BLOCKS:
            at = (c - DOWN_BLOCKS) * 128
            return scale * tn(low, dq[:, at : at + 128])
        return jnp.zeros((PADDED_RANK, 128), F32)

    first = core_ref[0] == 0
    for c in range(CORE_BLOCKS):
        lower, upper = block(c), block(c + CORE_BLOCKS)
        at = slice(c * PADDED_RANK, (c + 1) * PADDED_RANK)
        mine_ref[at, :] = jnp.where(first, lower, upper).astype(BF16)
        other_ref[at, :] = jnp.where(first, upper, lower).astype(BF16)
    for copy in stores:
        copy.wait()


def spread_kernel(core_ref, mine_ref, other_ref, down_ref, up_ref):
    first = core_ref[0] == 0
    for c in range(GRAD_BLOCKS):
        at = c % CORE_BLOCKS * PADDED_RANK
        mine = mine_ref[at : at + PADDED_RANK, :].astype(F32)
        other = other_ref[at : at + PADDED_RANK, :].astype(F32)
        part = jnp.where(first, mine, other) if c < CORE_BLOCKS else jnp.where(first, other, mine)
        if c < DOWN_BLOCKS:
            down_ref[:, c * 128 : (c + 1) * 128] = part
        else:
            at = (c - DOWN_BLOCKS) * 128
            up_ref[:, at : at + 128] = part


VMEM = pl.BlockSpec(memory_space=pltpu.VMEM)
SMEM = pl.BlockSpec(memory_space=pltpu.SMEM)
HBM = pl.BlockSpec(memory_space=pltpu.HBM)


def call(kernel, in_specs, outs, scratch=(), out_specs=None, vmem_mib=40):
    return pl.pallas_call(
        kernel,
        out_shape=[jax.ShapeDtypeStruct(shape, dtype) for shape, dtype in outs],
        in_specs=in_specs,
        out_specs=out_specs or [VMEM] * len(outs),
        scratch_shapes=list(scratch),
        compiler_params=pltpu.CompilerParams(vmem_limit_bytes=vmem_mib * 1024 * 1024),
    )


def like(arrays):
    return [
        (pltpu.SMEM if a.dtype == jnp.int32 else pltpu.VMEM)(a.shape, a.dtype) for a in arrays
    ]


def run_prepare(*arrays):
    return call(
        prepare_kernel,
        [HBM] * len(arrays),
        [((SLOTS, 16, SEND_WIDTH), BF16)],
        like(arrays)
        + [
            pltpu.VMEM((ROWS, SEND_WIDTH), BF16),
            pltpu.SemaphoreType.DMA((9 + X_PARTS + 2 * SLOTS,)),
        ],
        [HBM],
        60,
    )(*arrays)[0]


def run_owner(rows, keys, values):
    return call(
        owner_kernel,
        [VMEM] * 3,
        [((ROWS, BACK_WIDTH), BF16)] + [((PLEN, KEY_VALUE_HEADS * HEAD_SIZE), BF16)] * 2,
    )(rows, keys, values)


def run_finish(*arrays):
    kv_width = KEY_VALUE_HEADS * HEAD_SIZE
    return call(
        finish_kernel,
        [HBM] * len(arrays),
        [
            ((1, TOKENS, QUERY_WIDTH), BF16),
            ((1, TOKENS, kv_width), BF16),
            ((1, TOKENS, kv_width), BF16),
            ((CORE_ROWS, 128), BF16),
            ((CORE_ROWS, 128), BF16),
        ],
        like(arrays[:7])
        + [
            pltpu.VMEM((ROWS, SEND_WIDTH), BF16),
            pltpu.VMEM((ROWS, BACK_WIDTH), BF16),
            pltpu.VMEM((TOKENS, QUERY_WIDTH), BF16),
            pltpu.VMEM((TOKENS, kv_width), BF16),
            pltpu.VMEM((TOKENS, kv_width), BF16),
            pltpu.SemaphoreType.DMA((10 + 2 * SLOTS,)),
        ],
        [HBM] * 3 + [VMEM] * 2,
        60,
    )(*arrays)


def run_spread(core, mine, other):
    return call(
        spread_kernel,
        [SMEM] + [VMEM] * 2,
        [((PADDED_RANK, MODEL_WIDTH), F32), ((PADDED_RANK, QUERY_WIDTH), F32)],
    )(core, mine, other)


def by_core(part):
    return lax.ppermute(part, "comp", [(i, i ^ 1) for i in range(16)])


def layer_groups():
    return [
        [(x * 4 + z_hi) * 16 + zy * 2 + core for x in range(4) for zy in range(8)]
        for z_hi in range(4)
        for core in range(2)
    ]


def sum_all(mine, other):
    rows = CORE_ROWS // 32
    swap = functools.partial(
        lax.all_to_all, axis_name=("prompt", "comp"), split_axis=0, concat_axis=0,
        axis_index_groups=layer_groups(), tiled=True,
    )
    pair = (mine.astype(F32) + by_core(other).astype(F32)).astype(BF16)
    total = jnp.sum(swap(pair.reshape(32, rows, 128)).astype(F32), axis=0)
    for flip in (lambda i: i ^ 1, lambda i: i // 4 * 4 + 3 - i % 4):
        total = total + lax.ppermute(total, "prompt", [(i, flip(i)) for i in range(16)])
    total = total.astype(BF16)
    half = swap(jnp.broadcast_to(total[None], (32, rows, 128))).reshape(CORE_ROWS, 128)
    return half, by_core(half)


def per_device(
    normed_hidden_input,
    frozen_query_base,
    attention_output_grad,
    completion_keys,
    completion_values,
    owner_prompt_keys,
    owner_prompt_values,
    adapter_down_weight,
    adapter_up_weight,
    adapter_rank,
    route,
    lengths,
):
    hidden = normed_hidden_input[0]
    keys, values = completion_keys[0], completion_values[0]
    send = run_prepare(
        adapter_rank, route, lengths, hidden, frozen_query_base[0], attention_output_grad[0],
        keys, values, adapter_down_weight.T, adapter_up_weight,
    )
    arrived = lax.all_to_all(send, "prompt", 0, 0, tiled=True)
    back, dk, dv = run_owner(
        arrived.reshape(ROWS, SEND_WIDTH), owner_prompt_keys[0], owner_prompt_values[0]
    )
    back = lax.all_to_all(back.reshape(SLOTS, 16, BACK_WIDTH), "prompt", 0, 0, tiled=True)
    core = (lax.axis_index("comp") % 2).astype(jnp.int32)[None]
    dq, dsk, dsv, mine, other = run_finish(
        route, adapter_rank, core, keys, values, adapter_up_weight, hidden, send, back
    )
    down, up = run_spread(core, *sum_all(mine, other))
    return dq, dsk, dsv, dk[None], dv[None], down.T, up


def solution(mesh):
    split = P("comp", "prompt", None)
    return jax.shard_map(
        per_device,
        mesh=mesh,
        in_specs=(split,) * 7 + (P(),) * 3 + (split,) * 2,
        out_specs=(split,) * 5 + (P(),) * 2,
        check_vma=False,
    )
```

```python
import functools
import math

import jax
import jax.numpy as jnp
from jax import lax
from jax.experimental import pallas as pl
from jax.experimental.pallas import tpu as pltpu
from jax.sharding import PartitionSpec as P

KEY_VALUE_HEADS = 4
GROUP = 5
HEAD_SIZE = 128
PLEN = 128
CL = 8
SLOTS = 16
TOKENS = SLOTS * CL
QUERY_HEADS = KEY_VALUE_HEADS * GROUP
PAIRS = QUERY_HEADS // 2
HALF = PAIRS * HEAD_SIZE
KV_HALF = KEY_VALUE_HEADS * HEAD_SIZE // 2
ROWS = 2 * TOKENS
MODEL_WIDTH = 5120
PADDED_RANK = 64
QUERY_WIDTH = QUERY_HEADS * HEAD_SIZE
SEND_WIDTH = 2 * HALF + 128
X_PARTS = 4
X_PART = MODEL_WIDTH // X_PARTS
BACK_WIDTH = HALF + 128
DOWN_BLOCKS = MODEL_WIDTH // 128
GRAD_BLOCKS = (MODEL_WIDTH + QUERY_WIDTH) // 128
CORE_BLOCKS = 32
CORE_ROWS = CORE_BLOCKS * PADDED_RANK

INV_SQRT = 1.0 / math.sqrt(HEAD_SIZE)
adapter_strength = 32.0
masked_score = -1e30

BF16 = jnp.bfloat16
F32 = jnp.float32


def dot(a, b, dims):
    return lax.dot_general(a, b, (dims, ((), ())), preferred_element_type=F32)


def nt(a, b):
    return dot(a, b, ((1,), (1,)))


def nn(a, b):
    return dot(a, b, ((1,), (0,)))


def tn(a, b):
    return dot(a, b, ((0,), (0,)))


def fold(wide):
    width = wide.shape[1] // 2
    left = wide[:, :width].reshape(SLOTS, 1, CL, width)
    right = wide[:, width:].reshape(SLOTS, 1, CL, width)
    return jnp.concatenate([left, right], axis=1).reshape(ROWS, width)


def unfold(rows):
    split = rows.reshape(SLOTS, 2, CL, rows.shape[1])
    return split[:, 0].reshape(TOKENS, -1), split[:, 1].reshape(TOKENS, -1)


def own_mask():
    key = lax.broadcasted_iota(jnp.int32, (TOKENS, ROWS), 0)
    row = lax.broadcasted_iota(jnp.int32, (TOKENS, ROWS), 1) % TOKENS
    return (key // CL == row // CL) & (key <= row)


def own_scores(keys, rows):
    return jnp.concatenate(
        [nt(keys[at : at + TOKENS], rows[at : at + TOKENS]) for at in (0, TOKENS)], axis=1
    )


def own_product(scores, rows, product):
    return jnp.concatenate(
        [product(scores[:, at : at + TOKENS], rows[at : at + TOKENS]) for at in (0, TOKENS)], axis=0
    )


def pack_stats(rows):
    value = jnp.concatenate(rows, axis=0)
    first = value.astype(BF16).astype(F32)
    rest = value - first
    second = rest.astype(BF16).astype(F32)
    third = rest - second
    pad = jnp.zeros((128 - 3 * len(rows), ROWS), F32)
    return jnp.concatenate([first, second, third, pad], axis=0).T


def unpack_stats(columns, count):
    parts = columns.astype(F32).T
    return parts[:count] + (parts[count : 2 * count] + parts[2 * count : 3 * count])


def prepare_kernel(
    rank_hbm, route_hbm, length_hbm, x_hbm, base_hbm, g_hbm, sk_hbm, sv_hbm, wd_hbm, wu_hbm,
    send_hbm,
    rank_ref, route_ref, length_ref, x_ref, base_ref, g_ref, sk_ref, sv_ref, wd_ref, wu_ref, rows_ref, sems,
):
    columns = [slice(i * X_PART, (i + 1) * X_PART) for i in range(X_PARTS)]
    pairs = [(rank_hbm, rank_ref), (length_hbm, length_ref), (route_hbm, route_ref)]
    pairs += [(wd_hbm, wd_ref)] + [(x_hbm.at[:, c], x_ref.at[:, c]) for c in columns]
    pairs += [
        (g_hbm, g_ref), (sv_hbm, sv_ref), (sk_hbm, sk_ref), (wu_hbm, wu_ref), (base_hbm, base_ref)
    ]
    loads = [
        pltpu.make_async_copy(source, target, sems.at[i])
        for i, (source, target) in enumerate(pairs)
    ]
    for copy in loads:
        copy.start()

    def sends(start, width, sem):
        return [
            pltpu.make_async_copy(
                rows_ref.at[pl.ds(s * 16, 16), pl.ds(start, width)],
                send_hbm.at[route_ref[0, 0, s], :, pl.ds(start, width)],
                sems.at[sem + s],
            )
            for s in range(SLOTS)
        ]

    for copy in loads[:3]:
        copy.wait()
    rank = rank_ref[0]
    scale = adapter_strength / rank.astype(F32)
    position = lax.broadcasted_iota(jnp.int32, (CL, 128), 0)
    live = jnp.concatenate(
        [jnp.where(position < length_ref[0, 0, s], 1.0, 0.0) for s in range(SLOTS)], axis=0
    )
    mask = own_mask()
    loads[3].wait()
    low = jnp.zeros((TOKENS, PADDED_RANK), F32)
    for i, c in enumerate(columns):
        loads[4 + i].wait()
        low = low + nt(x_ref[:, c], wd_ref[:, c])
    rest = 4 + X_PARTS
    loads[rest].wait()
    for n in range(PAIRS):
        left, right = (g_ref[:, m * 128 : (m + 1) * 128].astype(F32) * live for m in (n, n + PAIRS))
        rows_ref[:, n * 128 : (n + 1) * 128] = fold(
            jnp.concatenate([left, right], axis=1)
        ).astype(BF16)
    early = sends(0, HALF, rest + 5)
    for copy in early:
        copy.start()
    for copy in loads[rest + 1 :]:
        copy.wait()
    values = fold(sv_ref[...].astype(F32)).astype(BF16)
    keys = fold(sk_ref[...].astype(F32)).astype(BF16)
    keep = lax.broadcasted_iota(jnp.int32, (TOKENS, PADDED_RANK), 1) < rank
    low = jnp.where(keep, low, 0.0).astype(BF16)
    query = base_ref[...].astype(F32) + scale * nn(low, wu_ref[...])
    rows_ref[:, HALF : 2 * HALF] = fold(query).astype(BF16)

    def products(b):
        h = b // GROUP
        g = rows_ref[:, b * 128 : (b + 1) * 128]
        q = rows_ref[:, HALF + b * 128 : HALF + (b + 1) * 128]
        return (
            own_scores(keys[:, h * 128 : (h + 1) * 128], q),
            own_scores(values[:, h * 128 : (h + 1) * 128], g),
        )

    lses, deltas = [], []
    ready = products(0)
    for b in range(PAIRS):
        scores, dprob = ready
        if b + 1 < PAIRS:
            ready = products(b + 1)
        scores = jnp.where(mask, scores * INV_SQRT, masked_score)
        top = jnp.max(scores, axis=0, keepdims=True)
        weight = jnp.exp(scores - top)
        total = jnp.sum(weight, axis=0, keepdims=True)
        lses.append(top + jnp.log(total))
        deltas.append(jnp.sum(weight * dprob, axis=0, keepdims=True) / total)
    none = jnp.zeros((TOKENS, PADDED_RANK), F32)
    low_rows = fold(jnp.concatenate([none, low.astype(F32), none, none], axis=1))
    rows_ref[:, 2 * HALF :] = (pack_stats(lses + deltas) + low_rows).astype(BF16)
    late = sends(HALF, SEND_WIDTH - HALF, rest + 5 + SLOTS)
    for copy in late:
        copy.start()
    for copy in early + late:
        copy.wait()


def owner_kernel(rows_ref, k_ref, v_ref, back_ref, dk_ref, dv_ref):
    lower = (lax.broadcasted_iota(jnp.int32, (ROWS, HEAD_SIZE), 0) // CL % 2 == 0).astype(F32)
    lower, upper = lower.astype(BF16), (1.0 - lower).astype(BF16)
    stats = unpack_stats(rows_ref[:, 2 * HALF :], 2 * PAIRS)

    def beside(ref, h):
        return jnp.concatenate([ref[:, m * 128 : (m + 1) * 128] for m in (h, h + 2)], axis=1)

    def apart(rows):
        return jnp.concatenate([rows * lower, rows * upper], axis=1)

    sides = [(beside(k_ref, h), beside(v_ref, h)) for h in range(2)]

    def products(b):
        g = apart(rows_ref[:, b * 128 : (b + 1) * 128])
        q = apart(rows_ref[:, HALF + b * 128 : HALF + (b + 1) * 128])
        keys, values = sides[b // GROUP]
        return q, g, nt(keys, q), nt(values, g)

    lses, deltas = [], []
    ready = products(0)
    for h in range(2):
        keys = sides[h][0]
        dk = jnp.zeros((PLEN, 2 * HEAD_SIZE), F32)
        dv = jnp.zeros((PLEN, 2 * HEAD_SIZE), F32)
        for b in range(h * GROUP, (h + 1) * GROUP):
            q, g, scores, dprob = ready
            if b + 1 < PAIRS:
                ready = products(b + 1)
            own_lse, own_delta = stats[b : b + 1], stats[PAIRS + b : PAIRS + b + 1]
            scores = scores * INV_SQRT
            top = jnp.max(scores, axis=0, keepdims=True)
            weight = jnp.exp(scores - top)
            prompt_lse = top + jnp.log(jnp.sum(weight, axis=0, keepdims=True))
            high = jnp.maximum(prompt_lse, own_lse)
            lse = high + jnp.log(jnp.exp(prompt_lse - high) + jnp.exp(own_lse - high))
            probs = weight * jnp.exp(top - lse)
            probs_b = probs.astype(BF16)
            delta = jnp.sum(probs_b.astype(F32) * dprob, axis=0, keepdims=True) + own_delta * jnp.exp(
                own_lse - lse
            )
            dscore = (probs * (dprob - delta)).astype(BF16)
            dv = dv + nn(probs_b, g)
            dk = dk + nn(dscore, q)
            dq = (tn(dscore, keys) * INV_SQRT).reshape(SLOTS, 2, CL, 2 * HEAD_SIZE)
            dq = jnp.concatenate([dq[:, :1, :, :HEAD_SIZE], dq[:, 1:, :, HEAD_SIZE:]], axis=1)
            back_ref[:, b * 128 : (b + 1) * 128] = dq.reshape(ROWS, HEAD_SIZE).astype(BF16)
            lses.append(lse)
            deltas.append(delta)
        for at, m in ((0, h), (HEAD_SIZE, h + 2)):
            dk_ref[:, m * 128 : (m + 1) * 128] = (dk[:, at : at + HEAD_SIZE] * INV_SQRT).astype(BF16)
            dv_ref[:, m * 128 : (m + 1) * 128] = dv[:, at : at + HEAD_SIZE].astype(BF16)
    back_ref[:, HALF:] = pack_stats(lses + deltas).astype(BF16)


def own_kernel(
    rank_ref, route_ref, core_ref, sk_hbm, sv_hbm, send_hbm,
    rows_ref, keys_ref, values_ref, order_ref, factors_ref,
    sk_ref, sv_ref, sems,
):
    pairs = [(sk_hbm, sk_ref), (sv_hbm, sv_ref)]
    pairs += [
        (send_hbm.at[route_ref[0, 0, s]], rows_ref.at[pl.ds(s * 16, 16)]) for s in range(SLOTS)
    ]
    loads = [
        pltpu.make_async_copy(source, target, sems.at[i])
        for i, (source, target) in enumerate(pairs)
    ]
    for copy in loads:
        copy.start()
    rank = rank_ref[0]
    scale = adapter_strength / rank.astype(F32)
    block = (PADDED_RANK, 128)
    keep = lax.broadcasted_iota(jnp.int32, block, 1) < rank
    factors_ref[0] = jnp.full(block, scale, F32)
    factors_ref[1] = jnp.where(keep, scale, 0.0)
    factors_ref[2] = jnp.full(block, 1.0, F32) * (core_ref[0] == 0).astype(F32)
    lane = lax.broadcasted_iota(jnp.int32, (16, ROWS), 1)
    place = lax.broadcasted_iota(jnp.int32, (16, ROWS), 0)
    for s in range(SLOTS):
        at = (lane == route_ref[0, 0, s] * 16 + place).astype(F32)
        order_ref[s * 16 : (s + 1) * 16, :] = at.astype(BF16)
    for copy in loads:
        copy.wait()
    keys_ref[...] = fold(sk_ref[...].astype(F32)).astype(BF16)
    values_ref[...] = fold(sv_ref[...].astype(F32)).astype(BF16)


def finish_kernel(
    x_hbm, wu_hbm, rows_ref, keys_ref, values_ref, order_ref, factors_ref, back_ref,
    dq_hbm, dsk_hbm, dsv_hbm, mine_ref, other_ref,
    x_ref, wu_ref, dq_rows_ref, dq_ref, dsk_ref, dsv_ref, sems,
):
    loads = [
        pltpu.make_async_copy(wu_hbm, wu_ref, sems.at[3]),
        pltpu.make_async_copy(x_hbm, x_ref, sems.at[4]),
    ]
    for copy in loads:
        copy.start()
    order = order_ref[...]
    mask = own_mask()

    def products(b):
        h = b // GROUP
        g = rows_ref[:, b * 128 : (b + 1) * 128]
        q = rows_ref[:, HALF + b * 128 : HALF + (b + 1) * 128]
        return (
            q, g,
            own_scores(keys_ref[:, h * 128 : (h + 1) * 128], q),
            own_scores(values_ref[:, h * 128 : (h + 1) * 128], g),
        )

    ready = products(0)
    stats = unpack_stats(nn(order, back_ref[:, HALF:]), 2 * PAIRS)
    dq_rows_ref[...] = nn(order, back_ref[:, :HALF])
    for h in range(2):
        k2 = keys_ref[:, h * 128 : (h + 1) * 128]
        dsk = jnp.zeros((ROWS, HEAD_SIZE), F32)
        dsv = jnp.zeros((ROWS, HEAD_SIZE), F32)
        for b in range(h * GROUP, (h + 1) * GROUP):
            q, g, scores, dprob = ready
            if b + 1 < PAIRS:
                ready = products(b + 1)
            lse, delta = stats[b : b + 1], stats[PAIRS + b : PAIRS + b + 1]
            probs = jnp.exp(jnp.where(mask, scores * INV_SQRT - lse, masked_score))
            dscore = (probs * (dprob - delta)).astype(BF16)
            dq = dq_rows_ref[:, b * 128 : (b + 1) * 128] + own_product(dscore, k2, tn) * INV_SQRT
            for at, part in zip((b, b + PAIRS), unfold(dq)):
                dq_ref[:, at * 128 : (at + 1) * 128] = part.astype(BF16)
            dsv = dsv + own_product(probs.astype(BF16), g, nn)
            dsk = dsk + own_product(dscore, q, nn)
        for at, k_part, v_part in zip((h, h + 2), unfold(dsk * INV_SQRT), unfold(dsv)):
            dsk_ref[:, at * 128 : (at + 1) * 128] = k_part.astype(BF16)
            dsv_ref[:, at * 128 : (at + 1) * 128] = v_part.astype(BF16)
    stores = [
        pltpu.make_async_copy(source, target.at[0], sems.at[i])
        for i, (source, target) in enumerate(
            [(dq_ref, dq_hbm), (dsk_ref, dsk_hbm), (dsv_ref, dsv_hbm)]
        )
    ]
    for copy in stores:
        copy.start()
    dq = dq_ref[...]
    for copy in loads:
        copy.wait()
    lifted = (nt(dq, wu_ref[...]) * factors_ref[1, :1, :PADDED_RANK]).astype(BF16)
    low = unfold(rows_ref[:, 2 * HALF :].astype(F32))[0][:, PADDED_RANK:].astype(BF16)
    scale, first = factors_ref[0], factors_ref[2] > 0.5

    def block(c):
        if c < DOWN_BLOCKS:
            return tn(lifted, x_ref[:, c * 128 : (c + 1) * 128])
        if c < GRAD_BLOCKS:
            at = (c - DOWN_BLOCKS) * 128
            return scale * tn(low, dq[:, at : at + 128])
        return jnp.zeros((PADDED_RANK, 128), F32)

    for c in range(CORE_BLOCKS):
        lower, upper = block(c), block(c + CORE_BLOCKS)
        at = slice(c * PADDED_RANK, (c + 1) * PADDED_RANK)
        mine_ref[at, :] = jnp.where(first, lower, upper).astype(BF16)
        other_ref[at, :] = jnp.where(first, upper, lower).astype(BF16)
    for copy in stores:
        copy.wait()


def spread_kernel(factors_ref, mine_ref, other_ref, down_ref, up_ref):
    first = factors_ref[2] > 0.5
    for c in range(GRAD_BLOCKS):
        at = c % CORE_BLOCKS * PADDED_RANK
        mine = mine_ref[at : at + PADDED_RANK, :].astype(F32)
        other = other_ref[at : at + PADDED_RANK, :].astype(F32)
        part = jnp.where(first, mine, other) if c < CORE_BLOCKS else jnp.where(first, other, mine)
        if c < DOWN_BLOCKS:
            down_ref[:, c * 128 : (c + 1) * 128] = part
        else:
            at = (c - DOWN_BLOCKS) * 128
            up_ref[:, at : at + 128] = part


VMEM = pl.BlockSpec(memory_space=pltpu.VMEM)
SMEM = pl.BlockSpec(memory_space=pltpu.SMEM)
HBM = pl.BlockSpec(memory_space=pltpu.HBM)


def call(kernel, in_specs, outs, scratch=(), out_specs=None, vmem_mib=40):
    return pl.pallas_call(
        kernel,
        out_shape=[jax.ShapeDtypeStruct(shape, dtype) for shape, dtype in outs],
        in_specs=in_specs,
        out_specs=out_specs or [VMEM] * len(outs),
        scratch_shapes=list(scratch),
        compiler_params=pltpu.CompilerParams(vmem_limit_bytes=vmem_mib * 1024 * 1024),
    )


def like(arrays):
    return [
        (pltpu.SMEM if a.dtype == jnp.int32 else pltpu.VMEM)(a.shape, a.dtype) for a in arrays
    ]


def run_prepare(*arrays):
    return call(
        prepare_kernel,
        [HBM] * len(arrays),
        [((SLOTS, 16, SEND_WIDTH), BF16)],
        like(arrays)
        + [
            pltpu.VMEM((ROWS, SEND_WIDTH), BF16),
            pltpu.SemaphoreType.DMA((9 + X_PARTS + 2 * SLOTS,)),
        ],
        [HBM],
        60,
    )(*arrays)[0]


def run_owner(rows, keys, values):
    return call(
        owner_kernel,
        [VMEM] * 3,
        [((ROWS, BACK_WIDTH), BF16)] + [((PLEN, KEY_VALUE_HEADS * HEAD_SIZE), BF16)] * 2,
    )(rows, keys, values)


def run_own(rank, route, core, *arrays):
    return call(
        own_kernel,
        [SMEM] * 3 + [HBM] * len(arrays),
        [
            ((ROWS, SEND_WIDTH), BF16),
            ((ROWS, KV_HALF), BF16),
            ((ROWS, KV_HALF), BF16),
            ((ROWS, ROWS), BF16),
            ((3, PADDED_RANK, 128), F32),
        ],
        like(arrays[:2]) + [pltpu.SemaphoreType.DMA((2 + SLOTS,))],
    )(rank, route, core, *in_hbm(arrays))


def in_hbm(arrays):
    return [pltpu.with_memory_space_constraint(a, pltpu.HBM) for a in arrays]


def run_finish(x, wu, *arrays):
    kv_width = KEY_VALUE_HEADS * HEAD_SIZE
    return call(
        finish_kernel,
        [HBM] * 2 + [VMEM] * len(arrays),
        [
            ((1, TOKENS, QUERY_WIDTH), BF16),
            ((1, TOKENS, kv_width), BF16),
            ((1, TOKENS, kv_width), BF16),
            ((CORE_ROWS, 128), BF16),
            ((CORE_ROWS, 128), BF16),
        ],
        like([x, wu])
        + [
            pltpu.VMEM((ROWS, HALF), F32),
            pltpu.VMEM((TOKENS, QUERY_WIDTH), BF16),
            pltpu.VMEM((TOKENS, kv_width), BF16),
            pltpu.VMEM((TOKENS, kv_width), BF16),
            pltpu.SemaphoreType.DMA((5,)),
        ],
        [HBM] * 3 + [VMEM] * 2,
    )(*in_hbm([x, wu]), *arrays)


def run_spread(*arrays):
    return call(
        spread_kernel,
        [VMEM] * len(arrays),
        [((PADDED_RANK, MODEL_WIDTH), F32), ((PADDED_RANK, QUERY_WIDTH), F32)],
    )(*arrays)


def by_core(part):
    return lax.ppermute(part, "comp", [(i, i ^ 1) for i in range(16)])


def layer_groups():
    return [
        [(x * 4 + z_hi) * 16 + zy * 2 + core for x in range(4) for zy in range(8)]
        for z_hi in range(4)
        for core in range(2)
    ]


def sum_all(mine, other):
    rows = CORE_ROWS // 32
    swap = functools.partial(
        lax.all_to_all, axis_name=("prompt", "comp"), split_axis=0, concat_axis=0,
        axis_index_groups=layer_groups(), tiled=True,
    )
    pair = (mine.astype(F32) + by_core(other).astype(F32)).astype(BF16)
    total = jnp.sum(swap(pair.reshape(32, rows, 128)).astype(F32), axis=0)
    for flip in (lambda i: i ^ 1, lambda i: i // 4 * 4 + 3 - i % 4):
        total = total + lax.ppermute(total, "prompt", [(i, flip(i)) for i in range(16)])
    total = total.astype(BF16)
    half = swap(jnp.broadcast_to(total[None], (32, rows, 128))).reshape(CORE_ROWS, 128)
    return half, by_core(half)


def per_device(
    normed_hidden_input,
    frozen_query_base,
    attention_output_grad,
    completion_keys,
    completion_values,
    owner_prompt_keys,
    owner_prompt_values,
    adapter_down_weight,
    adapter_up_weight,
    adapter_rank,
    route,
    lengths,
):
    hidden = normed_hidden_input[0]
    keys, values = completion_keys[0], completion_values[0]
    send = run_prepare(
        adapter_rank, route, lengths, hidden, frozen_query_base[0], attention_output_grad[0],
        keys, values, adapter_down_weight.T, adapter_up_weight,
    )
    arrived = lax.all_to_all(send, "prompt", 0, 0, tiled=True)
    back, dk, dv = run_owner(
        arrived.reshape(ROWS, SEND_WIDTH), owner_prompt_keys[0], owner_prompt_values[0]
    )
    back = lax.all_to_all(back.reshape(SLOTS, 16, BACK_WIDTH), "prompt", 0, 0, tiled=True)
    core = (lax.axis_index("comp") % 2).astype(jnp.int32)[None]
    own = run_own(adapter_rank, route, core, keys, values, send)
    dq, dsk, dsv, mine, other = run_finish(
        hidden, adapter_up_weight, *own, back.reshape(ROWS, BACK_WIDTH)
    )
    down, up = run_spread(own[-1], *sum_all(mine, other))
    return dq, dsk, dsv, dk[None], dv[None], down.T, up


def solution(mesh):
    split = P("comp", "prompt", None)
    return jax.shard_map(
        per_device,
        mesh=mesh,
        in_specs=(split,) * 7 + (P(),) * 3 + (split,) * 2,
        out_specs=(split,) * 5 + (P(),) * 2,
        check_vma=False,
    )
```

```python
import functools
import math

import jax
import jax.numpy as jnp
from jax import lax
from jax.experimental import pallas as pl
from jax.experimental.pallas import tpu as pltpu
from jax.sharding import PartitionSpec as P

KEY_VALUE_HEADS = 4
GROUP = 5
HEAD_SIZE = 128
PLEN = 128
CL = 8
SLOTS = 16
TOKENS = SLOTS * CL
QUERY_HEADS = KEY_VALUE_HEADS * GROUP
PAIRS = QUERY_HEADS // 2
HALF = PAIRS * HEAD_SIZE
KV_HALF = KEY_VALUE_HEADS * HEAD_SIZE // 2
ROWS = 2 * TOKENS
MODEL_WIDTH = 5120
PADDED_RANK = 64
QUERY_WIDTH = QUERY_HEADS * HEAD_SIZE
SEND_WIDTH = 2 * HALF + 128
X_PARTS = 4
COST_FLOPS = 10**9
COST_BYTES = 60 * 10**6
X_PART = MODEL_WIDTH // X_PARTS
BACK_WIDTH = HALF + 128
DOWN_BLOCKS = MODEL_WIDTH // 128
GRAD_BLOCKS = (MODEL_WIDTH + QUERY_WIDTH) // 128
CORE_BLOCKS = 32
CORE_ROWS = CORE_BLOCKS * PADDED_RANK

INV_SQRT = 1.0 / math.sqrt(HEAD_SIZE)
adapter_strength = 32.0
masked_score = -1e30

BF16 = jnp.bfloat16
F32 = jnp.float32


def dot(a, b, dims):
    return lax.dot_general(a, b, (dims, ((), ())), preferred_element_type=F32)


def nt(a, b):
    return dot(a, b, ((1,), (1,)))


def nn(a, b):
    return dot(a, b, ((1,), (0,)))


def tn(a, b):
    return dot(a, b, ((0,), (0,)))


def fold(wide):
    width = wide.shape[1] // 2
    left = wide[:, :width].reshape(SLOTS, 1, CL, width)
    right = wide[:, width:].reshape(SLOTS, 1, CL, width)
    return jnp.concatenate([left, right], axis=1).reshape(ROWS, width)


def unfold(rows):
    split = rows.reshape(SLOTS, 2, CL, rows.shape[1])
    return split[:, 0].reshape(TOKENS, -1), split[:, 1].reshape(TOKENS, -1)


def own_mask():
    key = lax.broadcasted_iota(jnp.int32, (TOKENS, ROWS), 0)
    row = lax.broadcasted_iota(jnp.int32, (TOKENS, ROWS), 1) % TOKENS
    return (key // CL == row // CL) & (key <= row)


def own_scores(keys, rows):
    return jnp.concatenate(
        [nt(keys[at : at + TOKENS], rows[at : at + TOKENS]) for at in (0, TOKENS)], axis=1
    )


def own_product(scores, rows, product):
    return jnp.concatenate(
        [product(scores[:, at : at + TOKENS], rows[at : at + TOKENS]) for at in (0, TOKENS)], axis=0
    )


def pack_stats(rows):
    value = jnp.concatenate(rows, axis=0)
    first = value.astype(BF16).astype(F32)
    rest = value - first
    second = rest.astype(BF16).astype(F32)
    third = rest - second
    pad = jnp.zeros((128 - 3 * len(rows), ROWS), F32)
    return jnp.concatenate([first, second, third, pad], axis=0).T


def unpack_stats(columns, count):
    parts = columns.astype(F32).T
    return parts[:count] + (parts[count : 2 * count] + parts[2 * count : 3 * count])


def prepare_kernel(
    rank_hbm, route_hbm, length_hbm, x_hbm, base_hbm, g_hbm, sk_hbm, sv_hbm, wd_hbm, wu_hbm,
    send_hbm,
    rank_ref, route_ref, length_ref, x_ref, base_ref, g_ref, sk_ref, sv_ref, wd_ref, wu_ref, rows_ref, sems,
):
    columns = [slice(i * X_PART, (i + 1) * X_PART) for i in range(X_PARTS)]
    pairs = [(rank_hbm, rank_ref), (length_hbm, length_ref), (route_hbm, route_ref)]
    pairs += [(wd_hbm, wd_ref)] + [(x_hbm.at[:, c], x_ref.at[:, c]) for c in columns]
    pairs += [
        (g_hbm, g_ref), (sv_hbm, sv_ref), (sk_hbm, sk_ref), (wu_hbm, wu_ref), (base_hbm, base_ref)
    ]
    loads = [
        pltpu.make_async_copy(source, target, sems.at[i])
        for i, (source, target) in enumerate(pairs)
    ]
    for copy in loads:
        copy.start()

    def sends(start, width, sem):
        return [
            pltpu.make_async_copy(
                rows_ref.at[pl.ds(s * 16, 16), pl.ds(start, width)],
                send_hbm.at[route_ref[0, 0, s], :, pl.ds(start, width)],
                sems.at[sem + s],
            )
            for s in range(SLOTS)
        ]

    for copy in loads[:3]:
        copy.wait()
    rank = rank_ref[0]
    scale = adapter_strength / rank.astype(F32)
    position = lax.broadcasted_iota(jnp.int32, (CL, 128), 0)
    live = jnp.concatenate(
        [jnp.where(position < length_ref[0, 0, s], 1.0, 0.0) for s in range(SLOTS)], axis=0
    )
    mask = own_mask()
    loads[3].wait()
    low = jnp.zeros((TOKENS, PADDED_RANK), F32)
    for i, c in enumerate(columns):
        loads[4 + i].wait()
        low = low + nt(x_ref[:, c], wd_ref[:, c])
    rest = 4 + X_PARTS
    loads[rest].wait()
    for n in range(PAIRS):
        left, right = (g_ref[:, m * 128 : (m + 1) * 128].astype(F32) * live for m in (n, n + PAIRS))
        rows_ref[:, n * 128 : (n + 1) * 128] = fold(
            jnp.concatenate([left, right], axis=1)
        ).astype(BF16)
    early = sends(0, HALF, rest + 5)
    for copy in early:
        copy.start()
    for copy in loads[rest + 1 :]:
        copy.wait()
    values = fold(sv_ref[...].astype(F32)).astype(BF16)
    keys = fold(sk_ref[...].astype(F32)).astype(BF16)
    keep = lax.broadcasted_iota(jnp.int32, (TOKENS, PADDED_RANK), 1) < rank
    low = jnp.where(keep, low, 0.0).astype(BF16)
    query = base_ref[...].astype(F32) + scale * nn(low, wu_ref[...])
    rows_ref[:, HALF : 2 * HALF] = fold(query).astype(BF16)

    def products(b):
        h = b // GROUP
        g = rows_ref[:, b * 128 : (b + 1) * 128]
        q = rows_ref[:, HALF + b * 128 : HALF + (b + 1) * 128]
        return (
            own_scores(keys[:, h * 128 : (h + 1) * 128], q),
            own_scores(values[:, h * 128 : (h + 1) * 128], g),
        )

    lses, deltas = [], []
    ready = products(0)
    for b in range(PAIRS):
        scores, dprob = ready
        if b + 1 < PAIRS:
            ready = products(b + 1)
        scores = jnp.where(mask, scores * INV_SQRT, masked_score)
        top = jnp.max(scores, axis=0, keepdims=True)
        weight = jnp.exp(scores - top)
        total = jnp.sum(weight, axis=0, keepdims=True)
        lses.append(top + jnp.log(total))
        deltas.append(jnp.sum(weight * dprob, axis=0, keepdims=True) / total)
    none = jnp.zeros((TOKENS, PADDED_RANK), F32)
    low_rows = fold(jnp.concatenate([none, low.astype(F32), none, none], axis=1))
    rows_ref[:, 2 * HALF :] = (pack_stats(lses + deltas) + low_rows).astype(BF16)
    late = sends(HALF, SEND_WIDTH - HALF, rest + 5 + SLOTS)
    for copy in late:
        copy.start()
    for copy in early + late:
        copy.wait()


def owner_kernel(
    rows_ref, kv0_ref, kv1_ref, kv2_ref, kv3_ref,
    back_ref, part0_ref, part1_ref, part2_ref, part3_ref,
):
    kv_refs = (kv0_ref, kv1_ref, kv2_ref, kv3_ref)
    part_refs = (part0_ref, part1_ref, part2_ref, part3_ref)
    places = [(x * 4 + k) * 16 for k in range(4) for x in range(4)]
    lower = (lax.broadcasted_iota(jnp.int32, (ROWS, HEAD_SIZE), 0) // CL % 2 == 0).astype(F32)
    lower, upper = lower.astype(BF16), (1.0 - lower).astype(BF16)
    even = lax.broadcasted_iota(jnp.int32, (PLEN, 128), 1) < 64

    def load(at):
        return jnp.concatenate([rows_ref[p : p + 16, at : at + 128] for p in places], axis=0)

    def store(at, value):
        for i, p in enumerate(places):
            back_ref[p : p + 16, at : at + 128] = value[i * 16 : (i + 1) * 16]

    def beside(k, at):
        return jnp.concatenate([kv_refs[k][:, at + m : at + m + 128] for m in (0, 256)], axis=1)

    def apart(rows):
        return jnp.concatenate([rows * lower, rows * upper], axis=1)

    def by_prompt(rows):
        none = jnp.zeros((64, 256), BF16)
        return jnp.concatenate(
            [
                jnp.concatenate([rows[:64], none], axis=1),
                jnp.concatenate([none, rows[64:]], axis=1),
            ],
            axis=0,
        )

    def against(sides, rows):
        parts = []
        for p in range(2):
            two = rows[p * 128 : (p + 1) * 128]
            parts.append(jnp.where(even, nt(sides[2 * p], two), nt(sides[2 * p + 1], two)))
        return jnp.concatenate(parts, axis=1)

    sides = [
        ([beside(k, h * 128) for k in range(4)], [beside(k, 512 + h * 128) for k in range(4)])
        for h in range(2)
    ]
    stats = unpack_stats(load(2 * HALF), 2 * PAIRS)

    def products(b):
        g = apart(load(b * 128))
        q = apart(load(HALF + b * 128))
        keys, values = sides[b // GROUP]
        return q, g, against(keys, q), against(values, g)

    lses, deltas = [], []
    ready = products(0)
    for h in range(2):
        keys = sides[h][0]
        done = []
        for b in range(h * GROUP, (h + 1) * GROUP):
            q, g, scores, dprob = ready
            if b + 1 < PAIRS:
                ready = products(b + 1)
            own_lse, own_delta = stats[b : b + 1], stats[PAIRS + b : PAIRS + b + 1]
            scores = scores * INV_SQRT
            top = jnp.max(scores, axis=0, keepdims=True)
            weight = jnp.exp(scores - top)
            prompt_lse = top + jnp.log(jnp.sum(weight, axis=0, keepdims=True))
            high = jnp.maximum(prompt_lse, own_lse)
            lse = high + jnp.log(jnp.exp(prompt_lse - high) + jnp.exp(own_lse - high))
            probs = weight * jnp.exp(top - lse)
            probs_b = probs.astype(BF16)
            delta = jnp.sum(probs_b.astype(F32) * dprob, axis=0, keepdims=True) + own_delta * jnp.exp(
                own_lse - lse
            )
            dscore = (probs * (dprob - delta)).astype(BF16)
            picks = []
            for p in range(2):
                both = jnp.concatenate([keys[2 * p], keys[2 * p + 1]], axis=1)
                full = tn(dscore[:, p * 128 : (p + 1) * 128], both) * INV_SQRT
                for k in range(2):
                    rows = full[k * 64 : (k + 1) * 64, k * 256 : (k + 1) * 256]
                    rows = rows.reshape(4, 2, CL, 256)
                    rows = jnp.concatenate(
                        [rows[:, :1, :, :HEAD_SIZE], rows[:, 1:, :, HEAD_SIZE:]], axis=1
                    )
                    picks.append(rows.reshape(64, HEAD_SIZE))
            store(b * 128, jnp.concatenate(picks, axis=0).astype(BF16))
            done.append((dscore, q, probs_b, g))
            lses.append(lse)
            deltas.append(delta)
        for p in range(2):
            at = slice(p * 128, (p + 1) * 128)
            for first, scale, base in ((0, INV_SQRT, 0), (2, 1.0, 512)):
                left = jnp.concatenate([d[first][:, at] for d in done], axis=1)
                right = jnp.concatenate([by_prompt(d[first + 1][at]) for d in done], axis=0)
                grad = nn(left, right) * scale
                for k in range(2):
                    ref = part_refs[2 * p + k]
                    for i, m in enumerate((h, h + 2)):
                        column = k * 256 + i * 128
                        ref[:, base + m * 128 : base + (m + 1) * 128] = grad[
                            :, column : column + 128
                        ].astype(ref.dtype)
    store(HALF, pack_stats(lses + deltas).astype(BF16))


def own_kernel(
    rank_ref, route_ref, core_ref, sk_hbm, sv_hbm, send_hbm,
    rows_ref, keys_ref, values_ref, order_ref, factors_ref,
    sk_ref, sv_ref, sems,
):
    pairs = [(sk_hbm, sk_ref), (sv_hbm, sv_ref)]
    pairs += [
        (send_hbm.at[route_ref[0, 0, s]], rows_ref.at[pl.ds(s * 16, 16)]) for s in range(SLOTS)
    ]
    loads = [
        pltpu.make_async_copy(source, target, sems.at[i])
        for i, (source, target) in enumerate(pairs)
    ]
    for copy in loads:
        copy.start()
    rank = rank_ref[0]
    scale = adapter_strength / rank.astype(F32)
    block = (PADDED_RANK, 128)
    keep = lax.broadcasted_iota(jnp.int32, block, 1) < rank
    factors_ref[0] = jnp.full(block, scale, F32)
    factors_ref[1] = jnp.where(keep, scale, 0.0)
    factors_ref[2] = jnp.full(block, 1.0, F32) * (core_ref[0] == 0).astype(F32)
    lane = lax.broadcasted_iota(jnp.int32, (16, ROWS), 1)
    place = lax.broadcasted_iota(jnp.int32, (16, ROWS), 0)
    for s in range(SLOTS):
        at = (lane == route_ref[0, 0, s] * 16 + place).astype(F32)
        order_ref[s * 16 : (s + 1) * 16, :] = at.astype(BF16)
    for copy in loads:
        copy.wait()
    keys_ref[...] = fold(sk_ref[...].astype(F32)).astype(BF16)
    values_ref[...] = fold(sv_ref[...].astype(F32)).astype(BF16)


def finish_kernel(
    x_hbm, wu_hbm, rows_ref, keys_ref, values_ref, order_ref, factors_ref, back_ref,
    dq_hbm, dsk_hbm, dsv_hbm, mine_ref, other_ref,
    x_ref, wu_ref, dq_rows_ref, dq_ref, dsk_ref, dsv_ref, sems,
):
    loads = [
        pltpu.make_async_copy(wu_hbm, wu_ref, sems.at[3]),
        pltpu.make_async_copy(x_hbm, x_ref, sems.at[4]),
    ]
    for copy in loads:
        copy.start()
    order = order_ref[...]
    mask = own_mask()

    def products(b):
        h = b // GROUP
        g = rows_ref[:, b * 128 : (b + 1) * 128]
        q = rows_ref[:, HALF + b * 128 : HALF + (b + 1) * 128]
        return (
            q, g,
            own_scores(keys_ref[:, h * 128 : (h + 1) * 128], q),
            own_scores(values_ref[:, h * 128 : (h + 1) * 128], g),
        )

    ready = products(0)
    stats = unpack_stats(nn(order, back_ref[:, HALF:]), 2 * PAIRS)
    dq_rows_ref[...] = nn(order, back_ref[:, :HALF])
    for h in range(2):
        k2 = keys_ref[:, h * 128 : (h + 1) * 128]
        dsk = jnp.zeros((ROWS, HEAD_SIZE), F32)
        dsv = jnp.zeros((ROWS, HEAD_SIZE), F32)
        for b in range(h * GROUP, (h + 1) * GROUP):
            q, g, scores, dprob = ready
            if b + 1 < PAIRS:
                ready = products(b + 1)
            lse, delta = stats[b : b + 1], stats[PAIRS + b : PAIRS + b + 1]
            probs = jnp.exp(jnp.where(mask, scores * INV_SQRT - lse, masked_score))
            dscore = (probs * (dprob - delta)).astype(BF16)
            dq = dq_rows_ref[:, b * 128 : (b + 1) * 128] + own_product(dscore, k2, tn) * INV_SQRT
            for at, part in zip((b, b + PAIRS), unfold(dq)):
                dq_ref[:, at * 128 : (at + 1) * 128] = part.astype(BF16)
            dsv = dsv + own_product(probs.astype(BF16), g, nn)
            dsk = dsk + own_product(dscore, q, nn)
        for at, k_part, v_part in zip((h, h + 2), unfold(dsk * INV_SQRT), unfold(dsv)):
            dsk_ref[:, at * 128 : (at + 1) * 128] = k_part.astype(BF16)
            dsv_ref[:, at * 128 : (at + 1) * 128] = v_part.astype(BF16)
    stores = [
        pltpu.make_async_copy(source, target.at[0], sems.at[i])
        for i, (source, target) in enumerate(
            [(dq_ref, dq_hbm), (dsk_ref, dsk_hbm), (dsv_ref, dsv_hbm)]
        )
    ]
    for copy in stores:
        copy.start()
    dq = dq_ref[...]
    for copy in loads:
        copy.wait()
    lifted = (nt(dq, wu_ref[...]) * factors_ref[1, :1, :PADDED_RANK]).astype(BF16)
    low = unfold(rows_ref[:, 2 * HALF :].astype(F32))[0][:, PADDED_RANK:].astype(BF16)
    scale, first = factors_ref[0], factors_ref[2] > 0.5

    def block(c):
        if c < DOWN_BLOCKS:
            return tn(lifted, x_ref[:, c * 128 : (c + 1) * 128])
        if c < GRAD_BLOCKS:
            at = (c - DOWN_BLOCKS) * 128
            return scale * tn(low, dq[:, at : at + 128])
        return jnp.zeros((PADDED_RANK, 128), F32)

    for c in range(CORE_BLOCKS):
        lower, upper = block(c), block(c + CORE_BLOCKS)
        at = slice(c * PADDED_RANK, (c + 1) * PADDED_RANK)
        mine_ref[at, :] = jnp.where(first, lower, upper).astype(BF16)
        other_ref[at, :] = jnp.where(first, upper, lower).astype(BF16)
    for copy in stores:
        copy.wait()


def spread_kernel(factors_ref, mine_ref, other_ref, down_ref, up_ref):
    first = factors_ref[2] > 0.5
    for c in range(GRAD_BLOCKS):
        at = c % CORE_BLOCKS * PADDED_RANK
        mine = mine_ref[at : at + PADDED_RANK, :].astype(F32)
        other = other_ref[at : at + PADDED_RANK, :].astype(F32)
        part = jnp.where(first, mine, other) if c < CORE_BLOCKS else jnp.where(first, other, mine)
        if c < DOWN_BLOCKS:
            down_ref[:, c * 128 : (c + 1) * 128] = part
        else:
            at = (c - DOWN_BLOCKS) * 128
            up_ref[:, at : at + 128] = part


VMEM = pl.BlockSpec(memory_space=pltpu.VMEM)
SMEM = pl.BlockSpec(memory_space=pltpu.SMEM)
HBM = pl.BlockSpec(memory_space=pltpu.HBM)


def call(kernel, in_specs, outs, scratch=(), out_specs=None, vmem_mib=40, cost=None):
    return pl.pallas_call(
        kernel,
        out_shape=[jax.ShapeDtypeStruct(shape, dtype) for shape, dtype in outs],
        in_specs=in_specs,
        out_specs=out_specs or [VMEM] * len(outs),
        scratch_shapes=list(scratch),
        compiler_params=pltpu.CompilerParams(vmem_limit_bytes=vmem_mib * 1024 * 1024),
        cost_estimate=cost,
    )


def like(arrays):
    return [
        (pltpu.SMEM if a.dtype == jnp.int32 else pltpu.VMEM)(a.shape, a.dtype) for a in arrays
    ]


def run_prepare(*arrays):
    return call(
        prepare_kernel,
        [HBM] * len(arrays),
        [((SLOTS, 16, SEND_WIDTH), BF16)],
        like(arrays)
        + [
            pltpu.VMEM((ROWS, SEND_WIDTH), BF16),
            pltpu.SemaphoreType.DMA((9 + X_PARTS + 2 * SLOTS,)),
        ],
        [HBM],
        60,
        pl.CostEstimate(flops=COST_FLOPS, bytes_accessed=COST_BYTES, transcendentals=0),
    )(*arrays)[0]


def run_owner(rows, *prompts):
    part = (PLEN, 2 * KEY_VALUE_HEADS * HEAD_SIZE)
    return call(
        owner_kernel,
        [VMEM] * 5,
        [((ROWS, BACK_WIDTH), BF16), (part, F32)] + [(part, BF16)] * 3,
    )(rows, *prompts)


def by_z(part, step):
    pairs = [(x * 4 + z, x * 4 + (z + step) % 4) for x in range(4) for z in range(4)]
    return lax.ppermute(part, "prompt", pairs)


def over_x(blocks):
    groups = [[x * 4 + z for x in range(4)] for z in range(4)]
    shape = blocks.shape
    blocks = blocks.reshape(4, 64, shape[-1])
    moved = lax.all_to_all(blocks, "prompt", 0, 0, axis_index_groups=groups, tiled=True)
    return moved.reshape(shape)


def run_own(rank, route, core, *arrays):
    return call(
        own_kernel,
        [SMEM] * 3 + [HBM] * len(arrays),
        [
            ((ROWS, SEND_WIDTH), BF16),
            ((ROWS, KV_HALF), BF16),
            ((ROWS, KV_HALF), BF16),
            ((ROWS, ROWS), BF16),
            ((3, PADDED_RANK, 128), F32),
        ],
        like(arrays[:2]) + [pltpu.SemaphoreType.DMA((2 + SLOTS,))],
    )(rank, route, core, *in_hbm(arrays))


def in_hbm(arrays):
    return [pltpu.with_memory_space_constraint(a, pltpu.HBM) for a in arrays]


def run_finish(x, wu, *arrays):
    kv_width = KEY_VALUE_HEADS * HEAD_SIZE
    return call(
        finish_kernel,
        [HBM] * 2 + [VMEM] * len(arrays),
        [
            ((1, TOKENS, QUERY_WIDTH), BF16),
            ((1, TOKENS, kv_width), BF16),
            ((1, TOKENS, kv_width), BF16),
            ((CORE_ROWS, 128), BF16),
            ((CORE_ROWS, 128), BF16),
        ],
        like([x, wu])
        + [
            pltpu.VMEM((ROWS, HALF), F32),
            pltpu.VMEM((TOKENS, QUERY_WIDTH), BF16),
            pltpu.VMEM((TOKENS, kv_width), BF16),
            pltpu.VMEM((TOKENS, kv_width), BF16),
            pltpu.SemaphoreType.DMA((5,)),
        ],
        [HBM] * 3 + [VMEM] * 2,
    )(*in_hbm([x, wu]), *arrays)


def run_spread(*arrays):
    return call(
        spread_kernel,
        [VMEM] * len(arrays),
        [((PADDED_RANK, MODEL_WIDTH), F32), ((PADDED_RANK, QUERY_WIDTH), F32)],
    )(*arrays)


def by_core(part):
    return lax.ppermute(part, "comp", [(i, i ^ 1) for i in range(16)])


def layer_groups():
    return [
        [(x * 4 + z_hi) * 16 + zy * 2 + core for x in range(4) for zy in range(8)]
        for z_hi in range(4)
        for core in range(2)
    ]


def sum_all(mine, other, beside):
    rows = CORE_ROWS // 32
    swap = functools.partial(
        lax.all_to_all, axis_name=("prompt", "comp"), split_axis=0, concat_axis=0,
        axis_index_groups=layer_groups(), tiled=True,
    )
    pair = (mine.astype(F32) + by_core(other).astype(F32)).astype(BF16)
    total = jnp.sum(swap(pair.reshape(32, rows, 128)).astype(F32), axis=0)
    for flip in (lambda i: i ^ 1, lambda i: i // 4 * 4 + 3 - i % 4):
        total = total + lax.ppermute(total, "prompt", [(i, flip(i)) for i in range(16)])
    total = total.astype(BF16)
    half = swap(jnp.broadcast_to(total[None], (32, rows, 128))).reshape(CORE_ROWS, 128)
    half, beside = lax.optimization_barrier((half, beside))
    return half, by_core(half), beside


def per_device(
    normed_hidden_input,
    frozen_query_base,
    attention_output_grad,
    completion_keys,
    completion_values,
    owner_prompt_keys,
    owner_prompt_values,
    adapter_down_weight,
    adapter_up_weight,
    adapter_rank,
    route,
    lengths,
):
    hidden = normed_hidden_input[0]
    keys, values = completion_keys[0], completion_values[0]
    prompt = jnp.concatenate([owner_prompt_keys[0], owner_prompt_values[0]], axis=1)
    prompts = [prompt] + [by_z(prompt, -k) for k in (1, 2, 3)]
    z = lax.axis_index("prompt") % 4
    route = route // 4 * 4 + (route - z) % 4
    send = run_prepare(
        adapter_rank, route, lengths, hidden, frozen_query_base[0], attention_output_grad[0],
        keys, values, adapter_down_weight.T, adapter_up_weight,
    )
    send, prompts[2] = lax.optimization_barrier((send, prompts[2]))
    arrived = over_x(send)
    back, total, *parts = run_owner(arrived.reshape(ROWS, SEND_WIDTH), *prompts)
    back = over_x(back.reshape(SLOTS, 16, BACK_WIDTH))
    back, far = lax.optimization_barrier((back, by_z(parts[1], 2)))
    core = (lax.axis_index("comp") % 2).astype(jnp.int32)[None]
    own = run_own(adapter_rank, route, core, keys, values, send)
    dq, dsk, dsv, mine, other = run_finish(
        hidden, adapter_up_weight, *own, back.reshape(ROWS, BACK_WIDTH)
    )
    near = [by_z(parts[0], 1), by_z(parts[2], 3)]
    half, other_half, near = sum_all(mine, other, near)
    for part in [far] + near:
        total = total + part.astype(F32)
    width = KEY_VALUE_HEADS * HEAD_SIZE
    dk, dv = total[:, :width].astype(BF16), total[:, width:].astype(BF16)
    down, up = run_spread(own[-1], half, other_half)
    return dq, dsk, dsv, dk[None], dv[None], down.T, up


def solution(mesh):
    split = P("comp", "prompt", None)
    return jax.shard_map(
        per_device,
        mesh=mesh,
        in_specs=(split,) * 7 + (P(),) * 3 + (split,) * 2,
        out_specs=(split,) * 5 + (P(),) * 2,
        check_vma=False,
    )
```

```python
import functools
import math

import jax
import jax.numpy as jnp
from jax import lax
from jax.experimental import pallas as pl
from jax.experimental.pallas import tpu as pltpu
from jax.sharding import PartitionSpec as P

KEY_VALUE_HEADS = 4
GROUP = 5
HEAD_SIZE = 128
PLEN = 128
CL = 8
SLOTS = 16
TOKENS = SLOTS * CL
QUERY_HEADS = KEY_VALUE_HEADS * GROUP
PAIRS = QUERY_HEADS // 2
HALF = PAIRS * HEAD_SIZE
KV_HALF = KEY_VALUE_HEADS * HEAD_SIZE // 2
ROWS = 2 * TOKENS
MODEL_WIDTH = 5120
PADDED_RANK = 64
QUERY_WIDTH = QUERY_HEADS * HEAD_SIZE
SEND_WIDTH = 2 * HALF + 128
X_PARTS = 4
COST_FLOPS = 10**9
COST_BYTES = 60 * 10**6
X_PART = MODEL_WIDTH // X_PARTS
BACK_WIDTH = HALF + 128
DOWN_BLOCKS = MODEL_WIDTH // 128
GRAD_BLOCKS = (MODEL_WIDTH + QUERY_WIDTH) // 128
CORE_BLOCKS = 32
CORE_ROWS = CORE_BLOCKS * PADDED_RANK

INV_SQRT = 1.0 / math.sqrt(HEAD_SIZE)
adapter_strength = 32.0
masked_score = -1e30

BF16 = jnp.bfloat16
F32 = jnp.float32


def dot(a, b, dims):
    return lax.dot_general(a, b, (dims, ((), ())), preferred_element_type=F32)


def nt(a, b):
    return dot(a, b, ((1,), (1,)))


def nn(a, b):
    return dot(a, b, ((1,), (0,)))


def tn(a, b):
    return dot(a, b, ((0,), (0,)))


def fold(wide):
    width = wide.shape[1] // 2
    left = wide[:, :width].reshape(SLOTS, 1, CL, width)
    right = wide[:, width:].reshape(SLOTS, 1, CL, width)
    return jnp.concatenate([left, right], axis=1).reshape(ROWS, width)


def unfold(rows):
    split = rows.reshape(SLOTS, 2, CL, rows.shape[1])
    return split[:, 0].reshape(TOKENS, -1), split[:, 1].reshape(TOKENS, -1)


def own_mask():
    key = lax.broadcasted_iota(jnp.int32, (TOKENS, ROWS), 0)
    row = lax.broadcasted_iota(jnp.int32, (TOKENS, ROWS), 1) % TOKENS
    return (key // CL == row // CL) & (key <= row)


def own_scores(keys, rows):
    return jnp.concatenate(
        [nt(keys[at : at + TOKENS], rows[at : at + TOKENS]) for at in (0, TOKENS)], axis=1
    )


def own_product(scores, rows, product):
    return jnp.concatenate(
        [product(scores[:, at : at + TOKENS], rows[at : at + TOKENS]) for at in (0, TOKENS)], axis=0
    )


def pack_stats(rows):
    value = jnp.concatenate(rows, axis=0)
    first = value.astype(BF16).astype(F32)
    rest = value - first
    second = rest.astype(BF16).astype(F32)
    third = rest - second
    pad = jnp.zeros((128 - 3 * len(rows), ROWS), F32)
    return jnp.concatenate([first, second, third, pad], axis=0).T


def unpack_stats(columns, count):
    parts = columns.astype(F32).T
    return parts[:count] + (parts[count : 2 * count] + parts[2 * count : 3 * count])


def prepare_kernel(
    rank_hbm, route_hbm, length_hbm, x_hbm, base_hbm, g_hbm, sk_hbm, sv_hbm, wd_hbm, wu_hbm,
    send_hbm,
    rank_ref, route_ref, length_ref, x_ref, base_ref, g_ref, sk_ref, sv_ref, wd_ref, wu_ref, rows_ref, sems,
):
    columns = [slice(i * X_PART, (i + 1) * X_PART) for i in range(X_PARTS)]
    pairs = [(rank_hbm, rank_ref), (length_hbm, length_ref), (route_hbm, route_ref)]
    pairs += [(wd_hbm, wd_ref)] + [(x_hbm.at[:, c], x_ref.at[:, c]) for c in columns]
    pairs += [
        (g_hbm, g_ref), (sv_hbm, sv_ref), (sk_hbm, sk_ref), (wu_hbm, wu_ref), (base_hbm, base_ref)
    ]
    loads = [
        pltpu.make_async_copy(source, target, sems.at[i])
        for i, (source, target) in enumerate(pairs)
    ]
    for copy in loads:
        copy.start()

    def sends(start, width, sem):
        return [
            pltpu.make_async_copy(
                rows_ref.at[pl.ds(s * 16, 16), pl.ds(start, width)],
                send_hbm.at[route_ref[0, 0, s], :, pl.ds(start, width)],
                sems.at[sem + s],
            )
            for s in range(SLOTS)
        ]

    for copy in loads[:3]:
        copy.wait()
    rank = rank_ref[0]
    scale = adapter_strength / rank.astype(F32)
    position = lax.broadcasted_iota(jnp.int32, (CL, 128), 0)
    live = jnp.concatenate(
        [jnp.where(position < length_ref[0, 0, s], 1.0, 0.0) for s in range(SLOTS)], axis=0
    )
    mask = own_mask()
    loads[3].wait()
    low = jnp.zeros((TOKENS, PADDED_RANK), F32)
    for i, c in enumerate(columns):
        loads[4 + i].wait()
        low = low + nt(x_ref[:, c], wd_ref[:, c])
    rest = 4 + X_PARTS
    loads[rest].wait()
    for n in range(PAIRS):
        left, right = (g_ref[:, m * 128 : (m + 1) * 128].astype(F32) * live for m in (n, n + PAIRS))
        rows_ref[:, n * 128 : (n + 1) * 128] = fold(
            jnp.concatenate([left, right], axis=1)
        ).astype(BF16)
    early = sends(0, HALF, rest + 5)
    for copy in early:
        copy.start()
    for copy in loads[rest + 1 :]:
        copy.wait()
    values = fold(sv_ref[...].astype(F32)).astype(BF16)
    keys = fold(sk_ref[...].astype(F32)).astype(BF16)
    keep = lax.broadcasted_iota(jnp.int32, (TOKENS, PADDED_RANK), 1) < rank
    low = jnp.where(keep, low, 0.0).astype(BF16)
    query = base_ref[...].astype(F32) + scale * nn(low, wu_ref[...])
    rows_ref[:, HALF : 2 * HALF] = fold(query).astype(BF16)

    def products(b):
        h = b // GROUP
        g = rows_ref[:, b * 128 : (b + 1) * 128]
        q = rows_ref[:, HALF + b * 128 : HALF + (b + 1) * 128]
        return (
            own_scores(keys[:, h * 128 : (h + 1) * 128], q),
            own_scores(values[:, h * 128 : (h + 1) * 128], g),
        )

    lses, deltas = [], []
    ready = products(0)
    for b in range(PAIRS):
        scores, dprob = ready
        if b + 1 < PAIRS:
            ready = products(b + 1)
        scores = jnp.where(mask, scores * INV_SQRT, masked_score)
        top = jnp.max(scores, axis=0, keepdims=True)
        weight = jnp.exp(scores - top)
        total = jnp.sum(weight, axis=0, keepdims=True)
        lses.append(top + jnp.log(total))
        deltas.append(jnp.sum(weight * dprob, axis=0, keepdims=True) / total)
    none = jnp.zeros((TOKENS, PADDED_RANK), F32)
    low_rows = fold(jnp.concatenate([none, low.astype(F32), none, none], axis=1))
    rows_ref[:, 2 * HALF :] = (pack_stats(lses + deltas) + low_rows).astype(BF16)
    late = sends(HALF, SEND_WIDTH - HALF, rest + 5 + SLOTS)
    for copy in late:
        copy.start()
    for copy in early + late:
        copy.wait()


def owner_kernel(
    rows_ref, kv0_ref, kv1_ref, kv3_ref, k2_ref, v2_ref,
    back_ref, part0_hbm, part1_hbm, part3_hbm, dk2_hbm, dv2_hbm,
    part0_ref, part1_ref, part3_ref, dk2_ref, dv2_ref, sems,
):
    width = KEY_VALUE_HEADS * HEAD_SIZE

    def halves(ref):
        return ref.at[:, :width], ref.at[:, width:]

    kv_refs = (halves(kv0_ref), halves(kv1_ref), (k2_ref, v2_ref), halves(kv3_ref))
    part_refs = (halves(part0_ref), halves(part1_ref), (dk2_ref, dv2_ref), halves(part3_ref))
    places = [(x * 4 + k) * 16 for k in range(4) for x in range(4)]
    lower = (lax.broadcasted_iota(jnp.int32, (ROWS, HEAD_SIZE), 0) // CL % 2 == 0).astype(F32)
    lower, upper = lower.astype(BF16), (1.0 - lower).astype(BF16)
    even = lax.broadcasted_iota(jnp.int32, (PLEN, 128), 1) < 64

    def load(at):
        return jnp.concatenate([rows_ref[p : p + 16, at : at + 128] for p in places], axis=0)

    def store(at, value):
        for i, p in enumerate(places):
            back_ref[p : p + 16, at : at + 128] = value[i * 16 : (i + 1) * 16]

    def beside(ref, h):
        return jnp.concatenate([ref[:, m * 128 : (m + 1) * 128] for m in (h, h + 2)], axis=1)

    def apart(rows):
        return jnp.concatenate([rows * lower, rows * upper], axis=1)

    def by_prompt(rows):
        none = jnp.zeros((64, 256), BF16)
        return jnp.concatenate(
            [
                jnp.concatenate([rows[:64], none], axis=1),
                jnp.concatenate([none, rows[64:]], axis=1),
            ],
            axis=0,
        )

    def against(sides, rows):
        parts = []
        for p in range(2):
            two = rows[p * 128 : (p + 1) * 128]
            parts.append(jnp.where(even, nt(sides[2 * p], two), nt(sides[2 * p + 1], two)))
        return jnp.concatenate(parts, axis=1)

    sides = [
        ([beside(refs[0], h) for refs in kv_refs], [beside(refs[1], h) for refs in kv_refs])
        for h in range(2)
    ]
    stats = unpack_stats(load(2 * HALF), 2 * PAIRS)

    def products(b):
        g = apart(load(b * 128))
        q = apart(load(HALF + b * 128))
        keys, values = sides[b // GROUP]
        return q, g, against(keys, q), against(values, g)

    lses, deltas = [], []
    ready = products(0)
    for h in range(2):
        keys = sides[h][0]
        done = []
        for b in range(h * GROUP, (h + 1) * GROUP):
            q, g, scores, dprob = ready
            if b + 1 < PAIRS:
                ready = products(b + 1)
            own_lse, own_delta = stats[b : b + 1], stats[PAIRS + b : PAIRS + b + 1]
            scores = scores * INV_SQRT
            top = jnp.max(scores, axis=0, keepdims=True)
            weight = jnp.exp(scores - top)
            prompt_lse = top + jnp.log(jnp.sum(weight, axis=0, keepdims=True))
            high = jnp.maximum(prompt_lse, own_lse)
            lse = high + jnp.log(jnp.exp(prompt_lse - high) + jnp.exp(own_lse - high))
            probs = weight * jnp.exp(top - lse)
            probs_b = probs.astype(BF16)
            delta = jnp.sum(probs_b.astype(F32) * dprob, axis=0, keepdims=True) + own_delta * jnp.exp(
                own_lse - lse
            )
            dscore = (probs * (dprob - delta)).astype(BF16)
            picks = []
            for p in range(2):
                both = jnp.concatenate([keys[2 * p], keys[2 * p + 1]], axis=1)
                full = tn(dscore[:, p * 128 : (p + 1) * 128], both) * INV_SQRT
                for k in range(2):
                    rows = full[k * 64 : (k + 1) * 64, k * 256 : (k + 1) * 256]
                    rows = rows.reshape(4, 2, CL, 256)
                    rows = jnp.concatenate(
                        [rows[:, :1, :, :HEAD_SIZE], rows[:, 1:, :, HEAD_SIZE:]], axis=1
                    )
                    picks.append(rows.reshape(64, HEAD_SIZE))
            store(b * 128, jnp.concatenate(picks, axis=0).astype(BF16))
            done.append((dscore, q, probs_b, g))
            lses.append(lse)
            deltas.append(delta)
        for p in range(2):
            at = slice(p * 128, (p + 1) * 128)
            for kind, first, scale in ((0, 0, INV_SQRT), (1, 2, 1.0)):
                left = jnp.concatenate([d[first][:, at] for d in done], axis=1)
                right = jnp.concatenate([by_prompt(d[first + 1][at]) for d in done], axis=0)
                grad = nn(left, right) * scale
                for k in range(2):
                    ref = part_refs[2 * p + k][kind]
                    for i, m in enumerate((h, h + 2)):
                        column = k * 256 + i * 128
                        ref[:, m * 128 : (m + 1) * 128] = grad[:, column : column + 128].astype(
                            ref.dtype
                        )
    outs = [
        (dk2_ref, dk2_hbm), (dv2_ref, dv2_hbm), (part1_ref, part1_hbm), (part3_ref, part3_hbm),
        (part0_ref, part0_hbm),
    ]
    copies = [
        pltpu.make_async_copy(source, target, sems.at[i])
        for i, (source, target) in enumerate(outs)
    ]
    for copy in copies:
        copy.start()
    store(HALF, pack_stats(lses + deltas).astype(BF16))
    for copy in copies:
        copy.wait()


def own_kernel(
    rank_ref, route_ref, core_ref, sk_hbm, sv_hbm, send_hbm,
    rows_ref, keys_ref, values_ref, order_ref, factors_ref,
    sk_ref, sv_ref, sems,
):
    pairs = [(sk_hbm, sk_ref), (sv_hbm, sv_ref)]
    pairs += [
        (send_hbm.at[route_ref[0, 0, s]], rows_ref.at[pl.ds(s * 16, 16)]) for s in range(SLOTS)
    ]
    loads = [
        pltpu.make_async_copy(source, target, sems.at[i])
        for i, (source, target) in enumerate(pairs)
    ]
    for copy in loads:
        copy.start()
    rank = rank_ref[0]
    scale = adapter_strength / rank.astype(F32)
    block = (PADDED_RANK, 128)
    keep = lax.broadcasted_iota(jnp.int32, block, 1) < rank
    factors_ref[0] = jnp.full(block, scale, F32)
    factors_ref[1] = jnp.where(keep, scale, 0.0)
    factors_ref[2] = jnp.full(block, 1.0, F32) * (core_ref[0] == 0).astype(F32)
    lane = lax.broadcasted_iota(jnp.int32, (16, ROWS), 1)
    place = lax.broadcasted_iota(jnp.int32, (16, ROWS), 0)
    for s in range(SLOTS):
        at = (lane == route_ref[0, 0, s] * 16 + place).astype(F32)
        order_ref[s * 16 : (s + 1) * 16, :] = at.astype(BF16)
    for copy in loads:
        copy.wait()
    keys_ref[...] = fold(sk_ref[...].astype(F32)).astype(BF16)
    values_ref[...] = fold(sv_ref[...].astype(F32)).astype(BF16)


def finish_kernel(
    x_hbm, wu_hbm, rows_ref, keys_ref, values_ref, order_ref, factors_ref, back_ref,
    dq_hbm, dsk_hbm, dsv_hbm, mine_ref, other_ref,
    x_ref, wu_ref, dq_rows_ref, dq_ref, dsk_ref, dsv_ref, sems,
):
    loads = [
        pltpu.make_async_copy(wu_hbm, wu_ref, sems.at[3]),
        pltpu.make_async_copy(x_hbm, x_ref, sems.at[4]),
    ]
    for copy in loads:
        copy.start()
    order = order_ref[...]
    mask = own_mask()

    def products(b):
        h = b // GROUP
        g = rows_ref[:, b * 128 : (b + 1) * 128]
        q = rows_ref[:, HALF + b * 128 : HALF + (b + 1) * 128]
        return (
            q, g,
            own_scores(keys_ref[:, h * 128 : (h + 1) * 128], q),
            own_scores(values_ref[:, h * 128 : (h + 1) * 128], g),
        )

    ready = products(0)
    stats = unpack_stats(nn(order, back_ref[:, HALF:]), 2 * PAIRS)
    dq_rows_ref[...] = nn(order, back_ref[:, :HALF])
    for h in range(2):
        k2 = keys_ref[:, h * 128 : (h + 1) * 128]
        dsk = jnp.zeros((ROWS, HEAD_SIZE), F32)
        dsv = jnp.zeros((ROWS, HEAD_SIZE), F32)
        for b in range(h * GROUP, (h + 1) * GROUP):
            q, g, scores, dprob = ready
            if b + 1 < PAIRS:
                ready = products(b + 1)
            lse, delta = stats[b : b + 1], stats[PAIRS + b : PAIRS + b + 1]
            probs = jnp.exp(jnp.where(mask, scores * INV_SQRT - lse, masked_score))
            dscore = (probs * (dprob - delta)).astype(BF16)
            dq = dq_rows_ref[:, b * 128 : (b + 1) * 128] + own_product(dscore, k2, tn) * INV_SQRT
            for at, part in zip((b, b + PAIRS), unfold(dq)):
                dq_ref[:, at * 128 : (at + 1) * 128] = part.astype(BF16)
            dsv = dsv + own_product(probs.astype(BF16), g, nn)
            dsk = dsk + own_product(dscore, q, nn)
        for at, k_part, v_part in zip((h, h + 2), unfold(dsk * INV_SQRT), unfold(dsv)):
            dsk_ref[:, at * 128 : (at + 1) * 128] = k_part.astype(BF16)
            dsv_ref[:, at * 128 : (at + 1) * 128] = v_part.astype(BF16)
    stores = [
        pltpu.make_async_copy(source, target.at[0], sems.at[i])
        for i, (source, target) in enumerate(
            [(dq_ref, dq_hbm), (dsk_ref, dsk_hbm), (dsv_ref, dsv_hbm)]
        )
    ]
    for copy in stores:
        copy.start()
    dq = dq_ref[...]
    for copy in loads:
        copy.wait()
    lifted = (nt(dq, wu_ref[...]) * factors_ref[1, :1, :PADDED_RANK]).astype(BF16)
    low = unfold(rows_ref[:, 2 * HALF :].astype(F32))[0][:, PADDED_RANK:].astype(BF16)
    scale, first = factors_ref[0], factors_ref[2] > 0.5

    def block(c):
        if c < DOWN_BLOCKS:
            return tn(lifted, x_ref[:, c * 128 : (c + 1) * 128])
        if c < GRAD_BLOCKS:
            at = (c - DOWN_BLOCKS) * 128
            return scale * tn(low, dq[:, at : at + 128])
        return jnp.zeros((PADDED_RANK, 128), F32)

    for c in range(CORE_BLOCKS):
        lower, upper = block(c), block(c + CORE_BLOCKS)
        at = slice(c * PADDED_RANK, (c + 1) * PADDED_RANK)
        mine_ref[at, :] = jnp.where(first, lower, upper).astype(BF16)
        other_ref[at, :] = jnp.where(first, upper, lower).astype(BF16)
    for copy in stores:
        copy.wait()


def spread_kernel(factors_ref, mine_ref, other_ref, down_ref, up_ref):
    first = factors_ref[2] > 0.5
    for c in range(GRAD_BLOCKS):
        at = c % CORE_BLOCKS * PADDED_RANK
        mine = mine_ref[at : at + PADDED_RANK, :].astype(F32)
        other = other_ref[at : at + PADDED_RANK, :].astype(F32)
        part = jnp.where(first, mine, other) if c < CORE_BLOCKS else jnp.where(first, other, mine)
        if c < DOWN_BLOCKS:
            down_ref[:, c * 128 : (c + 1) * 128] = part
        else:
            at = (c - DOWN_BLOCKS) * 128
            up_ref[:, at : at + 128] = part


VMEM = pl.BlockSpec(memory_space=pltpu.VMEM)
SMEM = pl.BlockSpec(memory_space=pltpu.SMEM)
HBM = pl.BlockSpec(memory_space=pltpu.HBM)


def call(kernel, in_specs, outs, scratch=(), out_specs=None, vmem_mib=40, cost=None):
    return pl.pallas_call(
        kernel,
        out_shape=[
            jax.ShapeDtypeStruct(*out) if len(out) == 2 else out[0](*out[1:]) for out in outs
        ],
        in_specs=in_specs,
        out_specs=out_specs or [VMEM] * len(outs),
        scratch_shapes=list(scratch),
        compiler_params=pltpu.CompilerParams(vmem_limit_bytes=vmem_mib * 1024 * 1024),
        cost_estimate=cost,
    )


def like(arrays):
    return [
        (pltpu.SMEM if a.dtype == jnp.int32 else pltpu.VMEM)(a.shape, a.dtype) for a in arrays
    ]


def run_prepare(*arrays):
    return call(
        prepare_kernel,
        [HBM] * len(arrays),
        [((SLOTS, 16, SEND_WIDTH), BF16)],
        like(arrays)
        + [
            pltpu.VMEM((ROWS, SEND_WIDTH), BF16),
            pltpu.SemaphoreType.DMA((9 + X_PARTS + 2 * SLOTS,)),
        ],
        [HBM],
        60,
        pl.CostEstimate(flops=COST_FLOPS, bytes_accessed=COST_BYTES, transcendentals=0),
    )(*arrays)[0]


def run_owner(rows, *prompts):
    half = (PLEN, KEY_VALUE_HEADS * HEAD_SIZE)
    part = (PLEN, 2 * KEY_VALUE_HEADS * HEAD_SIZE)
    parts = [(part, F32)] + [(part, BF16)] * 2 + [(half, BF16)] * 2
    return call(
        owner_kernel,
        [VMEM] * 6,
        [((ROWS, BACK_WIDTH), BF16)] + [(pltpu.HBM, *p) for p in parts],
        [pltpu.VMEM(*p) for p in parts] + [pltpu.SemaphoreType.DMA((5,))],
        [VMEM] + [HBM] * 5,
    )(rows, *prompts)


def by_z(part, step):
    pairs = [(x * 4 + z, x * 4 + (z + step) % 4) for x in range(4) for z in range(4)]
    return lax.ppermute(part, "prompt", pairs)


def over_x(blocks):
    groups = [[x * 4 + z for x in range(4)] for z in range(4)]
    shape = blocks.shape
    blocks = blocks.reshape(4, 64, shape[-1])
    moved = lax.all_to_all(blocks, "prompt", 0, 0, axis_index_groups=groups, tiled=True)
    return moved.reshape(shape)


def run_own(rank, route, core, *arrays):
    return call(
        own_kernel,
        [SMEM] * 3 + [HBM] * len(arrays),
        [
            ((ROWS, SEND_WIDTH), BF16),
            ((ROWS, KV_HALF), BF16),
            ((ROWS, KV_HALF), BF16),
            ((ROWS, ROWS), BF16),
            ((3, PADDED_RANK, 128), F32),
        ],
        like(arrays[:2]) + [pltpu.SemaphoreType.DMA((2 + SLOTS,))],
    )(rank, route, core, *in_hbm(arrays))


def in_hbm(arrays):
    return [pltpu.with_memory_space_constraint(a, pltpu.HBM) for a in arrays]


def run_finish(x, wu, *arrays):
    kv_width = KEY_VALUE_HEADS * HEAD_SIZE
    return call(
        finish_kernel,
        [HBM] * 2 + [VMEM] * len(arrays),
        [
            ((1, TOKENS, QUERY_WIDTH), BF16),
            ((1, TOKENS, kv_width), BF16),
            ((1, TOKENS, kv_width), BF16),
            ((CORE_ROWS, 128), BF16),
            ((CORE_ROWS, 128), BF16),
        ],
        like([x, wu])
        + [
            pltpu.VMEM((ROWS, HALF), F32),
            pltpu.VMEM((TOKENS, QUERY_WIDTH), BF16),
            pltpu.VMEM((TOKENS, kv_width), BF16),
            pltpu.VMEM((TOKENS, kv_width), BF16),
            pltpu.SemaphoreType.DMA((5,)),
        ],
        [HBM] * 3 + [VMEM] * 2,
    )(*in_hbm([x, wu]), *arrays)


def run_spread(*arrays):
    return call(
        spread_kernel,
        [VMEM] * len(arrays),
        [((PADDED_RANK, MODEL_WIDTH), F32), ((PADDED_RANK, QUERY_WIDTH), F32)],
    )(*arrays)


def by_core(part):
    return lax.ppermute(part, "comp", [(i, i ^ 1) for i in range(16)])


def layer_groups():
    return [
        [(x * 4 + z_hi) * 16 + zy * 2 + core for x in range(4) for zy in range(8)]
        for z_hi in range(4)
        for core in range(2)
    ]


def sum_all(mine, other, beside):
    rows = CORE_ROWS // 32
    swap = functools.partial(
        lax.all_to_all, axis_name=("prompt", "comp"), split_axis=0, concat_axis=0,
        axis_index_groups=layer_groups(), tiled=True,
    )
    pair = (mine.astype(F32) + by_core(other).astype(F32)).astype(BF16)
    total = jnp.sum(swap(pair.reshape(32, rows, 128)).astype(F32), axis=0)
    for flip in (lambda i: i ^ 1, lambda i: i // 4 * 4 + 3 - i % 4):
        total = total + lax.ppermute(total, "prompt", [(i, flip(i)) for i in range(16)])
    total = total.astype(BF16)
    half = swap(jnp.broadcast_to(total[None], (32, rows, 128))).reshape(CORE_ROWS, 128)
    half, beside = lax.optimization_barrier((half, beside))
    return half, by_core(half), beside


def per_device(
    normed_hidden_input,
    frozen_query_base,
    attention_output_grad,
    completion_keys,
    completion_values,
    owner_prompt_keys,
    owner_prompt_values,
    adapter_down_weight,
    adapter_up_weight,
    adapter_rank,
    route,
    lengths,
):
    hidden = normed_hidden_input[0]
    keys, values = completion_keys[0], completion_values[0]
    prompt = jnp.concatenate([owner_prompt_keys[0], owner_prompt_values[0]], axis=1)
    after, before = by_z(prompt, -1), by_z(prompt, 1)
    z = lax.axis_index("prompt") % 4
    route = route // 4 * 4 + (route - z) % 4
    send = run_prepare(
        adapter_rank, route, lengths, hidden, frozen_query_base[0], attention_output_grad[0],
        keys, values, adapter_down_weight.T, adapter_up_weight,
    )
    send, after, before = lax.optimization_barrier((send, after, before))
    arrived = over_x(send)
    width = KEY_VALUE_HEADS * HEAD_SIZE
    far = by_z(after[:, :width], -1), by_z(before[:, width:], 1)
    back, total, to_after, to_before, *far = run_owner(
        arrived.reshape(ROWS, SEND_WIDTH), prompt, after, before, *far
    )
    back = over_x(back.reshape(SLOTS, 16, BACK_WIDTH))
    back, *far = lax.optimization_barrier((back, by_z(far[0], 1), by_z(far[1], -1)))
    to_after = jnp.concatenate([to_after[:, :width] + far[0], to_after[:, width:]], axis=1)
    to_before = jnp.concatenate([to_before[:, :width], to_before[:, width:] + far[1]], axis=1)
    core = (lax.axis_index("comp") % 2).astype(jnp.int32)[None]
    own = run_own(adapter_rank, route, core, keys, values, send)
    dq, dsk, dsv, mine, other = run_finish(
        hidden, adapter_up_weight, *own, back.reshape(ROWS, BACK_WIDTH)
    )
    near = [by_z(to_after, 1), by_z(to_before, -1)]
    half, other_half, near = sum_all(mine, other, near)
    for part in near:
        total = total + part.astype(F32)
    dk, dv = total[:, :width].astype(BF16), total[:, width:].astype(BF16)
    down, up = run_spread(own[-1], half, other_half)
    return dq, dsk, dsv, dk[None], dv[None], down.T, up


def solution(mesh):
    split = P("comp", "prompt", None)
    return jax.shard_map(
        per_device,
        mesh=mesh,
        in_specs=(split,) * 7 + (P(),) * 3 + (split,) * 2,
        out_specs=(split,) * 5 + (P(),) * 2,
        check_vma=False,
    )
```

```python
import functools
import math

import jax
import jax.numpy as jnp
from jax import lax
from jax.experimental import pallas as pl
from jax.experimental.pallas import tpu as pltpu
from jax.sharding import PartitionSpec as P

KEY_VALUE_HEADS = 4
GROUP = 5
HEAD_SIZE = 128
PLEN = 128
CL = 8
SLOTS = 16
TOKENS = SLOTS * CL
QUERY_HEADS = KEY_VALUE_HEADS * GROUP
PAIRS = QUERY_HEADS // 2
HALF = PAIRS * HEAD_SIZE
KV_HALF = KEY_VALUE_HEADS * HEAD_SIZE // 2
ROWS = 2 * TOKENS
MODEL_WIDTH = 5120
PADDED_RANK = 64
QUERY_WIDTH = QUERY_HEADS * HEAD_SIZE
SEND_WIDTH = 2 * HALF + 128
X_PARTS = 4
COST_FLOPS = 10**9
COST_BYTES = 60 * 10**6
X_PART = MODEL_WIDTH // X_PARTS
BACK_WIDTH = HALF + 128
DOWN_BLOCKS = MODEL_WIDTH // 128
GRAD_BLOCKS = (MODEL_WIDTH + QUERY_WIDTH) // 128
CORE_BLOCKS = 32
CORE_ROWS = CORE_BLOCKS * PADDED_RANK

INV_SQRT = 1.0 / math.sqrt(HEAD_SIZE)
adapter_strength = 32.0
masked_score = -1e30

BF16 = jnp.bfloat16
F32 = jnp.float32


def dot(a, b, dims):
    return lax.dot_general(a, b, (dims, ((), ())), preferred_element_type=F32)


def nt(a, b):
    return dot(a, b, ((1,), (1,)))


def nn(a, b):
    return dot(a, b, ((1,), (0,)))


def tn(a, b):
    return dot(a, b, ((0,), (0,)))


def fold(wide):
    width = wide.shape[1] // 2
    left = wide[:, :width].reshape(SLOTS, 1, CL, width)
    right = wide[:, width:].reshape(SLOTS, 1, CL, width)
    return jnp.concatenate([left, right], axis=1).reshape(ROWS, width)


def unfold(rows):
    split = rows.reshape(SLOTS, 2, CL, rows.shape[1])
    return split[:, 0].reshape(TOKENS, -1), split[:, 1].reshape(TOKENS, -1)


def own_mask():
    key = lax.broadcasted_iota(jnp.int32, (TOKENS, ROWS), 0)
    row = lax.broadcasted_iota(jnp.int32, (TOKENS, ROWS), 1) % TOKENS
    return (key // CL == row // CL) & (key <= row)


def own_scores(keys, rows):
    return jnp.concatenate(
        [nt(keys[at : at + TOKENS], rows[at : at + TOKENS]) for at in (0, TOKENS)], axis=1
    )


def own_product(scores, rows, product):
    return jnp.concatenate(
        [product(scores[:, at : at + TOKENS], rows[at : at + TOKENS]) for at in (0, TOKENS)], axis=0
    )


def pack_stats(rows):
    value = jnp.concatenate(rows, axis=0)
    first = value.astype(BF16).astype(F32)
    rest = value - first
    second = rest.astype(BF16).astype(F32)
    third = rest - second
    pad = jnp.zeros((128 - 3 * len(rows), ROWS), F32)
    return jnp.concatenate([first, second, third, pad], axis=0).T


def unpack_stats(columns, count):
    parts = columns.astype(F32).T
    return parts[:count] + (parts[count : 2 * count] + parts[2 * count : 3 * count])


def prepare_kernel(
    rank_hbm, route_hbm, length_hbm, x_hbm, base_hbm, g_hbm, sk_hbm, sv_hbm, wd_hbm, wu_hbm,
    send_hbm,
    rank_ref, route_ref, length_ref, x_ref, base_ref, g_ref, sk_ref, sv_ref, wd_ref, wu_ref, rows_ref, sems,
):
    columns = [slice(i * X_PART, (i + 1) * X_PART) for i in range(X_PARTS)]
    pairs = [(rank_hbm, rank_ref), (length_hbm, length_ref), (route_hbm, route_ref)]
    pairs += [(wd_hbm, wd_ref)] + [(x_hbm.at[:, c], x_ref.at[:, c]) for c in columns]
    pairs += [
        (g_hbm, g_ref), (sv_hbm, sv_ref), (sk_hbm, sk_ref), (wu_hbm, wu_ref), (base_hbm, base_ref)
    ]
    loads = [
        pltpu.make_async_copy(source, target, sems.at[i])
        for i, (source, target) in enumerate(pairs)
    ]
    for copy in loads:
        copy.start()

    def sends(start, width, sem):
        return [
            pltpu.make_async_copy(
                rows_ref.at[pl.ds(s * 16, 16), pl.ds(start, width)],
                send_hbm.at[route_ref[0, 0, s], :, pl.ds(start, width)],
                sems.at[sem + s],
            )
            for s in range(SLOTS)
        ]

    for copy in loads[:3]:
        copy.wait()
    rank = rank_ref[0]
    scale = adapter_strength / rank.astype(F32)
    position = lax.broadcasted_iota(jnp.int32, (CL, 128), 0)
    live = jnp.concatenate(
        [jnp.where(position < length_ref[0, 0, s], 1.0, 0.0) for s in range(SLOTS)], axis=0
    )
    mask = own_mask()
    loads[3].wait()
    low = jnp.zeros((TOKENS, PADDED_RANK), F32)
    for i, c in enumerate(columns):
        loads[4 + i].wait()
        low = low + nt(x_ref[:, c], wd_ref[:, c])
    rest = 4 + X_PARTS
    loads[rest].wait()
    for n in range(PAIRS):
        left, right = (g_ref[:, m * 128 : (m + 1) * 128].astype(F32) * live for m in (n, n + PAIRS))
        rows_ref[:, n * 128 : (n + 1) * 128] = fold(
            jnp.concatenate([left, right], axis=1)
        ).astype(BF16)
    early = sends(0, HALF, rest + 5)
    for copy in early:
        copy.start()
    for copy in loads[rest + 1 :]:
        copy.wait()
    values = fold(sv_ref[...].astype(F32)).astype(BF16)
    keys = fold(sk_ref[...].astype(F32)).astype(BF16)
    keep = lax.broadcasted_iota(jnp.int32, (TOKENS, PADDED_RANK), 1) < rank
    low = jnp.where(keep, low, 0.0).astype(BF16)
    query = base_ref[...].astype(F32) + scale * nn(low, wu_ref[...])
    rows_ref[:, HALF : 2 * HALF] = fold(query).astype(BF16)

    def products(b):
        h = b // GROUP
        g = rows_ref[:, b * 128 : (b + 1) * 128]
        q = rows_ref[:, HALF + b * 128 : HALF + (b + 1) * 128]
        return (
            own_scores(keys[:, h * 128 : (h + 1) * 128], q),
            own_scores(values[:, h * 128 : (h + 1) * 128], g),
        )

    lses, deltas = [], []
    ready = products(0)
    for b in range(PAIRS):
        scores, dprob = ready
        if b + 1 < PAIRS:
            ready = products(b + 1)
        scores = jnp.where(mask, scores * INV_SQRT, masked_score)
        top = jnp.max(scores, axis=0, keepdims=True)
        weight = jnp.exp(scores - top)
        total = jnp.sum(weight, axis=0, keepdims=True)
        lses.append(top + jnp.log(total))
        deltas.append(jnp.sum(weight * dprob, axis=0, keepdims=True) / total)
    none = jnp.zeros((TOKENS, PADDED_RANK), F32)
    low_rows = fold(jnp.concatenate([none, low.astype(F32), none, none], axis=1))
    rows_ref[:, 2 * HALF :] = (pack_stats(lses + deltas) + low_rows).astype(BF16)
    late = sends(HALF, SEND_WIDTH - HALF, rest + 5 + SLOTS)
    for copy in late:
        copy.start()
    for copy in early + late:
        copy.wait()


def owner_kernel(
    rows_ref, k0_ref, v0_ref, k1_ref, v1_ref, k2_ref, v2_ref, k3_ref, v3_ref,
    back_ref, part0_hbm, part1_hbm, part3_hbm, dk2_hbm, dv2_hbm,
    part0_ref, part1_ref, part3_ref, dk2_ref, dv2_ref, sems,
):
    width = KEY_VALUE_HEADS * HEAD_SIZE

    def halves(ref):
        return ref.at[:, :width], ref.at[:, width:]

    kv_refs = ((k0_ref, v0_ref), (k1_ref, v1_ref), (k2_ref, v2_ref), (k3_ref, v3_ref))
    part_refs = (halves(part0_ref), halves(part1_ref), (dk2_ref, dv2_ref), halves(part3_ref))
    places = [(x * 4 + k) * 16 for k in range(4) for x in range(4)]
    lower = (lax.broadcasted_iota(jnp.int32, (ROWS, HEAD_SIZE), 0) // CL % 2 == 0).astype(F32)
    lower, upper = lower.astype(BF16), (1.0 - lower).astype(BF16)
    even = lax.broadcasted_iota(jnp.int32, (PLEN, 128), 1) < 64

    def load(at):
        return jnp.concatenate([rows_ref[p : p + 16, at : at + 128] for p in places], axis=0)

    def store(at, value):
        for i, p in enumerate(places):
            back_ref[p : p + 16, at : at + 128] = value[i * 16 : (i + 1) * 16]

    def beside(ref, h):
        return jnp.concatenate([ref[:, m * 128 : (m + 1) * 128] for m in (h, h + 2)], axis=1)

    def apart(rows):
        return jnp.concatenate([rows * lower, rows * upper], axis=1)

    def by_prompt(rows):
        none = jnp.zeros((64, 256), BF16)
        return jnp.concatenate(
            [
                jnp.concatenate([rows[:64], none], axis=1),
                jnp.concatenate([none, rows[64:]], axis=1),
            ],
            axis=0,
        )

    def against(sides, rows):
        parts = []
        for p in range(2):
            two = rows[p * 128 : (p + 1) * 128]
            parts.append(jnp.where(even, nt(sides[2 * p], two), nt(sides[2 * p + 1], two)))
        return jnp.concatenate(parts, axis=1)

    sides = [
        ([beside(refs[0], h) for refs in kv_refs], [beside(refs[1], h) for refs in kv_refs])
        for h in range(2)
    ]
    stats = unpack_stats(load(2 * HALF), 2 * PAIRS)

    def products(b):
        g = apart(load(b * 128))
        q = apart(load(HALF + b * 128))
        keys, values = sides[b // GROUP]
        return q, g, against(keys, q), against(values, g)

    lses, deltas = [], []
    ready = products(0)
    for h in range(2):
        keys = sides[h][0]
        done = []
        for b in range(h * GROUP, (h + 1) * GROUP):
            q, g, scores, dprob = ready
            if b + 1 < PAIRS:
                ready = products(b + 1)
            own_lse, own_delta = stats[b : b + 1], stats[PAIRS + b : PAIRS + b + 1]
            scores = scores * INV_SQRT
            top = jnp.max(scores, axis=0, keepdims=True)
            weight = jnp.exp(scores - top)
            prompt_lse = top + jnp.log(jnp.sum(weight, axis=0, keepdims=True))
            high = jnp.maximum(prompt_lse, own_lse)
            lse = high + jnp.log(jnp.exp(prompt_lse - high) + jnp.exp(own_lse - high))
            probs = weight * jnp.exp(top - lse)
            probs_b = probs.astype(BF16)
            delta = jnp.sum(probs_b.astype(F32) * dprob, axis=0, keepdims=True) + own_delta * jnp.exp(
                own_lse - lse
            )
            dscore = (probs * (dprob - delta)).astype(BF16)
            picks = []
            for p in range(2):
                both = jnp.concatenate([keys[2 * p], keys[2 * p + 1]], axis=1)
                full = tn(dscore[:, p * 128 : (p + 1) * 128], both) * INV_SQRT
                for k in range(2):
                    rows = full[k * 64 : (k + 1) * 64, k * 256 : (k + 1) * 256]
                    rows = rows.reshape(4, 2, CL, 256)
                    rows = jnp.concatenate(
                        [rows[:, :1, :, :HEAD_SIZE], rows[:, 1:, :, HEAD_SIZE:]], axis=1
                    )
                    picks.append(rows.reshape(64, HEAD_SIZE))
            store(b * 128, jnp.concatenate(picks, axis=0).astype(BF16))
            done.append((dscore, q, probs_b, g))
            lses.append(lse)
            deltas.append(delta)
        for p in range(2):
            at = slice(p * 128, (p + 1) * 128)
            for kind, first, scale in ((0, 0, INV_SQRT), (1, 2, 1.0)):
                left = jnp.concatenate([d[first][:, at] for d in done], axis=1)
                right = jnp.concatenate([by_prompt(d[first + 1][at]) for d in done], axis=0)
                grad = nn(left, right) * scale
                for k in range(2):
                    ref = part_refs[2 * p + k][kind]
                    for i, m in enumerate((h, h + 2)):
                        column = k * 256 + i * 128
                        ref[:, m * 128 : (m + 1) * 128] = grad[:, column : column + 128].astype(
                            ref.dtype
                        )
    outs = [
        (dk2_ref, dk2_hbm), (dv2_ref, dv2_hbm), (part1_ref, part1_hbm), (part3_ref, part3_hbm),
        (part0_ref, part0_hbm),
    ]
    copies = [
        pltpu.make_async_copy(source, target, sems.at[i])
        for i, (source, target) in enumerate(outs)
    ]
    for copy in copies:
        copy.start()
    store(HALF, pack_stats(lses + deltas).astype(BF16))
    for copy in copies:
        copy.wait()


def own_kernel(
    rank_ref, route_ref, core_ref, sk_hbm, sv_hbm, send_hbm,
    rows_ref, keys_ref, values_ref, order_ref, factors_ref,
    sk_ref, sv_ref, sems,
):
    pairs = [(sk_hbm, sk_ref), (sv_hbm, sv_ref)]
    pairs += [
        (send_hbm.at[route_ref[0, 0, s]], rows_ref.at[pl.ds(s * 16, 16)]) for s in range(SLOTS)
    ]
    loads = [
        pltpu.make_async_copy(source, target, sems.at[i])
        for i, (source, target) in enumerate(pairs)
    ]
    for copy in loads:
        copy.start()
    rank = rank_ref[0]
    scale = adapter_strength / rank.astype(F32)
    block = (PADDED_RANK, 128)
    keep = lax.broadcasted_iota(jnp.int32, block, 1) < rank
    factors_ref[0] = jnp.full(block, scale, F32)
    factors_ref[1] = jnp.where(keep, scale, 0.0)
    factors_ref[2] = jnp.full(block, 1.0, F32) * (core_ref[0] == 0).astype(F32)
    lane = lax.broadcasted_iota(jnp.int32, (16, ROWS), 1)
    place = lax.broadcasted_iota(jnp.int32, (16, ROWS), 0)
    for s in range(SLOTS):
        at = (lane == route_ref[0, 0, s] * 16 + place).astype(F32)
        order_ref[s * 16 : (s + 1) * 16, :] = at.astype(BF16)
    for copy in loads:
        copy.wait()
    keys_ref[...] = fold(sk_ref[...].astype(F32)).astype(BF16)
    values_ref[...] = fold(sv_ref[...].astype(F32)).astype(BF16)


def finish_kernel(
    x_hbm, wu_hbm, rows_ref, keys_ref, values_ref, order_ref, factors_ref, back_ref,
    dq_hbm, dsk_hbm, dsv_hbm, mine_ref, other_ref,
    x_ref, wu_ref, dq_rows_ref, dq_ref, dsk_ref, dsv_ref, sems,
):
    loads = [
        pltpu.make_async_copy(wu_hbm, wu_ref, sems.at[3]),
        pltpu.make_async_copy(x_hbm, x_ref, sems.at[4]),
    ]
    for copy in loads:
        copy.start()
    order = order_ref[...]
    mask = own_mask()

    def products(b):
        h = b // GROUP
        g = rows_ref[:, b * 128 : (b + 1) * 128]
        q = rows_ref[:, HALF + b * 128 : HALF + (b + 1) * 128]
        return (
            q, g,
            own_scores(keys_ref[:, h * 128 : (h + 1) * 128], q),
            own_scores(values_ref[:, h * 128 : (h + 1) * 128], g),
        )

    ready = products(0)
    stats = unpack_stats(nn(order, back_ref[:, HALF:]), 2 * PAIRS)
    dq_rows_ref[...] = nn(order, back_ref[:, :HALF])
    for h in range(2):
        k2 = keys_ref[:, h * 128 : (h + 1) * 128]
        dsk = jnp.zeros((ROWS, HEAD_SIZE), F32)
        dsv = jnp.zeros((ROWS, HEAD_SIZE), F32)
        for b in range(h * GROUP, (h + 1) * GROUP):
            q, g, scores, dprob = ready
            if b + 1 < PAIRS:
                ready = products(b + 1)
            lse, delta = stats[b : b + 1], stats[PAIRS + b : PAIRS + b + 1]
            probs = jnp.exp(jnp.where(mask, scores * INV_SQRT - lse, masked_score))
            dscore = (probs * (dprob - delta)).astype(BF16)
            dq = dq_rows_ref[:, b * 128 : (b + 1) * 128] + own_product(dscore, k2, tn) * INV_SQRT
            for at, part in zip((b, b + PAIRS), unfold(dq)):
                dq_ref[:, at * 128 : (at + 1) * 128] = part.astype(BF16)
            dsv = dsv + own_product(probs.astype(BF16), g, nn)
            dsk = dsk + own_product(dscore, q, nn)
        for at, k_part, v_part in zip((h, h + 2), unfold(dsk * INV_SQRT), unfold(dsv)):
            dsk_ref[:, at * 128 : (at + 1) * 128] = k_part.astype(BF16)
            dsv_ref[:, at * 128 : (at + 1) * 128] = v_part.astype(BF16)
    stores = [
        pltpu.make_async_copy(source, target.at[0], sems.at[i])
        for i, (source, target) in enumerate(
            [(dq_ref, dq_hbm), (dsk_ref, dsk_hbm), (dsv_ref, dsv_hbm)]
        )
    ]
    for copy in stores:
        copy.start()
    dq = dq_ref[...]
    for copy in loads:
        copy.wait()
    lifted = (nt(dq, wu_ref[...]) * factors_ref[1, :1, :PADDED_RANK]).astype(BF16)
    low = unfold(rows_ref[:, 2 * HALF :].astype(F32))[0][:, PADDED_RANK:].astype(BF16)
    scale, first = factors_ref[0], factors_ref[2] > 0.5

    def block(c):
        if c < DOWN_BLOCKS:
            return tn(lifted, x_ref[:, c * 128 : (c + 1) * 128])
        if c < GRAD_BLOCKS:
            at = (c - DOWN_BLOCKS) * 128
            return scale * tn(low, dq[:, at : at + 128])
        return jnp.zeros((PADDED_RANK, 128), F32)

    for c in range(CORE_BLOCKS):
        lower, upper = block(c), block(c + CORE_BLOCKS)
        at = slice(c * PADDED_RANK, (c + 1) * PADDED_RANK)
        mine_ref[at, :] = jnp.where(first, lower, upper).astype(BF16)
        other_ref[at, :] = jnp.where(first, upper, lower).astype(BF16)
    for copy in stores:
        copy.wait()


def spread_kernel(factors_ref, mine_ref, other_ref, down_ref, up_ref):
    first = factors_ref[2] > 0.5
    for c in range(GRAD_BLOCKS):
        at = c % CORE_BLOCKS * PADDED_RANK
        mine = mine_ref[at : at + PADDED_RANK, :].astype(F32)
        other = other_ref[at : at + PADDED_RANK, :].astype(F32)
        part = jnp.where(first, mine, other) if c < CORE_BLOCKS else jnp.where(first, other, mine)
        if c < DOWN_BLOCKS:
            down_ref[:, c * 128 : (c + 1) * 128] = part
        else:
            at = (c - DOWN_BLOCKS) * 128
            up_ref[:, at : at + 128] = part


VMEM = pl.BlockSpec(memory_space=pltpu.VMEM)
SMEM = pl.BlockSpec(memory_space=pltpu.SMEM)
HBM = pl.BlockSpec(memory_space=pltpu.HBM)


def call(kernel, in_specs, outs, scratch=(), out_specs=None, vmem_mib=40, cost=None):
    return pl.pallas_call(
        kernel,
        out_shape=[
            jax.ShapeDtypeStruct(*out) if len(out) == 2 else out[0](*out[1:]) for out in outs
        ],
        in_specs=in_specs,
        out_specs=out_specs or [VMEM] * len(outs),
        scratch_shapes=list(scratch),
        compiler_params=pltpu.CompilerParams(vmem_limit_bytes=vmem_mib * 1024 * 1024),
        cost_estimate=cost,
    )


def like(arrays):
    return [
        (pltpu.SMEM if a.dtype == jnp.int32 else pltpu.VMEM)(a.shape, a.dtype) for a in arrays
    ]


def run_prepare(*arrays):
    return call(
        prepare_kernel,
        [HBM] * len(arrays),
        [((SLOTS, 16, SEND_WIDTH), BF16)],
        like(arrays)
        + [
            pltpu.VMEM((ROWS, SEND_WIDTH), BF16),
            pltpu.SemaphoreType.DMA((9 + X_PARTS + 2 * SLOTS,)),
        ],
        [HBM],
        60,
        pl.CostEstimate(flops=COST_FLOPS, bytes_accessed=COST_BYTES, transcendentals=0),
    )(*arrays)[0]


def run_owner(rows, *prompts):
    half = (PLEN, KEY_VALUE_HEADS * HEAD_SIZE)
    part = (PLEN, 2 * KEY_VALUE_HEADS * HEAD_SIZE)
    parts = [(part, F32)] + [(part, BF16)] * 2 + [(half, BF16)] * 2
    return call(
        owner_kernel,
        [VMEM] * 9,
        [((ROWS, BACK_WIDTH), BF16)] + [(pltpu.HBM, *p) for p in parts],
        [pltpu.VMEM(*p) for p in parts] + [pltpu.SemaphoreType.DMA((5,))],
        [VMEM] + [HBM] * 5,
    )(rows, *prompts)


def by_z(part, step):
    pairs = [(x * 4 + z, x * 4 + (z + step) % 4) for x in range(4) for z in range(4)]
    return lax.ppermute(part, "prompt", pairs)


def over_x(blocks):
    groups = [[x * 4 + z for x in range(4)] for z in range(4)]
    shape = blocks.shape
    blocks = blocks.reshape(4, 64, shape[-1])
    moved = lax.all_to_all(blocks, "prompt", 0, 0, axis_index_groups=groups, tiled=True)
    return moved.reshape(shape)


def run_own(rank, route, core, *arrays):
    return call(
        own_kernel,
        [SMEM] * 3 + [HBM] * len(arrays),
        [
            ((ROWS, SEND_WIDTH), BF16),
            ((ROWS, KV_HALF), BF16),
            ((ROWS, KV_HALF), BF16),
            ((ROWS, ROWS), BF16),
            ((3, PADDED_RANK, 128), F32),
        ],
        like(arrays[:2]) + [pltpu.SemaphoreType.DMA((2 + SLOTS,))],
    )(rank, route, core, *in_hbm(arrays))


def in_hbm(arrays):
    return [pltpu.with_memory_space_constraint(a, pltpu.HBM) for a in arrays]


def run_finish(x, wu, *arrays):
    kv_width = KEY_VALUE_HEADS * HEAD_SIZE
    return call(
        finish_kernel,
        [HBM] * 2 + [VMEM] * len(arrays),
        [
            ((1, TOKENS, QUERY_WIDTH), BF16),
            ((1, TOKENS, kv_width), BF16),
            ((1, TOKENS, kv_width), BF16),
            ((CORE_ROWS, 128), BF16),
            ((CORE_ROWS, 128), BF16),
        ],
        like([x, wu])
        + [
            pltpu.VMEM((ROWS, HALF), F32),
            pltpu.VMEM((TOKENS, QUERY_WIDTH), BF16),
            pltpu.VMEM((TOKENS, kv_width), BF16),
            pltpu.VMEM((TOKENS, kv_width), BF16),
            pltpu.SemaphoreType.DMA((5,)),
        ],
        [HBM] * 3 + [VMEM] * 2,
    )(*in_hbm([x, wu]), *arrays)


def run_spread(*arrays):
    return call(
        spread_kernel,
        [VMEM] * len(arrays),
        [((PADDED_RANK, MODEL_WIDTH), F32), ((PADDED_RANK, QUERY_WIDTH), F32)],
    )(*arrays)


def by_core(part):
    return lax.ppermute(part, "comp", [(i, i ^ 1) for i in range(16)])


def layer_groups():
    return [
        [(x * 4 + z_hi) * 16 + zy * 2 + core for x in range(4) for zy in range(8)]
        for z_hi in range(4)
        for core in range(2)
    ]


def sum_all(mine, other, beside):
    rows = CORE_ROWS // 32
    swap = functools.partial(
        lax.all_to_all, axis_name=("prompt", "comp"), split_axis=0, concat_axis=0,
        axis_index_groups=layer_groups(), tiled=True,
    )
    pair = (mine.astype(F32) + by_core(other).astype(F32)).astype(BF16)
    total = jnp.sum(swap(pair.reshape(32, rows, 128)).astype(F32), axis=0)
    for flip in (lambda i: i ^ 1, lambda i: i // 4 * 4 + 3 - i % 4):
        total = total + lax.ppermute(total, "prompt", [(i, flip(i)) for i in range(16)])
    total = total.astype(BF16)
    half = swap(jnp.broadcast_to(total[None], (32, rows, 128))).reshape(CORE_ROWS, 128)
    half, beside = lax.optimization_barrier((half, beside))
    return half, by_core(half), beside


def per_device(
    normed_hidden_input,
    frozen_query_base,
    attention_output_grad,
    completion_keys,
    completion_values,
    owner_prompt_keys,
    owner_prompt_values,
    adapter_down_weight,
    adapter_up_weight,
    adapter_rank,
    route,
    lengths,
):
    hidden = normed_hidden_input[0]
    keys, values = completion_keys[0], completion_values[0]
    k0, v0 = owner_prompt_keys[0], owner_prompt_values[0]
    k1, v3 = by_z(k0, -1), by_z(v0, 1)
    z = lax.axis_index("prompt") % 4
    route = route // 4 * 4 + (route - z) % 4
    send = run_prepare(
        adapter_rank, route, lengths, hidden, frozen_query_base[0], attention_output_grad[0],
        keys, values, adapter_down_weight.T, adapter_up_weight,
    )
    send, k1, v3 = lax.optimization_barrier((send, k1, v3))
    arrived = over_x(send)
    k2, v2 = by_z(k1, -1), by_z(v3, 1)
    k3, v1 = by_z(k0, 1), by_z(v0, -1)
    width = KEY_VALUE_HEADS * HEAD_SIZE
    back, total, to_after, to_before, *far = run_owner(
        arrived.reshape(ROWS, SEND_WIDTH), k0, v0, k1, v1, k2, v2, k3, v3
    )
    back = over_x(back.reshape(SLOTS, 16, BACK_WIDTH))
    back, *far = lax.optimization_barrier((back, by_z(far[0], 1), by_z(far[1], -1)))
    to_after = jnp.concatenate([to_after[:, :width] + far[0], to_after[:, width:]], axis=1)
    to_before = jnp.concatenate([to_before[:, :width], to_before[:, width:] + far[1]], axis=1)
    core = (lax.axis_index("comp") % 2).astype(jnp.int32)[None]
    own = run_own(adapter_rank, route, core, keys, values, send)
    dq, dsk, dsv, mine, other = run_finish(
        hidden, adapter_up_weight, *own, back.reshape(ROWS, BACK_WIDTH)
    )
    near = [by_z(to_after, 1), by_z(to_before, -1)]
    half, other_half, near = sum_all(mine, other, near)
    for part in near:
        total = total + part.astype(F32)
    dk, dv = total[:, :width].astype(BF16), total[:, width:].astype(BF16)
    down, up = run_spread(own[-1], half, other_half)
    return dq, dsk, dsv, dk[None], dv[None], down.T, up


def solution(mesh):
    split = P("comp", "prompt", None)
    return jax.shard_map(
        per_device,
        mesh=mesh,
        in_specs=(split,) * 7 + (P(),) * 3 + (split,) * 2,
        out_specs=(split,) * 5 + (P(),) * 2,
        check_vma=False,
    )
```

```python
import functools
import math

import jax
import jax.numpy as jnp
from jax import lax
from jax.experimental import pallas as pl
from jax.experimental.pallas import tpu as pltpu
from jax.sharding import PartitionSpec as P

KEY_VALUE_HEADS = 4
GROUP = 5
HEAD_SIZE = 128
PLEN = 128
CL = 8
SLOTS = 16
TOKENS = SLOTS * CL
QUERY_HEADS = KEY_VALUE_HEADS * GROUP
PAIRS = QUERY_HEADS // 2
HALF = PAIRS * HEAD_SIZE
KV_HALF = KEY_VALUE_HEADS * HEAD_SIZE // 2
ROWS = 2 * TOKENS
MODEL_WIDTH = 5120
PADDED_RANK = 64
QUERY_WIDTH = QUERY_HEADS * HEAD_SIZE
SEND_WIDTH = 2 * HALF + 128
X_PARTS = 4
COST_FLOPS = 10**9
COST_BYTES = 60 * 10**6
X_PART = MODEL_WIDTH // X_PARTS
BACK_WIDTH = HALF + 128
DOWN_BLOCKS = MODEL_WIDTH // 128
GRAD_BLOCKS = (MODEL_WIDTH + QUERY_WIDTH) // 128
CORE_BLOCKS = 32
CORE_ROWS = CORE_BLOCKS * PADDED_RANK

INV_SQRT = 1.0 / math.sqrt(HEAD_SIZE)
adapter_strength = 32.0
masked_score = -1e30

BF16 = jnp.bfloat16
F32 = jnp.float32


def dot(a, b, dims):
    return lax.dot_general(a, b, (dims, ((), ())), preferred_element_type=F32)


def nt(a, b):
    return dot(a, b, ((1,), (1,)))


def nn(a, b):
    return dot(a, b, ((1,), (0,)))


def tn(a, b):
    return dot(a, b, ((0,), (0,)))


def fold(wide):
    width = wide.shape[1] // 2
    left = wide[:, :width].reshape(SLOTS, 1, CL, width)
    right = wide[:, width:].reshape(SLOTS, 1, CL, width)
    return jnp.concatenate([left, right], axis=1).reshape(ROWS, width)


def unfold(rows):
    split = rows.reshape(SLOTS, 2, CL, rows.shape[1])
    return split[:, 0].reshape(TOKENS, -1), split[:, 1].reshape(TOKENS, -1)


def own_mask():
    key = lax.broadcasted_iota(jnp.int32, (TOKENS, ROWS), 0)
    row = lax.broadcasted_iota(jnp.int32, (TOKENS, ROWS), 1) % TOKENS
    return (key // CL == row // CL) & (key <= row)


def own_scores(keys, rows):
    return jnp.concatenate(
        [nt(keys[at : at + TOKENS], rows[at : at + TOKENS]) for at in (0, TOKENS)], axis=1
    )


def own_product(scores, rows, product):
    return jnp.concatenate(
        [product(scores[:, at : at + TOKENS], rows[at : at + TOKENS]) for at in (0, TOKENS)], axis=0
    )


def pack_stats(rows):
    value = jnp.concatenate(rows, axis=0)
    first = value.astype(BF16).astype(F32)
    rest = value - first
    second = rest.astype(BF16).astype(F32)
    third = rest - second
    pad = jnp.zeros((128 - 3 * len(rows), ROWS), F32)
    return jnp.concatenate([first, second, third, pad], axis=0).T


def unpack_stats(columns, count):
    parts = columns.astype(F32).T
    return parts[:count] + (parts[count : 2 * count] + parts[2 * count : 3 * count])


def prepare_kernel(
    rank_hbm, route_hbm, length_hbm, x_hbm, base_hbm, g_hbm, sk_hbm, sv_hbm, wd_hbm, wu_hbm,
    send_hbm,
    rank_ref, route_ref, length_ref, x_ref, base_ref, g_ref, sk_ref, sv_ref, wd_ref, wu_ref, rows_ref, sems,
):
    columns = [slice(i * X_PART, (i + 1) * X_PART) for i in range(X_PARTS)]
    pairs = [(rank_hbm, rank_ref), (length_hbm, length_ref), (route_hbm, route_ref)]
    pairs += [(wd_hbm, wd_ref)] + [(x_hbm.at[:, c], x_ref.at[:, c]) for c in columns]
    pairs += [
        (g_hbm, g_ref), (sv_hbm, sv_ref), (sk_hbm, sk_ref), (wu_hbm, wu_ref), (base_hbm, base_ref)
    ]
    loads = [
        pltpu.make_async_copy(source, target, sems.at[i])
        for i, (source, target) in enumerate(pairs)
    ]
    for copy in loads:
        copy.start()

    def sends(start, width, sem):
        return [
            pltpu.make_async_copy(
                rows_ref.at[pl.ds(s * 16, 16), pl.ds(start, width)],
                send_hbm.at[route_ref[0, 0, s], :, pl.ds(start, width)],
                sems.at[sem + s],
            )
            for s in range(SLOTS)
        ]

    for copy in loads[:3]:
        copy.wait()
    rank = rank_ref[0]
    scale = adapter_strength / rank.astype(F32)
    position = lax.broadcasted_iota(jnp.int32, (CL, 128), 0)
    live = jnp.concatenate(
        [jnp.where(position < length_ref[0, 0, s], 1.0, 0.0) for s in range(SLOTS)], axis=0
    )
    mask = own_mask()
    loads[3].wait()
    low = jnp.zeros((TOKENS, PADDED_RANK), F32)
    for i, c in enumerate(columns):
        loads[4 + i].wait()
        low = low + nt(x_ref[:, c], wd_ref[:, c])
    rest = 4 + X_PARTS
    loads[rest].wait()
    for n in range(PAIRS):
        left, right = (g_ref[:, m * 128 : (m + 1) * 128].astype(F32) * live for m in (n, n + PAIRS))
        rows_ref[:, n * 128 : (n + 1) * 128] = fold(
            jnp.concatenate([left, right], axis=1)
        ).astype(BF16)
    early = sends(0, HALF, rest + 5)
    for copy in early:
        copy.start()
    for copy in loads[rest + 1 :]:
        copy.wait()
    values = fold(sv_ref[...].astype(F32)).astype(BF16)
    keys = fold(sk_ref[...].astype(F32)).astype(BF16)
    keep = lax.broadcasted_iota(jnp.int32, (TOKENS, PADDED_RANK), 1) < rank
    low = jnp.where(keep, low, 0.0).astype(BF16)
    query = base_ref[...].astype(F32) + scale * nn(low, wu_ref[...])
    rows_ref[:, HALF : 2 * HALF] = fold(query).astype(BF16)

    def products(b):
        h = b // GROUP
        g = rows_ref[:, b * 128 : (b + 1) * 128]
        q = rows_ref[:, HALF + b * 128 : HALF + (b + 1) * 128]
        return (
            own_scores(keys[:, h * 128 : (h + 1) * 128], q),
            own_scores(values[:, h * 128 : (h + 1) * 128], g),
        )

    lses, deltas = [], []
    ready = products(0)
    for b in range(PAIRS):
        scores, dprob = ready
        if b + 1 < PAIRS:
            ready = products(b + 1)
        scores = jnp.where(mask, scores * INV_SQRT, masked_score)
        top = jnp.max(scores, axis=0, keepdims=True)
        weight = jnp.exp(scores - top)
        total = jnp.sum(weight, axis=0, keepdims=True)
        lses.append(top + jnp.log(total))
        deltas.append(jnp.sum(weight * dprob, axis=0, keepdims=True) / total)
    none = jnp.zeros((TOKENS, PADDED_RANK), F32)
    low_rows = fold(jnp.concatenate([none, low.astype(F32), none, none], axis=1))
    rows_ref[:, 2 * HALF :] = (pack_stats(lses + deltas) + low_rows).astype(BF16)
    late = sends(HALF, SEND_WIDTH - HALF, rest + 5 + SLOTS)
    for copy in late:
        copy.start()
    for copy in early + late:
        copy.wait()


def owner_kernel(
    rows_ref, k0_ref, v0_ref, k1_ref, v1_ref, k2_ref, v2_ref, k3_ref, v3_ref,
    back_hbm, part0_hbm, part1_hbm, part3_hbm, dk2_hbm, dv2_hbm,
    back_ref, part0_ref, part1_ref, part3_ref, dk2_ref, dv2_ref, sems,
):
    width = KEY_VALUE_HEADS * HEAD_SIZE

    def halves(ref):
        return ref.at[:, :width], ref.at[:, width:]

    kv_refs = ((k0_ref, v0_ref), (k1_ref, v1_ref), (k2_ref, v2_ref), (k3_ref, v3_ref))
    part_refs = (halves(part0_ref), halves(part1_ref), (dk2_ref, dv2_ref), halves(part3_ref))
    places = [(x * 4 + k) * 16 for k in range(4) for x in range(4)]
    lower = (lax.broadcasted_iota(jnp.int32, (ROWS, HEAD_SIZE), 0) // CL % 2 == 0).astype(F32)
    lower, upper = lower.astype(BF16), (1.0 - lower).astype(BF16)
    even = lax.broadcasted_iota(jnp.int32, (PLEN, 128), 1) < 64

    def load(at):
        return jnp.concatenate([rows_ref[p : p + 16, at : at + 128] for p in places], axis=0)

    def store(at, value):
        for i, p in enumerate(places):
            back_ref[p : p + 16, at : at + 128] = value[i * 16 : (i + 1) * 16]

    def beside(ref, h):
        return jnp.concatenate([ref[:, m * 128 : (m + 1) * 128] for m in (h, h + 2)], axis=1)

    def apart(rows):
        return jnp.concatenate([rows * lower, rows * upper], axis=1)

    def by_prompt(rows):
        none = jnp.zeros((64, 256), BF16)
        return jnp.concatenate(
            [
                jnp.concatenate([rows[:64], none], axis=1),
                jnp.concatenate([none, rows[64:]], axis=1),
            ],
            axis=0,
        )

    def against(sides, rows):
        parts = []
        for p in range(2):
            two = rows[p * 128 : (p + 1) * 128]
            parts.append(jnp.where(even, nt(sides[2 * p], two), nt(sides[2 * p + 1], two)))
        return jnp.concatenate(parts, axis=1)

    sides = [
        ([beside(refs[0], h) for refs in kv_refs], [beside(refs[1], h) for refs in kv_refs])
        for h in range(2)
    ]
    stats = unpack_stats(load(2 * HALF), 2 * PAIRS)

    def products(b):
        g = apart(load(b * 128))
        q = apart(load(HALF + b * 128))
        keys, values = sides[b // GROUP]
        return q, g, against(keys, q), against(values, g)

    lses, deltas = [], []
    ready = products(0)
    for h in range(2):
        keys = sides[h][0]
        done = []
        for b in range(h * GROUP, (h + 1) * GROUP):
            q, g, scores, dprob = ready
            if b + 1 < PAIRS:
                ready = products(b + 1)
            own_lse, own_delta = stats[b : b + 1], stats[PAIRS + b : PAIRS + b + 1]
            scores = scores * INV_SQRT
            top = jnp.max(scores, axis=0, keepdims=True)
            weight = jnp.exp(scores - top)
            prompt_lse = top + jnp.log(jnp.sum(weight, axis=0, keepdims=True))
            high = jnp.maximum(prompt_lse, own_lse)
            lse = high + jnp.log(jnp.exp(prompt_lse - high) + jnp.exp(own_lse - high))
            probs = weight * jnp.exp(top - lse)
            probs_b = probs.astype(BF16)
            delta = jnp.sum(probs_b.astype(F32) * dprob, axis=0, keepdims=True) + own_delta * jnp.exp(
                own_lse - lse
            )
            dscore = (probs * (dprob - delta)).astype(BF16)
            picks = []
            for p in range(2):
                both = jnp.concatenate([keys[2 * p], keys[2 * p + 1]], axis=1)
                full = tn(dscore[:, p * 128 : (p + 1) * 128], both) * INV_SQRT
                for k in range(2):
                    rows = full[k * 64 : (k + 1) * 64, k * 256 : (k + 1) * 256]
                    rows = rows.reshape(4, 2, CL, 256)
                    rows = jnp.concatenate(
                        [rows[:, :1, :, :HEAD_SIZE], rows[:, 1:, :, HEAD_SIZE:]], axis=1
                    )
                    picks.append(rows.reshape(64, HEAD_SIZE))
            store(b * 128, jnp.concatenate(picks, axis=0).astype(BF16))
            done.append((dscore, q, probs_b, g))
            lses.append(lse)
            deltas.append(delta)
        if h == 0:
            ahead = pl.ds(0, HALF // 2)
            early = pltpu.make_async_copy(back_ref.at[:, ahead], back_hbm.at[:, ahead], sems.at[5])
            early.start()
        for p in range(2):
            at = slice(p * 128, (p + 1) * 128)
            for kind, first, scale in ((0, 0, INV_SQRT), (1, 2, 1.0)):
                left = jnp.concatenate([d[first][:, at] for d in done], axis=1)
                right = jnp.concatenate([by_prompt(d[first + 1][at]) for d in done], axis=0)
                grad = nn(left, right) * scale
                for k in range(2):
                    ref = part_refs[2 * p + k][kind]
                    for i, m in enumerate((h, h + 2)):
                        column = k * 256 + i * 128
                        ref[:, m * 128 : (m + 1) * 128] = grad[:, column : column + 128].astype(
                            ref.dtype
                        )
    outs = [
        (dk2_ref, dk2_hbm), (dv2_ref, dv2_hbm), (part1_ref, part1_hbm), (part3_ref, part3_hbm),
        (part0_ref, part0_hbm),
    ]
    copies = [
        pltpu.make_async_copy(source, target, sems.at[i])
        for i, (source, target) in enumerate(outs)
    ]
    for copy in copies:
        copy.start()
    store(HALF, pack_stats(lses + deltas).astype(BF16))
    last = pl.ds(HALF // 2, BACK_WIDTH - HALF // 2)
    copies += [
        early,
        pltpu.make_async_copy(back_ref.at[:, last], back_hbm.at[:, last], sems.at[6]),
    ]
    copies[-1].start()
    for copy in copies:
        copy.wait()


def own_kernel(
    rank_ref, route_ref, core_ref, sk_hbm, sv_hbm, send_hbm,
    rows_ref, keys_ref, values_ref, order_ref, factors_ref,
    sk_ref, sv_ref, sems,
):
    pairs = [(sk_hbm, sk_ref), (sv_hbm, sv_ref)]
    pairs += [
        (send_hbm.at[route_ref[0, 0, s]], rows_ref.at[pl.ds(s * 16, 16)]) for s in range(SLOTS)
    ]
    loads = [
        pltpu.make_async_copy(source, target, sems.at[i])
        for i, (source, target) in enumerate(pairs)
    ]
    for copy in loads:
        copy.start()
    rank = rank_ref[0]
    scale = adapter_strength / rank.astype(F32)
    block = (PADDED_RANK, 128)
    keep = lax.broadcasted_iota(jnp.int32, block, 1) < rank
    factors_ref[0] = jnp.full(block, scale, F32)
    factors_ref[1] = jnp.where(keep, scale, 0.0)
    factors_ref[2] = jnp.full(block, 1.0, F32) * (core_ref[0] == 0).astype(F32)
    lane = lax.broadcasted_iota(jnp.int32, (16, ROWS), 1)
    place = lax.broadcasted_iota(jnp.int32, (16, ROWS), 0)
    for s in range(SLOTS):
        at = (lane == route_ref[0, 0, s] * 16 + place).astype(F32)
        order_ref[s * 16 : (s + 1) * 16, :] = at.astype(BF16)
    for copy in loads:
        copy.wait()
    keys_ref[...] = fold(sk_ref[...].astype(F32)).astype(BF16)
    values_ref[...] = fold(sv_ref[...].astype(F32)).astype(BF16)


def finish_kernel(
    x_hbm, wu_hbm, rows_ref, keys_ref, values_ref, order_ref, factors_ref, back_ref,
    dq_hbm, dsk_hbm, dsv_hbm, mine_ref, other_ref,
    x_ref, wu_ref, dq_rows_ref, dq_ref, dsk_ref, dsv_ref, sems,
):
    loads = [
        pltpu.make_async_copy(wu_hbm, wu_ref, sems.at[3]),
        pltpu.make_async_copy(x_hbm, x_ref, sems.at[4]),
    ]
    for copy in loads:
        copy.start()
    order = order_ref[...]
    mask = own_mask()

    def products(b):
        h = b // GROUP
        g = rows_ref[:, b * 128 : (b + 1) * 128]
        q = rows_ref[:, HALF + b * 128 : HALF + (b + 1) * 128]
        return (
            q, g,
            own_scores(keys_ref[:, h * 128 : (h + 1) * 128], q),
            own_scores(values_ref[:, h * 128 : (h + 1) * 128], g),
        )

    ready = products(0)
    stats = unpack_stats(nn(order, back_ref[:, HALF:]), 2 * PAIRS)
    dq_rows_ref[...] = nn(order, back_ref[:, :HALF])
    for h in range(2):
        k2 = keys_ref[:, h * 128 : (h + 1) * 128]
        dsk = jnp.zeros((ROWS, HEAD_SIZE), F32)
        dsv = jnp.zeros((ROWS, HEAD_SIZE), F32)
        for b in range(h * GROUP, (h + 1) * GROUP):
            q, g, scores, dprob = ready
            if b + 1 < PAIRS:
                ready = products(b + 1)
            lse, delta = stats[b : b + 1], stats[PAIRS + b : PAIRS + b + 1]
            probs = jnp.exp(jnp.where(mask, scores * INV_SQRT - lse, masked_score))
            dscore = (probs * (dprob - delta)).astype(BF16)
            dq = dq_rows_ref[:, b * 128 : (b + 1) * 128] + own_product(dscore, k2, tn) * INV_SQRT
            for at, part in zip((b, b + PAIRS), unfold(dq)):
                dq_ref[:, at * 128 : (at + 1) * 128] = part.astype(BF16)
            dsv = dsv + own_product(probs.astype(BF16), g, nn)
            dsk = dsk + own_product(dscore, q, nn)
        for at, k_part, v_part in zip((h, h + 2), unfold(dsk * INV_SQRT), unfold(dsv)):
            dsk_ref[:, at * 128 : (at + 1) * 128] = k_part.astype(BF16)
            dsv_ref[:, at * 128 : (at + 1) * 128] = v_part.astype(BF16)
    stores = [
        pltpu.make_async_copy(source, target.at[0], sems.at[i])
        for i, (source, target) in enumerate(
            [(dq_ref, dq_hbm), (dsk_ref, dsk_hbm), (dsv_ref, dsv_hbm)]
        )
    ]
    for copy in stores:
        copy.start()
    dq = dq_ref[...]
    for copy in loads:
        copy.wait()
    lifted = (nt(dq, wu_ref[...]) * factors_ref[1, :1, :PADDED_RANK]).astype(BF16)
    low = unfold(rows_ref[:, 2 * HALF :].astype(F32))[0][:, PADDED_RANK:].astype(BF16)
    scale, first = factors_ref[0], factors_ref[2] > 0.5

    def block(c):
        if c < DOWN_BLOCKS:
            return tn(lifted, x_ref[:, c * 128 : (c + 1) * 128])
        if c < GRAD_BLOCKS:
            at = (c - DOWN_BLOCKS) * 128
            return scale * tn(low, dq[:, at : at + 128])
        return jnp.zeros((PADDED_RANK, 128), F32)

    for c in range(CORE_BLOCKS):
        lower, upper = block(c), block(c + CORE_BLOCKS)
        at = slice(c * PADDED_RANK, (c + 1) * PADDED_RANK)
        mine_ref[at, :] = jnp.where(first, lower, upper).astype(BF16)
        other_ref[at, :] = jnp.where(first, upper, lower).astype(BF16)
    for copy in stores:
        copy.wait()


def spread_kernel(factors_ref, mine_ref, other_ref, down_ref, up_ref):
    first = factors_ref[2] > 0.5
    for c in range(GRAD_BLOCKS):
        at = c % CORE_BLOCKS * PADDED_RANK
        mine = mine_ref[at : at + PADDED_RANK, :].astype(F32)
        other = other_ref[at : at + PADDED_RANK, :].astype(F32)
        part = jnp.where(first, mine, other) if c < CORE_BLOCKS else jnp.where(first, other, mine)
        if c < DOWN_BLOCKS:
            down_ref[:, c * 128 : (c + 1) * 128] = part
        else:
            at = (c - DOWN_BLOCKS) * 128
            up_ref[:, at : at + 128] = part


VMEM = pl.BlockSpec(memory_space=pltpu.VMEM)
SMEM = pl.BlockSpec(memory_space=pltpu.SMEM)
HBM = pl.BlockSpec(memory_space=pltpu.HBM)


def call(kernel, in_specs, outs, scratch=(), out_specs=None, vmem_mib=40, cost=None):
    return pl.pallas_call(
        kernel,
        out_shape=[
            jax.ShapeDtypeStruct(*out) if len(out) == 2 else out[0](*out[1:]) for out in outs
        ],
        in_specs=in_specs,
        out_specs=out_specs or [VMEM] * len(outs),
        scratch_shapes=list(scratch),
        compiler_params=pltpu.CompilerParams(vmem_limit_bytes=vmem_mib * 1024 * 1024),
        cost_estimate=cost,
    )


def like(arrays):
    return [
        (pltpu.SMEM if a.dtype == jnp.int32 else pltpu.VMEM)(a.shape, a.dtype) for a in arrays
    ]


def run_prepare(*arrays):
    return call(
        prepare_kernel,
        [HBM] * len(arrays),
        [((SLOTS, 16, SEND_WIDTH), BF16)],
        like(arrays)
        + [
            pltpu.VMEM((ROWS, SEND_WIDTH), BF16),
            pltpu.SemaphoreType.DMA((9 + X_PARTS + 2 * SLOTS,)),
        ],
        [HBM],
        60,
        pl.CostEstimate(flops=COST_FLOPS, bytes_accessed=COST_BYTES, transcendentals=0),
    )(*arrays)[0]


def run_owner(rows, *prompts):
    half = (PLEN, KEY_VALUE_HEADS * HEAD_SIZE)
    part = (PLEN, 2 * KEY_VALUE_HEADS * HEAD_SIZE)
    parts = [((ROWS, BACK_WIDTH), BF16), (part, F32)] + [(part, BF16)] * 2 + [(half, BF16)] * 2
    return call(
        owner_kernel,
        [VMEM] * 9,
        [(pltpu.HBM, *p) for p in parts],
        [pltpu.VMEM(*p) for p in parts] + [pltpu.SemaphoreType.DMA((7,))],
        [HBM] * 6,
    )(rows, *prompts)


def by_z(part, step):
    pairs = [(x * 4 + z, x * 4 + (z + step) % 4) for x in range(4) for z in range(4)]
    return lax.ppermute(part, "prompt", pairs)


def over_x(blocks):
    groups = [[x * 4 + z for x in range(4)] for z in range(4)]
    shape = blocks.shape
    blocks = blocks.reshape(4, 64, shape[-1])
    moved = lax.all_to_all(blocks, "prompt", 0, 0, axis_index_groups=groups, tiled=True)
    return moved.reshape(shape)


def run_own(rank, route, core, *arrays):
    return call(
        own_kernel,
        [SMEM] * 3 + [HBM] * len(arrays),
        [
            ((ROWS, SEND_WIDTH), BF16),
            ((ROWS, KV_HALF), BF16),
            ((ROWS, KV_HALF), BF16),
            ((ROWS, ROWS), BF16),
            ((3, PADDED_RANK, 128), F32),
        ],
        like(arrays[:2]) + [pltpu.SemaphoreType.DMA((2 + SLOTS,))],
    )(rank, route, core, *in_hbm(arrays))


def in_hbm(arrays):
    return [pltpu.with_memory_space_constraint(a, pltpu.HBM) for a in arrays]


def run_finish(x, wu, *arrays):
    kv_width = KEY_VALUE_HEADS * HEAD_SIZE
    return call(
        finish_kernel,
        [HBM] * 2 + [VMEM] * len(arrays),
        [
            ((1, TOKENS, QUERY_WIDTH), BF16),
            ((1, TOKENS, kv_width), BF16),
            ((1, TOKENS, kv_width), BF16),
            ((CORE_ROWS, 128), BF16),
            ((CORE_ROWS, 128), BF16),
        ],
        like([x, wu])
        + [
            pltpu.VMEM((ROWS, HALF), F32),
            pltpu.VMEM((TOKENS, QUERY_WIDTH), BF16),
            pltpu.VMEM((TOKENS, kv_width), BF16),
            pltpu.VMEM((TOKENS, kv_width), BF16),
            pltpu.SemaphoreType.DMA((5,)),
        ],
        [HBM] * 3 + [VMEM] * 2,
    )(*in_hbm([x, wu]), *arrays)


def run_spread(*arrays):
    return call(
        spread_kernel,
        [VMEM] * len(arrays),
        [((PADDED_RANK, MODEL_WIDTH), F32), ((PADDED_RANK, QUERY_WIDTH), F32)],
    )(*arrays)


def by_core(part):
    return lax.ppermute(part, "comp", [(i, i ^ 1) for i in range(16)])


def layer_groups():
    return [
        [(x * 4 + z_hi) * 16 + zy * 2 + core for x in range(4) for zy in range(8)]
        for z_hi in range(4)
        for core in range(2)
    ]


def sum_all(mine, other, beside):
    rows = CORE_ROWS // 32
    swap = functools.partial(
        lax.all_to_all, axis_name=("prompt", "comp"), split_axis=0, concat_axis=0,
        axis_index_groups=layer_groups(), tiled=True,
    )
    pair = (mine.astype(F32) + by_core(other).astype(F32)).astype(BF16)
    total = jnp.sum(swap(pair.reshape(32, rows, 128)).astype(F32), axis=0)
    for flip in (lambda i: i ^ 1, lambda i: i // 4 * 4 + 3 - i % 4):
        total = total + lax.ppermute(total, "prompt", [(i, flip(i)) for i in range(16)])
    total = total.astype(BF16)
    half = swap(jnp.broadcast_to(total[None], (32, rows, 128))).reshape(CORE_ROWS, 128)
    half, beside = lax.optimization_barrier((half, beside))
    return half, by_core(half), beside


def per_device(
    normed_hidden_input,
    frozen_query_base,
    attention_output_grad,
    completion_keys,
    completion_values,
    owner_prompt_keys,
    owner_prompt_values,
    adapter_down_weight,
    adapter_up_weight,
    adapter_rank,
    route,
    lengths,
):
    hidden = normed_hidden_input[0]
    keys, values = completion_keys[0], completion_values[0]
    k0, v0 = owner_prompt_keys[0], owner_prompt_values[0]
    k1, v3 = by_z(k0, -1), by_z(v0, 1)
    z = lax.axis_index("prompt") % 4
    route = route // 4 * 4 + (route - z) % 4
    send = run_prepare(
        adapter_rank, route, lengths, hidden, frozen_query_base[0], attention_output_grad[0],
        keys, values, adapter_down_weight.T, adapter_up_weight,
    )
    send, k1, v3 = lax.optimization_barrier((send, k1, v3))
    arrived = over_x(send)
    k2, v2 = by_z(k1, -1), by_z(v3, 1)
    k3, v1 = by_z(k0, 1), by_z(v0, -1)
    width = KEY_VALUE_HEADS * HEAD_SIZE
    back, total, to_after, to_before, *far = run_owner(
        arrived.reshape(ROWS, SEND_WIDTH), k0, v0, k1, v1, k2, v2, k3, v3
    )
    back = over_x(back.reshape(SLOTS, 16, BACK_WIDTH))
    back, *far = lax.optimization_barrier((back, by_z(far[0], 1), by_z(far[1], -1)))
    to_after = jnp.concatenate([to_after[:, :width] + far[0], to_after[:, width:]], axis=1)
    to_before = jnp.concatenate([to_before[:, :width], to_before[:, width:] + far[1]], axis=1)
    core = (lax.axis_index("comp") % 2).astype(jnp.int32)[None]
    own = run_own(adapter_rank, route, core, keys, values, send)
    dq, dsk, dsv, mine, other = run_finish(
        hidden, adapter_up_weight, *own, back.reshape(ROWS, BACK_WIDTH)
    )
    near = [by_z(to_after, 1), by_z(to_before, -1)]
    half, other_half, near = sum_all(mine, other, near)
    for part in near:
        total = total + part.astype(F32)
    dk, dv = total[:, :width].astype(BF16), total[:, width:].astype(BF16)
    down, up = run_spread(own[-1], half, other_half)
    return dq, dsk, dsv, dk[None], dv[None], down.T, up


def solution(mesh):
    split = P("comp", "prompt", None)
    return jax.shard_map(
        per_device,
        mesh=mesh,
        in_specs=(split,) * 7 + (P(),) * 3 + (split,) * 2,
        out_specs=(split,) * 5 + (P(),) * 2,
        check_vma=False,
    )
```
